32 devices in a mesh: dp: 4 (over z), fsdp: 8 (over y, x, core).
Axes of the slice: x: 2, y: 2, z: 4, core: 2. Of those that a mesh axis runs over, the one named last changes fastest.
Arguments:
- token_ids: int32 [64, 512], P(('dp', 'fsdp')), may hold values from 0 to 32127, as said below
- task_ids: int32 [64], P(('dp', 'fsdp')), may hold values from 0 to 15, as said below
- lengths: int32 [64], P(('dp', 'fsdp')), may hold values from 128 to 512, as said below
- instruction: int32 [64, 512], P(('dp', 'fsdp')), may hold values from 0 to 1, as said below
- table: bfloat16 [32128, 768], P('fsdp'), may hold values from -6 to 6
- attn_gain: bfloat16 [768], P('fsdp'), may hold values from 0.099609375 to 1.8984375
- w_query: bfloat16 [768, 768], P('fsdp'), may hold values from -0.0546875 to 0.0546875
- w_key: bfloat16 [768, 768], P('fsdp'), may hold values from -0.21875 to 0.21875
- w_value: bfloat16 [768, 768], P('fsdp'), may hold values from -0.21875 to 0.21875
- w_out: bfloat16 [768, 768], P('fsdp'), may hold values from -0.875 to 0.875
- ffn_gain: bfloat16 [768], P('fsdp'), may hold values from 0.099609375 to 1.8984375
- w_in: bfloat16 [768, 3072], P('fsdp'), may hold values from -0.21875 to 0.21875
- w_back: bfloat16 [3072, 768], P('fsdp'), may hold values from -0.109375 to 0.109375
- rel_bias: bfloat16 [32, 12], P('fsdp'), may hold values from -4 to 4
- d_out: bfloat16 [64, 512, 768], P(('dp', 'fsdp')), may hold values from -6 to 6
Outputs:
- activations: bfloat16 [64, 512, 768], P(('dp', 'fsdp'))
- table_grad: float32 [32128, 768], P('fsdp')
- grad_attn_gain: float32 [768], P('fsdp')
- grad_w_query: float32 [768, 768], P('fsdp')
- grad_w_key: float32 [768, 768], P('fsdp')
- grad_w_value: float32 [768, 768], P('fsdp')
- grad_w_out: float32 [768, 768], P('fsdp')
- grad_ffn_gain: float32 [768], P('fsdp')
- grad_w_in: float32 [768, 3072], P('fsdp')
- grad_w_back: float32 [3072, 768], P('fsdp')
- grad_rel_bias: float32 [32, 12], P('fsdp')
The draws below stay inside these ranges and needn't reach their ends.
Inputs may be any that keep to these rules, and one draw needn't show every extreme that they name: `token_ids`: among the 1024 token slots of one device's rows, at most 256 hold ids of one block of 4016 consecutive ids, and in every device's rows some block holds exactly 256. `task_ids`: task ids never fall along the rows; 0 and 15 both occur. `lengths`: some row has length 512. Each row's instruction is its first tokens: 1 on a prefix of one or more positions shorter than the row's length, 0 elsewhere.
All inputs are finite; a program needn't handle non-finite values.
Results may differ from the reference program's by a relative error of at most 0.012.
The reference program's roundings to bfloat16 on the way count: a program that leaves them out, or rounds other values in their place, can miss the bound.
Values may be sent and summed in bfloat16 or wider, within the bound.
No kernel may reach another device: no remote copies, remote signals or barrier semaphores. Data moves between devices by JAX's collectives and lax.ppermute only.
A program may use at most 192 MiB of HBM per device.

```python
import math
import jax
import jax.numpy as jnp
from jax import lax

D = 768
H = 12
HD = 64
FF = 3072
VOCAB = 32128
NB = 32
SEQ = 512
INNER = 768
TOK_DEV = 1024
ROWS = 64
TASKS = 16
VSHARD = 4016
CAP = 256
N_FSDP = 8


def row_lengths(key):
    inner_key = jax.random.fold_in(key, 100)
    drawn = jax.random.randint(inner_key, (ROWS,), SEQ // 4, SEQ + 1)
    picked = jax.random.randint(jax.random.fold_in(inner_key, 1), (), 0, ROWS)
    return drawn.at[picked].set(SEQ).astype(jnp.int32)


def draw_lengths(key, part):
    return row_lengths(key)


def draw_instruction(key, part):
    row_lens = row_lengths(key)
    key = jax.random.fold_in(key, 7)
    spread = jax.random.randint(key, (ROWS,), 0, 2 ** 20)
    prefix = 1 + spread % (row_lens // 3)
    positions = jnp.arange(SEQ, dtype=jnp.int32)
    return (positions[None, :] < prefix[:, None]).astype(jnp.int32)


def draw_task_ids(key, part):
    key = jax.random.fold_in(key, 5)
    keys = jax.random.split(key, 3)
    first_pick = jax.random.randint(keys[0], (ROWS,), 0, TASKS)
    second_pick = jax.random.randint(keys[1], (ROWS,), 0, TASKS)
    chosen = jnp.minimum(first_pick, second_pick)
    where_top = jax.random.randint(keys[2], (), 1, ROWS)
    chosen = chosen.at[where_top].set(TASKS - 1).at[0].set(0)
    return jnp.sort(chosen).astype(jnp.int32)


def draw_token_ids(key, part):
    key = jax.random.fold_in(key, 3)
    keys = jax.random.split(key, 4)
    blocks = ROWS * SEQ // TOK_DEV
    slots = N_FSDP * CAP
    slot_index = jnp.arange(slots, dtype=jnp.int32)
    owner_of = slot_index // CAP
    hot_owner = jax.random.randint(keys[0], (blocks, 1), 0, N_FSDP)
    score = jax.random.randint(keys[1], (blocks, slots), 0, 2 ** 30 // slots) * slots + slot_index[None, :]
    score = jnp.where(owner_of[None, :] == hot_owner, slot_index[None, :] - slots, score)
    chosen = jnp.argsort(score, axis=1)[:, :TOK_DEV]
    owners = owner_of[chosen]
    token_index = jnp.arange(TOK_DEV, dtype=jnp.int32)
    placing = jax.random.randint(keys[2], (blocks, TOK_DEV), 0, 2 ** 30 // TOK_DEV) * TOK_DEV + token_index[None, :]
    ordering = jnp.argsort(placing, axis=1)
    owners = jnp.take_along_axis(owners, ordering, axis=1)
    offsets = jax.random.randint(keys[3], (blocks, TOK_DEV), 0, VSHARD)
    return (owners * VSHARD + offsets).reshape(ROWS, SEQ).astype(jnp.int32)


def shard_levels(key, dims, pieces, low, largest):
    gain, own = 1.0, jax.random.fold_in(key, 6)
    for axis_at, parts in pieces:
        draws = jnp.exp(jax.random.uniform(jax.random.fold_in(own, axis_at), (parts,), jnp.float32, low / len(pieces), largest / len(pieces)))
        gain = gain * jnp.repeat(draws, dims[axis_at] // parts).reshape([-1 if axis == axis_at else 1 for axis in range(len(dims))])
    return gain


def scatter_about(own_key, dims, scale, most, cuts=(), held_as=jnp.bfloat16):
    values = scale * jax.random.normal(own_key, dims, jnp.float32)
    if cuts:
        values = values * shard_levels(own_key, dims, cuts, -0.22, 0.18)
    return jnp.clip(values, -most, most).astype(held_as)


def setup_inputs(seed: int = 0) -> dict:
    key_list = jax.random.split(jax.random.key(seed), 16)
    token_ids = draw_token_ids(jax.random.fold_in(key_list[15], 71), 0)
    task_ids = draw_task_ids(jax.random.fold_in(key_list[15], 71), 0)
    lengths = draw_lengths(jax.random.fold_in(key_list[15], 71), 0)
    instruction = draw_instruction(jax.random.fold_in(key_list[15], 71), 0)
    table = scatter_about(key_list[4], (VOCAB, D), 1.0, 6.0, ((0, 8),))
    attn_gain = jnp.clip(1.0 + 0.18 * jax.random.normal(key_list[5], (D,), jnp.float32), 0.099609375, 1.8984375).astype(jnp.bfloat16)
    w_query = scatter_about(key_list[6], (D, INNER), (D * HD // 4) ** -0.5, 0.0546875, ((0, 8),))
    w_key = scatter_about(key_list[7], (D, INNER), D ** -0.5, 0.21875, ((0, 8),))
    w_value = scatter_about(key_list[8], (D, INNER), D ** -0.5, 0.21875, ((0, 8),))
    w_out = scatter_about(key_list[9], (INNER, D), (INNER // 16) ** -0.5, 0.875, ((0, 8),))
    ffn_gain = jnp.clip(1.0 + 0.18 * jax.random.normal(key_list[10], (D,), jnp.float32), 0.099609375, 1.8984375).astype(jnp.bfloat16)
    w_in = scatter_about(key_list[11], (D, FF), D ** -0.5, 0.21875, ((0, 8),))
    w_back = scatter_about(key_list[12], (FF, D), FF ** -0.5, 0.109375, ((0, 8),))
    rel_bias = scatter_about(key_list[13], (NB, H), 1.0, 4.0, ((0, 8),))
    d_out = scatter_about(key_list[14], (ROWS, SEQ, D), 1.0, 6.0, ((0, 32),))
    return {"token_ids": token_ids, "task_ids": task_ids, "lengths": lengths, "instruction": instruction, "table": table, "attn_gain": attn_gain, "w_query": w_query, "w_key": w_key, "w_value": w_value, "w_out": w_out, "ffn_gain": ffn_gain, "w_in": w_in, "w_back": w_back, "rel_bias": rel_bias, "d_out": d_out}


EPS = 1e-06
NEG = -1000000000.0
LIMITS = (12, 16, 23, 32, 46, 64, 91)
HIGH = lax.Precision.HIGHEST

@jax.custom_vjp
def low(v):
    return lax.optimization_barrier(v.astype(jnp.bfloat16)).astype(jnp.float32)

@jax.custom_vjp
def low_back(v):
    return v

def low_keep(v):
    return (low(v), None)

def low_pass(kept, grad):
    return (grad,)

def back_keep(v):
    return (v, None)

def back_low(kept, grad):
    return (low(grad),)
low.defvjp(low_keep, low_pass)
low_back.defvjp(back_keep, back_low)

def bucket_map(length):
    positions = jnp.arange(length, dtype=jnp.int32)
    offset = positions[None, :] - positions[:, None]
    distance = jnp.abs(offset)
    far_bucket = 8 + sum(((distance >= limit).astype(jnp.int32) for limit in LIMITS))
    upper = jnp.where(offset > 0, 16, 0).astype(jnp.int32)
    return upper + jnp.where(distance < 8, distance, far_bucket).astype(jnp.int32)

def normed(values, gains):
    return values * lax.rsqrt(lax.optimization_barrier(jnp.mean(values * values, axis=-1, keepdims=True)) + EPS) * gains

def attend_row(queries, key_rows, value_rows, length, bias):
    scores = jnp.einsum('qhd,khd->hqk', queries, key_rows, precision=HIGH) + bias
    scores = low_back(scores)
    usable = jnp.arange(queries.shape[0], dtype=jnp.int32) < length
    scores = jnp.where(usable[None, None, :], scores, NEG)
    probs = jax.nn.softmax(scores, axis=-1)
    return jnp.einsum('hqk,khd->qhd', low(probs), value_rows, precision=HIGH)

def forward(params, table_full, ids_group, lengths_group):
    attn_gain, w_query, w_key, w_value, w_out, ffn_gain, w_in, w_back, rel_bias = params
    group_rows, seq_len = ids_group.shape
    model_width = table_full.shape[1]
    heads = rel_bias.shape[1]
    head_size = w_query.shape[1] // heads
    stream = jnp.take(table_full, ids_group.reshape(group_rows * seq_len), axis=0)
    normed_one = low(normed(stream, attn_gain))

    def project(weight):
        mixed = low_back(low(jnp.dot(normed_one, weight, precision=HIGH)))
        return mixed.reshape(group_rows, seq_len, heads, head_size)
    queries = project(w_query)
    key_rows = project(w_key)
    value_rows = project(w_value)
    bias = jnp.transpose(jnp.take(rel_bias, bucket_map(seq_len), axis=0), (2, 0, 1))

    def one_row(row_items):
        return attend_row(row_items[0], row_items[1], row_items[2], row_items[3], bias)
    attended = lax.map(jax.checkpoint(one_row), (queries, key_rows, value_rows, lengths_group))
    attended = low_back(low(attended.reshape(group_rows * seq_len, heads * head_size)))
    hidden = stream + low_back(jnp.dot(attended, w_out, precision=HIGH))
    normed_two = low(normed(hidden, ffn_gain))
    pre_act = low_back(jnp.dot(normed_two, w_in, precision=HIGH))
    activated = low(jax.nn.gelu(pre_act))
    result = hidden + low_back(jnp.dot(activated, w_back, precision=HIGH))
    return result.reshape(group_rows, seq_len, model_width)

def reference(token_ids, task_ids, lengths, instruction, table, attn_gain, w_query, w_key, w_value, w_out, ffn_gain, w_in, w_back, rel_bias, d_out):
    params = tuple((member.astype(jnp.float32) for member in (attn_gain, w_query, w_key, w_value, w_out, ffn_gain, w_in, w_back, rel_bias)))
    table_full = table.astype(jnp.float32)
    task_hot = (task_ids[:, None] == jnp.arange(TASKS, dtype=jnp.int32)[None, :]).astype(jnp.float32)
    counts = lax.optimization_barrier(jnp.sum(task_hot, axis=0))
    row_weight = 1.0 / lax.optimization_barrier(jnp.sum(task_hot * counts[None, :], axis=1))
    positions = jnp.arange(SEQ, dtype=jnp.int32)
    pool_mask = ((positions[None, :] < lengths[:, None]) & (instruction == 0)).astype(jnp.float32)
    seed_grad = d_out.astype(jnp.float32) * pool_mask[:, :, None] * row_weight[:, None, None]
    group_rows = math.gcd(ROWS, max(1, 4096 // SEQ))
    count_groups = ROWS // group_rows

    def group_step(totals, inputs):
        ids_group, lengths_group, seed_group = inputs

        def local_forward(weights, rows_table):
            return forward(weights, rows_table, ids_group, lengths_group)
        result, pullback = jax.vjp(local_forward, params, table_full)
        grad_params, grad_table = pullback(seed_group)
        return ((jax.tree.map(jnp.add, totals[0], grad_params), totals[1] + grad_table), result)
    initial = (jax.tree.map(jnp.zeros_like, params), jnp.zeros_like(table_full))
    inputs = (token_ids.reshape(count_groups, group_rows, SEQ), lengths.reshape(count_groups, group_rows), seed_grad.reshape(count_groups, group_rows, SEQ, D))
    (grads, table_grad), results = lax.scan(group_step, initial, inputs)
    activations = results.reshape(ROWS, SEQ, D).astype(jnp.bfloat16)
    return (activations, table_grad, grads[0], grads[1], grads[2], grads[3], grads[4], grads[5], grads[6], grads[7], grads[8])
```

```python
import jax
import jax.numpy as jnp
from jax import lax
from jax.sharding import PartitionSpec as P

NB = 32
EPS = 1e-06
NEG = -1000000000.0
LIMITS = (12, 16, 23, 32, 46, 64, 91)
HIGH = lax.Precision.HIGHEST
LOW = jnp.bfloat16
F32 = jnp.float32


def bucket_of(offset):
    distance = jnp.abs(offset)
    far_bucket = 8 + sum(((distance >= limit).astype(jnp.int32) for limit in LIMITS))
    upper = jnp.where(offset > 0, 16, 0).astype(jnp.int32)
    return upper + jnp.where(distance < 8, distance, far_bucket)


def bucket_map(length):
    positions = jnp.arange(length, dtype=jnp.int32)
    return bucket_of(positions[None, :] - positions[:, None])


def normed(values, gains):
    return values * lax.rsqrt(jnp.mean(values * values, axis=-1, keepdims=True) + EPS) * gains


def norm_back(values, gains, cotangent):
    unused_out, pullback = jax.vjp(normed, values, gains)
    return pullback(cotangent)


def contract_rows(left, right):
    return lax.dot_general(left, right, (((0,), (0,)), ((), ())), preferred_element_type=F32)


def times_transposed(left, right):
    return lax.dot_general(left, right, (((1,), (1,)), ((), ())), preferred_element_type=F32)


def flip(value, bits):
    shards = lax.axis_size("fsdp")
    return lax.ppermute(value, "fsdp", [(i, i ^ bits) for i in range(shards)])


def gather_pieces(own):
    shards = lax.axis_size("fsdp")
    rows = own.shape[0]
    half = rows // 2
    pieces = [(0, 0, own)]
    if shards == 8:
        by_x = flip(own, 2)
        by_y = flip(own, 4)
        pieces += [(2, 0, by_x), (4, 0, by_y)]
        pieces += [(6, 0, flip(by_y[:half], 2)), (6, half, flip(by_x[half:], 4))]
    else:
        pieces += [(bits, 0, flip(own, bits)) for bits in range(2, shards, 2)]
    return pieces + [(bits ^ 1, first, flip(part, 1)) for bits, first, part in pieces]


def gather_rows(own, me):
    shards = lax.axis_size("fsdp")
    rows = own.shape[0]
    whole = jnp.zeros((shards * rows,) + own.shape[1:], own.dtype)
    for bits, first, part in gather_pieces(own):
        start = (me ^ bits) * rows + first
        whole = lax.dynamic_update_slice(whole, part, (start,) + (0,) * (own.ndim - 1))
    return whole


def scatter_sum(whole, me):
    shards, rows, columns = whole.shape
    half = rows // 2
    core = me & 1
    pairs = whole.reshape(shards // 2, 2, rows, columns)
    away = lax.dynamic_slice_in_dim(pairs, 1 - core, 1, axis=1)[:, 0].astype(LOW)
    mine = lax.dynamic_slice_in_dim(pairs, core, 1, axis=1)[:, 0]
    mine = mine + flip(away, 1).astype(F32)
    place = me >> 1

    def block(relative):
        return lax.dynamic_slice_in_dim(mine, place ^ relative, 1, axis=0)[0]

    if shards == 8:
        across = block(3).astype(LOW)
        from_x = flip(across[:half], 2).astype(F32)
        from_y = flip(across[half:], 4).astype(F32)
        to_y = block(2) + jnp.concatenate([from_x, jnp.zeros((rows - half, columns), F32)])
        to_x = block(1) + jnp.concatenate([jnp.zeros((half, columns), F32), from_y])
        return block(0) + flip(to_x.astype(LOW), 2).astype(F32) + flip(to_y.astype(LOW), 4).astype(F32)
    total = block(0)
    for relative in range(1, shards // 2):
        total = total + flip(block(relative).astype(LOW), 2 * relative).astype(F32)
    return total


def line_sum(own, at):
    chunks = own.shape[0]
    groups = lax.axis_size("dp")
    right = [(i, i + 1) for i in range(groups - 1)]
    left = [(i + 1, i) for i in range(groups - 1)]
    result = own
    zero = jnp.zeros(own.shape[1:], LOW)

    def run(pairs, place, result):
        came = zero
        for step in range(chunks + groups - 2):
            index = jnp.clip(step - place, 0, chunks - 1)
            part = lax.dynamic_index_in_dim(own, index, 0, keepdims=False)
            came = lax.ppermute((part + came.astype(F32)).astype(LOW), "dp", pairs)
            target = step - place + 1
            live = (target >= 0) & (target < chunks) & (place > 0)
            came = jnp.where(live, came, zero)
            spot = jnp.clip(target, 0, chunks - 1)
            before = lax.dynamic_index_in_dim(result, spot, 0, keepdims=False)
            result = lax.dynamic_update_index_in_dim(result, before + came.astype(F32), spot, 0)
        return result

    result = run(right, at, result)
    return run(left, groups - 1 - at, result)


def block_step(weights, embedded, lengths, seed):
    attn_gain, w_joint, w_out, ffn_gain, w_in, w_back, rel_bias = weights
    rows_dev, seq_len, model_width = seed.shape
    heads = rel_bias.shape[1]
    inner_width = w_out.shape[0]
    head_size = inner_width // heads
    tokens = rows_dev * seq_len
    first_gain = attn_gain.astype(F32)
    second_gain = ffn_gain.astype(F32)
    stream = embedded.astype(F32)
    normed_one = normed(stream, first_gain).astype(LOW)
    joint = jnp.dot(normed_one, w_joint, preferred_element_type=F32).astype(LOW)
    split_heads = joint.reshape(rows_dev, seq_len, 3, heads, head_size)
    bucket_hot = (
        bucket_map(seq_len).reshape(seq_len * seq_len, 1) == jnp.arange(NB, dtype=jnp.int32)[None, :]
    ).astype(F32)
    bias = jnp.dot(bucket_hot, rel_bias.astype(F32), precision=HIGH).T.reshape(heads, seq_len, seq_len)
    positions = jnp.arange(seq_len, dtype=jnp.int32)
    key_usable = positions[None, :] < lengths[:, None]

    def row_scores(queries_row, keys_row, usable_row):
        scores = jnp.einsum("qhd,khd->hqk", queries_row, keys_row, preferred_element_type=F32) + bias
        return jnp.where(usable_row[None, None, :], scores, NEG)

    saved = []
    attended = []
    for row in range(rows_dev):
        queries_row, keys_row, values_row = (split_heads[row, :, part] for part in range(3))
        scores = row_scores(queries_row, keys_row, key_usable[row])
        largest = jnp.max(scores, axis=-1, keepdims=True)
        raised = jnp.exp(scores - largest)
        totals = jnp.sum(raised, axis=-1, keepdims=True)
        probs = raised / totals
        mixed = jnp.einsum("hqk,khd->qhd", probs.astype(LOW), values_row, preferred_element_type=F32)
        attended.append(mixed.astype(LOW))
        saved.append(largest + jnp.log(totals))
    flat_attended = jnp.stack(attended).reshape(tokens, inner_width)
    hidden = stream + jnp.dot(flat_attended, w_out, preferred_element_type=F32)
    normed_two = normed(hidden, second_gain).astype(LOW)
    pre_act = jnp.dot(normed_two, w_in, preferred_element_type=F32)
    activated = jax.nn.gelu(pre_act).astype(LOW)
    result = hidden + jnp.dot(activated, w_back, preferred_element_type=F32)
    grad_out = seed.reshape(tokens, model_width)
    grad_low = grad_out.astype(LOW)
    grad_back = contract_rows(activated, grad_low)
    unused_act, gelu_pull = jax.vjp(jax.nn.gelu, pre_act)
    grad_pre = gelu_pull(times_transposed(grad_low, w_back))[0].astype(LOW)
    grad_in = contract_rows(normed_two, grad_pre)
    grad_hidden_norm, grad_second = norm_back(hidden, second_gain, times_transposed(grad_pre, w_in))
    grad_hidden = grad_out + grad_hidden_norm
    grad_hidden_low = grad_hidden.astype(LOW)
    grad_out_weight = contract_rows(flat_attended, grad_hidden_low)
    grad_attended = (
        times_transposed(grad_hidden_low, w_out).astype(LOW).reshape(rows_dev, seq_len, heads, head_size)
    )
    score_total = 0.0
    grad_joint = []
    for row in range(rows_dev):
        queries_row, keys_row, values_row = (split_heads[row, :, part] for part in range(3))
        grad_row = grad_attended[row]
        probs = jnp.exp(row_scores(queries_row, keys_row, key_usable[row]) - saved[row])
        grad_values = jnp.einsum("hqk,qhd->khd", probs.astype(LOW), grad_row, preferred_element_type=F32)
        grad_probs = jnp.einsum("qhd,khd->hqk", grad_row, values_row, preferred_element_type=F32)
        grad_scores = (probs * (grad_probs - jnp.sum(probs * grad_probs, axis=-1, keepdims=True))).astype(LOW)
        grad_queries = jnp.einsum("hqk,khd->qhd", grad_scores, keys_row, preferred_element_type=F32)
        grad_keys = jnp.einsum("hqk,qhd->khd", grad_scores, queries_row, preferred_element_type=F32)
        score_total = score_total + grad_scores.astype(F32)
        grad_joint.append(
            jnp.stack([grad_queries.astype(LOW), grad_keys.astype(LOW), grad_values.astype(LOW)], axis=1)
        )
    grad_joint = jnp.stack(grad_joint).reshape(tokens, 3 * inner_width)
    grad_w_joint = contract_rows(normed_one, grad_joint)
    grad_stream_norm, grad_first = norm_back(stream, first_gain, times_transposed(grad_joint, w_joint))
    grad_rel = lax.dot_general(
        bucket_hot,
        score_total.reshape(heads, seq_len * seq_len),
        (((0,), (1,)), ((), ())),
        precision=HIGH,
        preferred_element_type=F32,
    )
    return (
        result,
        grad_hidden + grad_stream_norm,
        grad_back,
        grad_in,
        grad_out_weight,
        grad_w_joint,
        grad_first,
        grad_second,
        grad_rel,
    )


def per_device(
    token_ids,
    task_ids,
    lengths,
    instruction,
    table,
    attn_gain,
    w_query,
    w_key,
    w_value,
    w_out,
    ffn_gain,
    w_in,
    w_back,
    rel_bias,
    d_out,
):
    rows_dev, seq_len = token_ids.shape
    vshard, model_width = table.shape
    inner_width = w_query.shape[1]
    ff_width = w_in.shape[1]
    shards = lax.axis_size("fsdp")
    groups = lax.axis_size("dp")
    me = lax.axis_index("fsdp")
    at = lax.axis_index("dp")
    token_count = rows_dev * seq_len
    capacity = 2 * token_count // shards
    task_count = rows_dev * groups * shards // 4

    flat_ids = token_ids.reshape(token_count)
    owner = flat_ids // vshard
    local_row = flat_ids - owner * vshard
    relative = owner ^ me
    relative_hot = (relative[:, None] == jnp.arange(shards, dtype=jnp.int32)[None, :]).astype(jnp.int32)
    rank_within = jnp.sum((jnp.cumsum(relative_hot, axis=0) - relative_hot) * relative_hot, axis=1)
    slot = relative * capacity + rank_within
    slots = jnp.arange(shards * capacity, dtype=jnp.int32)
    slot_hot = slots[:, None] == slot[None, :]
    requests = (jnp.sum(jnp.where(slot_hot, local_row[None, :] + 1, 0), axis=1) - 1).reshape(shards, capacity)
    asked = [requests[0]] + [flip(requests[r], r) for r in range(1, shards)]
    looked = [jnp.take(table, jnp.maximum(ids, 0), axis=0) for ids in asked]
    replies = [looked[0]] + [flip(looked[r], r) for r in range(1, shards)]
    embedded = jnp.take(jnp.concatenate(replies, axis=0), slot, axis=0)

    task_hot = (task_ids[:, None] == jnp.arange(task_count, dtype=jnp.int32)[None, :]).astype(F32)
    counts = jnp.sum(task_hot, axis=0)
    bits = 1
    while bits < shards:
        counts = counts + flip(counts, bits)
        bits *= 2
    bits = 1
    while bits < groups:
        counts = counts + lax.ppermute(counts, "dp", [(i, i ^ bits) for i in range(groups)])
        bits *= 2
    row_weight = 1.0 / jnp.dot(task_hot, counts, precision=HIGH)
    positions = jnp.arange(seq_len, dtype=jnp.int32)
    pool_mask = ((positions[None, :] < lengths[:, None]) & (instruction == 0)).astype(F32)
    seed_grad = d_out.astype(F32) * pool_mask[:, :, None] * row_weight[:, None, None]

    small = jnp.concatenate([attn_gain, ffn_gain, rel_bias.reshape(-1)])
    joint_width = 3 * inner_width
    small_rows = -(-small.shape[0] // joint_width)
    small = jnp.pad(small, (0, small_rows * joint_width - small.shape[0])).reshape(small_rows, joint_width)
    small_all = gather_rows(small, me).reshape(shards, small_rows * joint_width)
    own_gain = attn_gain.shape[0]
    attn_gain_all = small_all[:, :own_gain].reshape(-1)
    ffn_gain_all = small_all[:, own_gain : 2 * own_gain].reshape(-1)
    rel_all = small_all[:, 2 * own_gain : 2 * own_gain + rel_bias.size].reshape(NB, rel_bias.shape[1])
    weights = (
        attn_gain_all,
        gather_rows(jnp.concatenate([w_query, w_key, w_value], axis=1), me),
        gather_rows(w_out, me),
        ffn_gain_all,
        gather_rows(w_in, me),
        gather_rows(w_back, me),
        rel_all,
    )
    result, token_grads, grad_back, grad_in, grad_out_weight, grad_w_joint, grad_first, grad_second, grad_rel = (
        block_step(weights, embedded, lengths, seed_grad)
    )

    def owned(grad, chunks):
        own_rows = grad.shape[0] // shards
        part = scatter_sum(grad.reshape(shards, own_rows, -1), me)
        return line_sum(part.reshape(chunks, own_rows // chunks, -1), at).reshape(part.shape)

    grad_back = owned(grad_back, 4)
    grad_in = owned(grad_in, 4)
    grad_out_weight = owned(grad_out_weight, 1)
    grad_w_joint = owned(grad_w_joint, 2)
    small_grad = jnp.concatenate(
        [grad_first.reshape(shards, -1), grad_second.reshape(shards, -1), grad_rel.reshape(shards, -1)], axis=1
    )
    small_size = small_grad.shape[1]
    small_grad = jnp.pad(small_grad, ((0, 0), (0, 256 - small_size))).reshape(shards, 2, 128)
    small_grad = line_sum(scatter_sum(small_grad, me)[None], at).reshape(-1)
    grad_first = small_grad[:own_gain]
    grad_second = small_grad[own_gain : 2 * own_gain]
    grad_rel = small_grad[2 * own_gain : small_size].reshape(rel_bias.shape)

    outgoing = jnp.dot(slot_hot.astype(LOW), token_grads.astype(LOW), preferred_element_type=F32).astype(LOW)
    outgoing = outgoing.reshape(shards, capacity, model_width)
    incoming = [outgoing[0]] + [flip(outgoing[r], r) for r in range(1, shards)]
    incoming = jnp.concatenate(incoming, axis=0)
    asked = jnp.concatenate(asked, axis=0)
    chunk_rows = 256
    chunks = -(-vshard // chunk_rows)
    table_rows = jnp.arange(chunks * chunk_rows, dtype=jnp.int32)
    row_hot = (table_rows[:, None] == asked[None, :]).astype(LOW)
    table_part = jnp.dot(row_hot, incoming, preferred_element_type=F32)
    table_grad = line_sum(table_part.reshape(chunks, chunk_rows, model_width), at)
    table_grad = table_grad.reshape(chunks * chunk_rows, model_width)[:vshard]

    activations = result.reshape(rows_dev, seq_len, model_width).astype(LOW)
    return (
        activations,
        table_grad,
        grad_first,
        grad_w_joint[:, :inner_width],
        grad_w_joint[:, inner_width : 2 * inner_width],
        grad_w_joint[:, 2 * inner_width :],
        grad_out_weight,
        grad_second,
        grad_in,
        grad_back,
        grad_rel,
    )


def solution(mesh):
    both = ("dp", "fsdp")
    in_specs = (
        P(both, None),
        P(both),
        P(both),
        P(both, None),
        P("fsdp", None),
        P("fsdp"),
        P("fsdp", None),
        P("fsdp", None),
        P("fsdp", None),
        P("fsdp", None),
        P("fsdp"),
        P("fsdp", None),
        P("fsdp", None),
        P("fsdp", None),
        P(both, None, None),
    )
    out_specs = (
        P(both, None, None),
        P("fsdp", None),
        P("fsdp"),
        P("fsdp", None),
        P("fsdp", None),
        P("fsdp", None),
        P("fsdp", None),
        P("fsdp"),
        P("fsdp", None),
        P("fsdp", None),
        P("fsdp", None),
    )
    return jax.shard_map(per_device, mesh=mesh, in_specs=in_specs, out_specs=out_specs, check_vma=False)
```

```python
import functools
import jax
import jax.numpy as jnp
from jax import lax
from jax.experimental import pallas as pl
from jax.experimental.pallas import tpu as pltpu
from jax.sharding import PartitionSpec as P

EPS = 1e-06
NEG = -1000000000.0
LIMITS = (12, 16, 23, 32, 46, 64, 91)
HIGH = lax.Precision.HIGHEST
LOW = jnp.bfloat16
F32 = jnp.float32
VMEM_LIMIT = 56 * 1024 * 1024
PAIR = 128
ROOT = (2.0 / 3.141592653589793) ** 0.5
CUBE = 0.044715


def dot(left, right):
    return jnp.dot(left, right, preferred_element_type=F32)


def dot_nt(left, right):
    return lax.dot_general(left, right, (((1,), (1,)), ((), ())), preferred_element_type=F32)


def dot_tn(left, right):
    return lax.dot_general(left, right, (((0,), (0,)), ((), ())), preferred_element_type=F32)


def params():
    return pltpu.CompilerParams(vmem_limit_bytes=VMEM_LIMIT)


def half_lanes(size):
    return lax.broadcasted_iota(jnp.int32, (size, PAIR), 1) < PAIR // 2


def spread_bias(diagonal, seq_len):
    wide = jnp.broadcast_to(diagonal, (seq_len, 2 * seq_len))
    wide = pltpu.roll(wide, seq_len + 1, 1, stride=1, stride_axis=0)
    return wide[:, :seq_len]


def gather_bias(grad):
    seq_len = grad.shape[0]
    blocks = seq_len // PAIR
    total = None
    for block in range(blocks):
        ahead = PAIR * (blocks - 1 - block)
        parts = [grad[block * PAIR : (block + 1) * PAIR, :], jnp.zeros((PAIR, seq_len - ahead), F32)]
        if ahead:
            parts = [jnp.zeros((PAIR, ahead), F32)] + parts
        wide = jnp.concatenate(parts, axis=1)
        total = wide if total is None else total + wide
    eight = None
    for group in range(PAIR // 8):
        moved = pltpu.roll(total[8 * group : 8 * group + 8, :], PAIR - 8 - 8 * group, 1)
        eight = moved if eight is None else eight + moved
    return sum(pltpu.roll(eight[sub : sub + 1, :], 7 - sub, 1) for sub in range(8))


def attend_kernel(lengths_ref, diagonal_ref, query_ref, key_ref, value_ref, out_ref, log_ref):
    rows = lengths_ref.shape[0]
    seq_len = query_ref.shape[0] // rows
    first = half_lanes(seq_len)
    key_at = lax.broadcasted_iota(jnp.int32, (seq_len, 1), 0)
    results = [[None, None] for _ in range(rows)]
    for head in range(2):
        bias = spread_bias(diagonal_ref[0, head : head + 1, :], seq_len)
        for row in range(rows):
            span = pl.ds(row * seq_len, seq_len)
            queries = query_ref[span, :]
            queries = jnp.where(first if head == 0 else ~first, queries, jnp.zeros_like(queries))
            scores = dot_nt(key_ref[span, :], queries) + bias
            scores = jnp.where(key_at < lengths_ref[row], scores, NEG)
            largest = jnp.max(scores, axis=0, keepdims=True)
            raised = jnp.exp(scores - largest)
            totals = jnp.sum(raised, axis=0, keepdims=True)
            probs = (raised * (1.0 / totals)).astype(LOW)
            results[row][head] = dot_tn(probs, value_ref[span, :])
            log_ref[0, 2 * row + head : 2 * row + head + 1, :] = largest + jnp.log(totals)
    for row in range(rows):
        out_ref[pl.ds(row * seq_len, seq_len), :] = jnp.where(first, *results[row]).astype(LOW)


def attend(lengths, diagonal, joint, heads):
    tokens = joint.shape[0]
    pairs = heads // 2
    rows = lengths.shape[0]
    seq_len = tokens // rows
    return pl.pallas_call(
        attend_kernel,
        grid=(pairs,),
        in_specs=[
            pl.BlockSpec(memory_space=pltpu.SMEM),
            pl.BlockSpec((1, 2, 2 * seq_len), lambda p: (p, 0, 0)),
            pl.BlockSpec((tokens, PAIR), lambda p: (0, p)),
            pl.BlockSpec((tokens, PAIR), lambda p: (0, pairs + p)),
            pl.BlockSpec((tokens, PAIR), lambda p: (0, 2 * pairs + p)),
        ],
        out_specs=[
            pl.BlockSpec((tokens, PAIR), lambda p: (0, p)),
            pl.BlockSpec((1, 2 * rows, seq_len), lambda p: (p, 0, 0)),
        ],
        out_shape=[
            jax.ShapeDtypeStruct((tokens, pairs * PAIR), LOW),
            jax.ShapeDtypeStruct((pairs, 2 * rows, seq_len), F32),
        ],
        compiler_params=params(),
        name="attend",
    )(lengths, diagonal.reshape(pairs, 2, 2 * seq_len), joint, joint, joint)


def attend_back_kernel(
    lengths_ref, diagonal_ref, query_ref, key_ref, value_ref, grad_ref, log_ref,
    query_out, key_out, value_out, bias_out,
):
    rows = lengths_ref.shape[0]
    seq_len = query_ref.shape[0] // rows
    first = half_lanes(seq_len)
    key_at = lax.broadcasted_iota(jnp.int32, (seq_len, 1), 0)
    results = [[None, None] for _ in range(rows)]
    for head in range(2):
        bias = spread_bias(diagonal_ref[0, head : head + 1, :], seq_len)
        keep = first if head == 0 else ~first
        total = None
        for row in range(rows):
            span = pl.ds(row * seq_len, seq_len)
            queries = query_ref[span, :]
            keys = key_ref[span, :]
            values = value_ref[span, :]
            grads = grad_ref[span, :]
            only = jnp.where(keep, queries, jnp.zeros_like(queries))
            scores = dot_nt(keys, only) + bias
            scores = jnp.where(key_at < lengths_ref[row], scores, NEG)
            probs = jnp.exp(scores - log_ref[0, 2 * row + head : 2 * row + head + 1, :])
            grad_values = dot(probs.astype(LOW), grads)
            grad_only = jnp.where(keep, grads, jnp.zeros_like(grads))
            grad_probs = dot_nt(values, grad_only)
            weighted = jnp.sum(probs * grad_probs, axis=0, keepdims=True)
            grad_scores = (probs * (grad_probs - weighted)).astype(LOW)
            grad_keys = dot(grad_scores, queries)
            grad_queries = dot_tn(grad_scores, keys)
            wide = grad_scores.astype(F32)
            total = wide if total is None else total + wide
            results[row][head] = (grad_queries, grad_keys, grad_values)
        bias_out[0, head : head + 1, :] = gather_bias(total)
    for row in range(rows):
        span = pl.ds(row * seq_len, seq_len)
        for out_ref, one, two in zip((query_out, key_out, value_out), *results[row]):
            out_ref[span, :] = jnp.where(first, one, two).astype(LOW)


def attend_back(lengths, diagonal, joint, grad_attended, logs, heads):
    tokens = joint.shape[0]
    pairs = heads // 2
    rows = lengths.shape[0]
    seq_len = tokens // rows
    part = pl.BlockSpec((tokens, PAIR), lambda p: (0, p))
    whole = jax.ShapeDtypeStruct((tokens, pairs * PAIR), LOW)
    lines = pl.BlockSpec((1, 2, 2 * seq_len), lambda p: (p, 0, 0))
    outs = pl.pallas_call(
        attend_back_kernel,
        grid=(pairs,),
        in_specs=[
            pl.BlockSpec(memory_space=pltpu.SMEM),
            lines,
            part,
            pl.BlockSpec((tokens, PAIR), lambda p: (0, pairs + p)),
            pl.BlockSpec((tokens, PAIR), lambda p: (0, 2 * pairs + p)),
            part,
            pl.BlockSpec((1, 2 * rows, seq_len), lambda p: (p, 0, 0)),
        ],
        out_specs=[part, part, part, lines],
        out_shape=[whole, whole, whole, jax.ShapeDtypeStruct((pairs, 2, 2 * seq_len), F32)],
        compiler_params=params(),
        name="attend_back",
    )(lengths, diagonal.reshape(pairs, 2, 2 * seq_len), joint, joint, joint, grad_attended, logs)
    return outs[0], outs[1], outs[2], outs[3].reshape(heads, 2 * seq_len)


def load_weights(me, loads, refs, targets, semaphores):
    pending = []
    for number, (source, target, column, relative, shard_rows, first, start, rows) in enumerate(loads):
        into = targets[target]
        width = refs[source].shape[1]
        place = first if relative is None else pl.multiple_of((me ^ relative) * shard_rows + first, 16)
        copy = pltpu.make_async_copy(
            refs[source].at[pl.ds(start, rows), :],
            into.at[pl.ds(place, rows), pl.ds(column, width)],
            semaphores.at[number],
        )
        copy.start()
        pending.append(copy)
    for copy in pending:
        copy.wait()


def plan_loads(pieces, sections):
    loads = []
    for source, (relative, first, part) in enumerate(pieces):
        start = 0
        for target, rows, column, shard_rows, offset in sections:
            low = max(start, first)
            high = min(start + rows, first + part.shape[0])
            if low < high:
                loads.append((source, target, column, relative, shard_rows, offset + low - start, low - first, high - low))
            start += rows
    return loads


def front_kernel(loads, count, me_ref, slot_ref, reply_ref, gain_ref, *rest):
    refs, (x_ref, normed_ref, joint_ref), (weight, semaphores) = rest[:count], rest[count : count + 3], rest[count + 3 :]

    @pl.when(pl.program_id(0) == 0)
    def _():
        load_weights(me_ref[0], loads, refs, [weight], semaphores)

    rows = slot_ref.shape[0]
    slots = reply_ref.shape[0]
    hot = slot_ref[...] == lax.broadcasted_iota(jnp.int32, (rows, slots), 1)
    x = dot(hot.astype(F32).astype(LOW), reply_ref[...])
    x_ref[...] = x.astype(LOW)
    scale = lax.rsqrt(jnp.mean(x * x, axis=-1, keepdims=True) + EPS)
    normed = (x * scale * gain_ref[...]).astype(LOW)
    normed_ref[...] = normed
    joint_ref[...] = dot(normed, weight[...]).astype(LOW)


ANY = pl.BlockSpec(memory_space=pl.ANY)
SMEM = pl.BlockSpec(memory_space=pltpu.SMEM)
BLOCK = 256


def full(shape):
    return pl.BlockSpec(shape, lambda *ids: (0,) * len(shape))


def down(width, rows=BLOCK):
    return pl.BlockSpec((rows, width), lambda i: (i, 0))


def front(me, slot, replies, gain, pieces, loads, width):
    tokens = slot.shape[0]
    model = replies.shape[1]
    return pl.pallas_call(
        functools.partial(front_kernel, loads, len(pieces)),
        grid=(tokens // BLOCK,),
        in_specs=[SMEM, down(1), full(replies.shape), full((1, model))] + [ANY] * len(pieces),
        out_specs=[down(model), down(model), down(width)],
        out_shape=[
            jax.ShapeDtypeStruct((tokens, model), LOW),
            jax.ShapeDtypeStruct((tokens, model), LOW),
            jax.ShapeDtypeStruct((tokens, width), LOW),
        ],
        scratch_shapes=[pltpu.VMEM((model, width), LOW), pltpu.SemaphoreType.DMA((len(loads),))],
        compiler_params=params(),
        name="front",
    )(me, slot, replies, gain, *pieces)


def ffn_kernel(loads, count, me_ref, x_ref, attended_ref, d_out_ref, seed_ref, gain_ref, *rest):
    refs = rest[:count]
    (y_ref, act_ref, grad_pre_ref, grad_low_ref, normed_ref, hidden_out, low_out, attended_out, gain_out) = rest[count : count + 9]
    w_out, w_in, w_back, semaphores = rest[count + 9 :]

    @pl.when(pl.program_id(0) == 0)
    def _():
        load_weights(me_ref[0], loads, refs, [w_out, w_in, w_back], semaphores)
        gain_out[...] = jnp.zeros_like(gain_out)

    hidden = x_ref[...].astype(F32) + dot(attended_ref[...], w_out[...])
    scale = lax.rsqrt(jnp.mean(hidden * hidden, axis=-1, keepdims=True) + EPS)
    unit = hidden * scale
    gain = gain_ref[...]
    normed = (unit * gain).astype(LOW)
    normed_ref[...] = normed
    grad_out = d_out_ref[...].astype(F32) * seed_ref[...]
    grad_low = grad_out.astype(LOW)
    grad_low_ref[...] = grad_low
    result = hidden
    back = jnp.zeros_like(hidden)
    model = hidden.shape[1]
    for start in range(0, w_in.shape[1], model):
        span = pl.ds(start, model)
        pre = dot(normed, w_in[:, span])
        square = pre * pre
        tanh = jnp.tanh(ROOT * (pre + CUBE * square * pre))
        half = 0.5 * (1.0 + tanh)
        act = (pre * half).astype(LOW)
        slope = half + 0.5 * pre * (1.0 - tanh * tanh) * ROOT * (1.0 + 3.0 * CUBE * square)
        act_ref[:, span] = act
        result = result + dot(act, w_back[span, :])
        grad_pre = (dot_nt(grad_low, w_back[span, :]) * slope).astype(LOW)
        grad_pre_ref[:, span] = grad_pre
        back = back + dot_nt(grad_pre, w_in[:, span])
    y_ref[...] = result.astype(LOW)
    gain_out[...] += jnp.sum(back * unit, axis=0, keepdims=True)
    scaled = back * gain
    grad_hidden = grad_out + scale * (scaled - unit * jnp.mean(scaled * unit, axis=-1, keepdims=True))
    hidden_out[...] = grad_hidden
    low = grad_hidden.astype(LOW)
    low_out[...] = low
    attended_out[...] = dot_nt(low, w_out[...]).astype(LOW)


def ffn(me, x, attended, d_out, seed, gain, pieces, loads, inner, ff_width):
    tokens, model = x.shape
    low = jax.ShapeDtypeStruct((tokens, model), LOW)
    wide = jax.ShapeDtypeStruct((tokens, ff_width), LOW)
    return pl.pallas_call(
        functools.partial(ffn_kernel, loads, len(pieces)),
        grid=(tokens // BLOCK,),
        in_specs=[SMEM, down(model), down(inner), down(model), down(1), full((1, model))] + [ANY] * len(pieces),
        out_specs=[
            down(model), down(ff_width), down(ff_width), down(model), down(model), down(model), down(model), down(inner),
            full((1, model)),
        ],
        out_shape=[
            low, wide, wide, low, low, jax.ShapeDtypeStruct((tokens, model), F32), low,
            jax.ShapeDtypeStruct((tokens, inner), LOW), jax.ShapeDtypeStruct((1, model), F32),
        ],
        scratch_shapes=[
            pltpu.VMEM((inner, model), LOW),
            pltpu.VMEM((model, ff_width), LOW),
            pltpu.VMEM((ff_width, model), LOW),
            pltpu.SemaphoreType.DMA((len(loads),)),
        ],
        compiler_params=params(),
        name="ffn",
    )(me, x, attended, d_out, seed, gain, *pieces)


def project_back_kernel(loads, count, me_ref, query_ref, key_ref, value_ref, x_ref, hidden_ref, gain_ref, *rest):
    refs, (out_ref, gain_out), (weight, semaphores) = rest[:count], rest[count : count + 2], rest[count + 2 :]

    @pl.when(pl.program_id(0) == 0)
    def _():
        load_weights(me_ref[0], loads, refs, [weight], semaphores)
        gain_out[...] = jnp.zeros_like(gain_out)

    inner = query_ref.shape[1]
    back = dot_nt(query_ref[...], weight[:, :inner])
    back = back + dot_nt(key_ref[...], weight[:, inner : 2 * inner])
    back = back + dot_nt(value_ref[...], weight[:, 2 * inner :])
    x = x_ref[...].astype(F32)
    scale = lax.rsqrt(jnp.mean(x * x, axis=-1, keepdims=True) + EPS)
    unit = x * scale
    gain_out[...] += jnp.sum(back * unit, axis=0, keepdims=True)
    scaled = back * gain_ref[...]
    grad = hidden_ref[...] + scale * (scaled - unit * jnp.mean(scaled * unit, axis=-1, keepdims=True))
    out_ref[...] = grad.astype(LOW)


def project_back(me, grads, x, grad_hidden, gain, pieces, loads):
    tokens, model = x.shape
    inner = grads[0].shape[1]
    return pl.pallas_call(
        functools.partial(project_back_kernel, loads, len(pieces)),
        grid=(tokens // BLOCK,),
        in_specs=[SMEM] + [down(inner)] * 3 + [down(model), down(model), full((1, model))] + [ANY] * len(pieces),
        out_specs=[down(model), full((1, model))],
        out_shape=[jax.ShapeDtypeStruct((tokens, model), LOW), jax.ShapeDtypeStruct((1, model), F32)],
        scratch_shapes=[pltpu.VMEM((model, 3 * inner), LOW), pltpu.SemaphoreType.DMA((len(loads),))],
        compiler_params=params(),
        name="project_back",
    )(me, *grads, x, grad_hidden, gain, *pieces)


def store_shards(me, value, shards, keep_ref, send_ref, columns):
    rows = value.shape[0] // shards
    for shard in range(shards):
        relative = me ^ shard
        part = value[shard * rows : (shard + 1) * rows, :]

        @pl.when(relative % 2 == 0)
        def _():
            keep_ref[relative // 2, :, columns] = part

        @pl.when(relative % 2 == 1)
        def _():
            send_ref[relative // 2, :, columns] = part.astype(LOW)


def rows_grad_kernel(shards, me_ref, left_ref, *rest):
    rights, (keep_ref, send_ref) = rest[:-2], rest[-2:]
    start = 0
    for right_ref in rights:
        value = dot_tn(left_ref[...], right_ref[...])
        store_shards(me_ref[0], value, shards, keep_ref, send_ref, pl.ds(start, value.shape[1]))
        start += value.shape[1]


def rows_grad(me, left, rights, shards, columns):
    tokens, width = left.shape
    total = sum(right.shape[1] for right in rights)
    steps = total // columns if len(rights) == 1 else 1
    each = columns if len(rights) == 1 else total
    shape = (shards // 2, width // shards, total)
    out = pl.BlockSpec((shards // 2, width // shards, each), lambda i: (0, 0, i))
    return pl.pallas_call(
        functools.partial(rows_grad_kernel, shards),
        grid=(steps,),
        in_specs=[SMEM, full(left.shape)]
        + [pl.BlockSpec((tokens, columns), lambda i: (0, i)) for right in rights],
        out_specs=[out, out],
        out_shape=[jax.ShapeDtypeStruct(shape, F32), jax.ShapeDtypeStruct(shape, LOW)],
        compiler_params=params(),
        name="rows_grad",
    )(me, left, *rights)


def blocks_grad_kernel(me_ref, keep_left, send_left, right_ref, keep_ref, send_ref):
    right = right_ref[...]
    keep_ref[0] = dot_tn(keep_left[...], right)
    send_ref[0] = dot_tn(send_left[...], right).astype(LOW)


def blocks_grad(me, left, right, shards):
    tokens, width = left.shape
    rows = width // shards
    shape = (shards // 2, rows, right.shape[1])
    out = pl.BlockSpec((1, rows, right.shape[1]), lambda i, me: (i, 0, 0))
    return pl.pallas_call(
        blocks_grad_kernel,
        grid_spec=pltpu.PrefetchScalarGridSpec(
            num_scalar_prefetch=1,
            grid=(shards // 2,),
            in_specs=[
                pl.BlockSpec((tokens, rows), lambda i, me: (0, me[0] ^ (2 * i))),
                pl.BlockSpec((tokens, rows), lambda i, me: (0, me[0] ^ (2 * i + 1))),
                pl.BlockSpec(right.shape, lambda i, me: (0, 0)),
            ],
            out_specs=[out, out],
        ),
        out_shape=[jax.ShapeDtypeStruct(shape, F32), jax.ShapeDtypeStruct(shape, LOW)],
        compiler_params=params(),
        name="blocks_grad",
    )(me, left, left, right)


def place_kernel(pieces, slot_ref, token_ref, *outs):
    capacity = outs[0].shape[0]
    tokens = token_ref.shape[0]
    at = lax.broadcasted_iota(jnp.int32, (capacity, tokens), 0)
    for number, out_ref in enumerate(outs):
        hot = (at + number * capacity) == slot_ref[...]
        out_ref[...] = dot(hot.astype(F32).astype(LOW), token_ref[...]).astype(LOW)


def place(slot, tokens, shards, capacity):
    model = tokens.shape[1]
    return pl.pallas_call(
        functools.partial(place_kernel, shards),
        in_specs=[full((1, tokens.shape[0])), full(tokens.shape)],
        out_specs=[full((capacity, model))] * shards,
        out_shape=[jax.ShapeDtypeStruct((capacity, model), LOW)] * shards,
        compiler_params=params(),
        name="place",
    )(slot, tokens)


TABLE_BLOCK = 512


def table_kernel(count, ids_ref, *rest):
    pieces = rest[:count]
    out_ref, stacked = rest[-2:]
    step = pl.program_id(0)

    @pl.when(step == 0)
    def _():
        capacity = pieces[0].shape[0]
        for number, piece in enumerate(pieces):
            stacked[pl.ds(number * capacity, capacity), :] = piece[...]

    rows = out_ref.shape[0]
    at = lax.broadcasted_iota(jnp.int32, (rows, ids_ref.shape[1]), 0) + step * rows
    total = dot((at == ids_ref[...]).astype(F32).astype(LOW), stacked[...])
    if len(rest) > count + 2:
        total = total + rest[count][...]
    out_ref[...] = total


def add_to_table(ids, pieces, before, vshard):
    model = pieces[0].shape[1]
    slots = ids.shape[1]
    more = [] if before is None else [before]
    return pl.pallas_call(
        functools.partial(table_kernel, len(pieces)),
        grid=(pl.cdiv(vshard, TABLE_BLOCK),),
        in_specs=[full(ids.shape)] + [full(pieces[0].shape)] * len(pieces) + [down(model, TABLE_BLOCK)] * len(more),
        out_specs=down(model, TABLE_BLOCK),
        out_shape=jax.ShapeDtypeStruct((vshard, model), F32),
        input_output_aliases={1 + len(pieces): 0} if more else {},
        scratch_shapes=[pltpu.VMEM((slots, model), LOW)],
        compiler_params=params(),
        name="table_rows",
    )(ids, *pieces, *more)


def flip(value, bits):
    shards = lax.axis_size("fsdp")
    return lax.ppermute(value, "fsdp", [(i, i ^ bits) for i in range(shards)])


def flip_line(value, bits):
    groups = lax.axis_size("dp")
    return lax.ppermute(value, "dp", [(i, i ^ bits) for i in range(groups)])


def gather_pieces(own):
    half = own.shape[0] // 32 * 16
    by_x = flip(own, 2)
    by_y = flip(own, 4)
    pieces = [(0, 0, own), (2, 0, by_x), (4, 0, by_y)]
    pieces += [(6, 0, flip(by_y[:half], 2)), (6, half, flip(by_x[half:], 4))]
    return pieces + [(bits ^ 1, first, flip(part, 1)) for bits, first, part in pieces]


def scatter_sum(keep, send):
    shards = lax.axis_size("fsdp")
    rows, columns = keep.shape[1:]
    mine = keep + flip(send, 1).astype(F32)
    if shards == 8:
        half = rows // 32 * 16
        across = mine[3].astype(LOW)
        from_x = flip(across[:half], 2).astype(F32)
        from_y = flip(across[half:], 4).astype(F32)
        to_y = mine[2] + jnp.concatenate([from_x, jnp.zeros((rows - half, columns), F32)])
        to_x = mine[1] + jnp.concatenate([jnp.zeros((half, columns), F32), from_y])
        return mine[0] + flip(to_x.astype(LOW), 2).astype(F32) + flip(to_y.astype(LOW), 4).astype(F32)
    total = mine[0]
    for relative in range(1, shards // 2):
        total = total + flip(mine[relative].astype(LOW), 2 * relative).astype(F32)
    return total


def bucket_of(offset):
    distance = jnp.abs(offset)
    far_bucket = 8 + sum(((distance >= limit).astype(jnp.int32) for limit in LIMITS))
    upper = jnp.where(offset > 0, 16, 0).astype(jnp.int32)
    return upper + jnp.where(distance < 8, distance, far_bucket)


def per_device(
    token_ids,
    task_ids,
    lengths,
    instruction,
    table,
    attn_gain,
    w_query,
    w_key,
    w_value,
    w_out,
    ffn_gain,
    w_in,
    w_back,
    rel_bias,
    d_out,
):
    rows_dev, seq_len = token_ids.shape
    vshard, model = table.shape
    inner = w_query.shape[1]
    ff_width = w_in.shape[1]
    heads = rel_bias.shape[1]
    shards = lax.axis_size("fsdp")
    groups = lax.axis_size("dp")
    me = lax.axis_index("fsdp")
    at = lax.axis_index("dp")
    me_ref = me.astype(jnp.int32).reshape(1)
    tokens = rows_dev * seq_len
    capacity = 2 * tokens // shards
    task_count = rows_dev * groups * shards // 4
    own_gain = attn_gain.shape[0]
    buckets = rel_bias.shape[0] * shards

    flat_ids = token_ids.reshape(tokens)
    owner = flat_ids // vshard
    local_row = flat_ids - owner * vshard
    relative = owner ^ me
    relative_hot = (relative[:, None] == jnp.arange(shards, dtype=jnp.int32)[None, :]).astype(LOW)
    token_at = jnp.arange(tokens, dtype=jnp.int32)
    before = (token_at[:, None] > token_at[None, :]).astype(LOW)
    ranks = jnp.dot(before, relative_hot, preferred_element_type=F32)
    rank_within = jnp.sum(ranks * relative_hot.astype(F32), axis=1).astype(jnp.int32)
    slot = relative * capacity + rank_within
    slots = jnp.arange(shards * capacity, dtype=jnp.int32)
    slot_hot = slots[:, None] == slot[None, :]
    requests = (jnp.sum(jnp.where(slot_hot, local_row[None, :] + 1, 0), axis=1) - 1).reshape(shards, capacity)
    asked = jnp.stack([requests[0]] + [flip(requests[r], r) for r in range(1, shards)])
    looked = jnp.take(table, jnp.maximum(asked, 0).reshape(-1), axis=0).reshape(shards, capacity, model)
    replies = jnp.concatenate([looked[0]] + [flip(looked[r], r) for r in range(1, shards)], axis=0)

    small = jnp.concatenate([attn_gain, ffn_gain, rel_bias.reshape(-1)])
    small_size = small.shape[0]
    joint_own = jnp.concatenate([w_query, w_key, w_value], axis=1)
    own_rows = w_query.shape[0]
    if shards == 8:
        extra = jnp.pad(small, (0, 16 * 3 * inner - small_size)).reshape(16, 3 * inner)
        joint_pieces = gather_pieces(jnp.concatenate([joint_own, extra]))
        joint_loads = plan_loads(joint_pieces, [(0, own_rows, 0, own_rows, 0)])
        lines = {
            bits: part[own_rows - first, :small_size]
            for bits, first, part in joint_pieces
            if first <= own_rows < first + part.shape[0]
        }
        small_all = jnp.stack([lines[bits] for bits in range(shards)])[jnp.arange(shards) ^ me]
        cuts = ff_width // model
        slab = jnp.concatenate([w_out] + [w_in[:, i * model : (i + 1) * model] for i in range(cuts)] + [w_back])
        sections = [(0, own_rows, 0, own_rows, 0)]
        sections += [(1, own_rows, i * model, own_rows, 0) for i in range(cuts)]
        sections += [(2, w_back.shape[0], 0, w_back.shape[0], 0)]
        ffn_pieces = gather_pieces(slab)
        ffn_loads = plan_loads(ffn_pieces, sections)
        joint_pieces = [part for unused_bits, unused_first, part in joint_pieces]
        ffn_pieces = [part for unused_bits, unused_first, part in ffn_pieces]
    else:
        joint_pieces, small_all, *ffn_pieces = (
            lax.all_gather(part, "fsdp", axis=0, tiled=True) for part in (joint_own, small[None], w_out, w_in, w_back)
        )
        joint_pieces = [joint_pieces]
        joint_loads = [(0, 0, 0, None, 0, 0, 0, model)]
        ffn_loads = [(i, i, 0, None, 0, 0, 0, part.shape[0]) for i, part in enumerate(ffn_pieces)]
    first_gain = small_all[:, :own_gain].reshape(1, model).astype(F32)
    second_gain = small_all[:, own_gain : 2 * own_gain].reshape(1, model).astype(F32)
    rel_all = small_all[:, 2 * own_gain :].reshape(buckets, heads).astype(F32)

    task_hot = (task_ids[:, None] == jnp.arange(task_count, dtype=jnp.int32)[None, :]).astype(F32)
    counts = jnp.sum(task_hot, axis=0)
    bits = 1
    while bits < shards:
        counts = counts + flip(counts, bits)
        bits *= 2
    bits = 1
    while bits < groups:
        counts = counts + flip_line(counts, bits)
        bits *= 2
    row_weight = 1.0 / jnp.sum(task_hot * counts[None, :], axis=1)
    positions = jnp.arange(seq_len, dtype=jnp.int32)
    pool_mask = ((positions[None, :] < lengths[:, None]) & (instruction == 0)).astype(F32)
    seed = (pool_mask * row_weight[:, None]).reshape(tokens, 1)

    offsets = (seq_len - 1) - jnp.arange(2 * seq_len, dtype=jnp.int32)
    bucket_hot = (jnp.arange(buckets, dtype=jnp.int32)[:, None] == bucket_of(offsets)[None, :]).astype(F32)
    diagonal = lax.dot_general(rel_all, bucket_hot, (((0,), (0,)), ((), ())), precision=HIGH)

    x, normed_one, joint = front(me_ref, slot[:, None], replies, first_gain, joint_pieces, joint_loads, 3 * inner)
    attended, logs = attend(lengths, diagonal, joint, heads)
    result, act, grad_pre, grad_low, normed_two, grad_hidden, hidden_low, grad_attended, grad_second = ffn(
        me_ref, x, attended, d_out.reshape(tokens, model), seed, second_gain, ffn_pieces, ffn_loads, inner, ff_width
    )
    if w_back.shape[0] % PAIR == 0:
        back_parts = blocks_grad(me_ref, act, grad_low, shards)
    else:
        back_parts = rows_grad(me_ref, act, [grad_low], shards, model // 3)
    in_parts = rows_grad(me_ref, normed_two, [grad_pre], shards, model)
    grad_back = scatter_sum(*back_parts)
    grad_in = scatter_sum(*in_parts)
    *grad_joint, bias_sums = attend_back(lengths, diagonal, joint, grad_attended, logs, heads)
    token_grads, grad_first = project_back(me_ref, grad_joint, x, grad_hidden, first_gain, joint_pieces, joint_loads)

    slot_of = [slot]
    asked_of = [asked]
    for bits in range(1, groups):
        theirs = flip_line(jnp.concatenate([slot, requests.reshape(-1)]), bits)
        slot_of.append(theirs[:tokens])
        asked_of.append(theirs[tokens:].reshape(shards, capacity))
    if groups > 1:
        away = jnp.stack(asked_of[1:], axis=1)
        away = jnp.stack([away[0]] + [flip(away[r], r) for r in range(1, shards)])
        asked_of = [asked] + [away[:, i] for i in range(groups - 1)]
    from_left = [token_grads]
    from_right = [token_grads]
    for step in range(1, groups):
        pairs = [(i, i + 1) for i in range(step - 1, groups - 1)]
        from_left.append(lax.ppermute(from_left[-1], "dp", pairs))
        from_right.append(lax.ppermute(from_right[-1], "dp", [(groups - 1 - i, groups - 1 - j) for i, j in pairs]))
    table_grad = None
    for bits in range(groups):
        block = token_grads
        if bits:
            distance = (at ^ bits) - at
            steps = sorted({(i ^ bits) - i for i in range(groups)})
            options = [from_right[step] if step > 0 else from_left[-step] for step in steps]
            block = options[0]
            for step, option in zip(steps[1:], options[1:]):
                block = jnp.where(distance == step, option, block)
        outgoing = place(slot_of[bits][None, :], block, shards, capacity)
        incoming = [outgoing[0]] + [flip(outgoing[r], r) for r in range(1, shards)]
        table_grad = add_to_table(asked_of[bits].reshape(1, -1), incoming, table_grad, vshard)

    joint_parts = rows_grad(me_ref, normed_one, grad_joint, shards, inner)
    out_parts = rows_grad(me_ref, attended, [hidden_low], shards, model)
    grad_w_joint = scatter_sum(*joint_parts)
    grad_out_weight = scatter_sum(*out_parts)
    grad_rel = lax.dot_general(bucket_hot, bias_sums, (((1,), (1,)), ((), ())), precision=HIGH)
    small_grad = jnp.concatenate(
        [grad_first.reshape(shards, -1), grad_second.reshape(shards, -1), grad_rel.reshape(shards, -1)], axis=1
    )
    small_grad = lax.psum(small_grad, ("dp", "fsdp"))[me]
    sums = lax.psum(tuple(part.astype(LOW) for part in (grad_back, grad_in, grad_out_weight, grad_w_joint)), "dp")
    grad_back, grad_in, grad_out_weight, grad_w_joint = (part.astype(F32) for part in sums)
    return (
        result.reshape(rows_dev, seq_len, model),
        table_grad,
        small_grad[:own_gain],
        grad_w_joint[:, :inner],
        grad_w_joint[:, inner : 2 * inner],
        grad_w_joint[:, 2 * inner :],
        grad_out_weight,
        small_grad[own_gain : 2 * own_gain],
        grad_in,
        grad_back,
        small_grad[2 * own_gain :].reshape(rel_bias.shape),
    )


def solution(mesh):
    both = ("dp", "fsdp")
    in_specs = (
        P(both, None),
        P(both),
        P(both),
        P(both, None),
        P("fsdp", None),
        P("fsdp"),
        P("fsdp", None),
        P("fsdp", None),
        P("fsdp", None),
        P("fsdp", None),
        P("fsdp"),
        P("fsdp", None),
        P("fsdp", None),
        P("fsdp", None),
        P(both, None, None),
    )
    out_specs = (
        P(both, None, None),
        P("fsdp", None),
        P("fsdp"),
        P("fsdp", None),
        P("fsdp", None),
        P("fsdp", None),
        P("fsdp", None),
        P("fsdp"),
        P("fsdp", None),
        P("fsdp", None),
        P("fsdp", None),
    )
    return jax.shard_map(per_device, mesh=mesh, in_specs=in_specs, out_specs=out_specs, check_vma=False)
```

```python
import functools
import jax
import jax.numpy as jnp
from jax import lax
from jax.experimental import pallas as pl
from jax.experimental.pallas import tpu as pltpu
from jax.sharding import PartitionSpec as P

EPS = 1e-06
NEG = -1000000000.0
LIMITS = (12, 16, 23, 32, 46, 64, 91)
HIGH = lax.Precision.HIGHEST
LOW = jnp.bfloat16
F32 = jnp.float32
VMEM_LIMIT = 56 * 1024 * 1024
PAIR = 128
ROOT = (2.0 / 3.141592653589793) ** 0.5
CUBE = 0.044715


def dot(left, right):
    return jnp.dot(left, right, preferred_element_type=F32)


def dot_nt(left, right):
    return lax.dot_general(left, right, (((1,), (1,)), ((), ())), preferred_element_type=F32)


def dot_tn(left, right):
    return lax.dot_general(left, right, (((0,), (0,)), ((), ())), preferred_element_type=F32)


def params():
    return pltpu.CompilerParams(vmem_limit_bytes=VMEM_LIMIT)


def cost(micros):
    return pl.CostEstimate(flops=int(micros * 1.15e9), bytes_accessed=int(micros * 3.6e6), transcendentals=0)


def half_lanes(size):
    return lax.broadcasted_iota(jnp.int32, (size, PAIR), 1) < PAIR // 2


def spread_bias(diagonal, seq_len):
    wide = jnp.broadcast_to(diagonal, (seq_len, 2 * seq_len))
    wide = pltpu.roll(wide, seq_len + 1, 1, stride=1, stride_axis=0)
    return wide[:, :seq_len]


def gather_bias(grad):
    seq_len = grad.shape[0]
    blocks = seq_len // PAIR
    total = None
    for block in range(blocks):
        ahead = PAIR * (blocks - 1 - block)
        parts = [grad[block * PAIR : (block + 1) * PAIR, :], jnp.zeros((PAIR, seq_len - ahead), F32)]
        if ahead:
            parts = [jnp.zeros((PAIR, ahead), F32)] + parts
        wide = jnp.concatenate(parts, axis=1)
        total = wide if total is None else total + wide
    eight = None
    for group in range(PAIR // 8):
        moved = pltpu.roll(total[8 * group : 8 * group + 8, :], PAIR - 8 - 8 * group, 1)
        eight = moved if eight is None else eight + moved
    return sum(pltpu.roll(eight[sub : sub + 1, :], 7 - sub, 1) for sub in range(8))


def attend_kernel(lengths_ref, diagonal_ref, query_ref, key_ref, value_ref, out_ref, log_ref):
    rows = lengths_ref.shape[0]
    seq_len = query_ref.shape[0] // rows
    first = half_lanes(seq_len)
    key_at = lax.broadcasted_iota(jnp.int32, (seq_len, 1), 0)
    results = [[None, None] for _ in range(rows)]
    for head in range(2):
        bias = spread_bias(diagonal_ref[0, head : head + 1, :], seq_len)
        for row in range(rows):
            span = pl.ds(row * seq_len, seq_len)
            queries = query_ref[span, :]
            queries = jnp.where(first if head == 0 else ~first, queries, jnp.zeros_like(queries))
            scores = dot_nt(key_ref[span, :], queries) + bias
            scores = jnp.where(key_at < lengths_ref[row], scores, NEG)
            largest = jnp.max(scores, axis=0, keepdims=True)
            raised = jnp.exp(scores - largest)
            totals = jnp.sum(raised, axis=0, keepdims=True)
            probs = (raised * (1.0 / totals)).astype(LOW)
            results[row][head] = dot_tn(probs, value_ref[span, :])
            log_ref[0, 2 * row + head : 2 * row + head + 1, :] = largest + jnp.log(totals)
    for row in range(rows):
        out_ref[pl.ds(row * seq_len, seq_len), :] = jnp.where(first, *results[row]).astype(LOW)


def attend(lengths, diagonal, joint, heads):
    tokens = joint.shape[0]
    pairs = heads // 2
    rows = lengths.shape[0]
    seq_len = tokens // rows
    return pl.pallas_call(
        attend_kernel,
        grid=(pairs,),
        in_specs=[
            pl.BlockSpec(memory_space=pltpu.SMEM),
            pl.BlockSpec((1, 2, 2 * seq_len), lambda p: (p, 0, 0)),
            pl.BlockSpec((tokens, PAIR), lambda p: (0, p)),
            pl.BlockSpec((tokens, PAIR), lambda p: (0, pairs + p)),
            pl.BlockSpec((tokens, PAIR), lambda p: (0, 2 * pairs + p)),
        ],
        out_specs=[
            pl.BlockSpec((tokens, PAIR), lambda p: (0, p)),
            pl.BlockSpec((1, 2 * rows, seq_len), lambda p: (p, 0, 0)),
        ],
        out_shape=[
            jax.ShapeDtypeStruct((tokens, pairs * PAIR), LOW),
            jax.ShapeDtypeStruct((pairs, 2 * rows, seq_len), F32),
        ],
        compiler_params=params(),
        cost_estimate=cost(16),
        name="attend",
    )(lengths, diagonal.reshape(pairs, 2, 2 * seq_len), joint, joint, joint)


def attend_back_kernel(
    lengths_ref, diagonal_ref, query_ref, key_ref, value_ref, grad_ref, log_ref, *outs
):
    query_out, key_out, value_out, bias_out = outs[-4:]
    rows = lengths_ref.shape[0]
    seq_len = query_ref.shape[0] // rows
    first = half_lanes(seq_len)
    key_at = lax.broadcasted_iota(jnp.int32, (seq_len, 1), 0)
    results = [[None, None] for _ in range(rows)]
    for head in range(2):
        bias = spread_bias(diagonal_ref[0, head : head + 1, :], seq_len)
        keep = first if head == 0 else ~first
        total = None
        for row in range(rows):
            span = pl.ds(row * seq_len, seq_len)
            queries = query_ref[span, :]
            keys = key_ref[span, :]
            values = value_ref[span, :]
            grads = grad_ref[span, :]
            only = jnp.where(keep, queries, jnp.zeros_like(queries))
            scores = dot_nt(keys, only) + bias
            scores = jnp.where(key_at < lengths_ref[row], scores, NEG)
            probs = jnp.exp(scores - log_ref[0, 2 * row + head : 2 * row + head + 1, :])
            grad_values = dot(probs.astype(LOW), grads)
            grad_only = jnp.where(keep, grads, jnp.zeros_like(grads))
            grad_probs = dot_nt(values, grad_only)
            weighted = jnp.sum(probs * grad_probs, axis=0, keepdims=True)
            grad_scores = (probs * (grad_probs - weighted)).astype(LOW)
            grad_keys = dot(grad_scores, queries)
            grad_queries = dot_tn(grad_scores, keys)
            wide = grad_scores.astype(F32)
            total = wide if total is None else total + wide
            results[row][head] = (grad_queries, grad_keys, grad_values)
        bias_out[0, head : head + 1, :] = gather_bias(total)
    for row in range(rows):
        span = pl.ds(row * seq_len, seq_len)
        for out_ref, one, two in zip((query_out, key_out, value_out), *results[row]):
            out_ref[span, :] = jnp.where(first, one, two).astype(LOW)


def attend_back(lengths, diagonal, joint, grad_attended, logs, heads, first, count, before=()):
    tokens = joint.shape[0]
    pairs = heads // 2
    rows = lengths.shape[0]
    seq_len = tokens // rows
    part = pl.BlockSpec((tokens, PAIR), lambda p: (0, first + p))
    whole = jax.ShapeDtypeStruct((tokens, pairs * PAIR), LOW)
    lines = pl.BlockSpec((1, 2, 2 * seq_len), lambda p: (first + p, 0, 0))
    return pl.pallas_call(
        attend_back_kernel,
        grid=(count,),
        in_specs=[
            pl.BlockSpec(memory_space=pltpu.SMEM),
            lines,
            part,
            pl.BlockSpec((tokens, PAIR), lambda p: (0, pairs + first + p)),
            pl.BlockSpec((tokens, PAIR), lambda p: (0, 2 * pairs + first + p)),
            part,
            pl.BlockSpec((1, 2 * rows, seq_len), lambda p: (first + p, 0, 0)),
        ]
        + [pl.BlockSpec(memory_space=pl.ANY)] * len(before),
        out_specs=[part, part, part, lines],
        out_shape=[whole, whole, whole, jax.ShapeDtypeStruct((pairs, 2, 2 * seq_len), F32)],
        input_output_aliases={7 + i: i for i in range(len(before))},
        compiler_params=params(),
        cost_estimate=cost(4.4 * count),
        name="attend_back",
    )(lengths, diagonal.reshape(pairs, 2, 2 * seq_len), joint, joint, joint, grad_attended, logs, *before)


def weight_copy(me, number, load, refs, targets, semaphores):
    source, target, column, relative, shard_rows, first, start, rows = load
    width = refs[source].shape[1]
    place = first if relative is None else pl.multiple_of((me ^ relative) * shard_rows + first, 16)
    return pltpu.make_async_copy(
        refs[source].at[pl.ds(start, rows), :],
        targets[target].at[pl.ds(place, rows), pl.ds(column, width)],
        semaphores.at[number],
    )


def weights_of(me_ref, plans, refs, targets, semaphores):
    def each(act):
        for value, loads in enumerate(plans):

            @pl.when(me_ref[1] == value)
            def _():
                for number, load in enumerate(loads):
                    act(number, load)

    def start():
        each(lambda number, load: weight_copy(me_ref[0], number, load, refs, targets, semaphores).start())

    def wait(target):
        def act(number, load):
            if load[1] == target:
                weight_copy(me_ref[0], number, load, refs, targets, semaphores).wait()

        @pl.when(pl.program_id(0) == 0)
        def _():
            each(act)

    return start, wait


def plan_loads(pieces, sections):
    loads = []
    for source, (relative, first, part) in enumerate(pieces):
        start = 0
        for target, rows, column, shard_rows, offset in sections:
            low = max(start, first)
            high = min(start + rows, first + part.shape[0])
            if low < high:
                loads.append((source, target, column, relative, shard_rows, offset + low - start, low - first, high - low))
            start += rows
    return loads


def front_kernel(loads, count, me_ref, slot_ref, reply_ref, gain_ref, *rest):
    refs, (x_ref, normed_ref, joint_ref), (weight, semaphores) = rest[:count], rest[count : count + 3], rest[count + 3 :]

    start, wait = weights_of(me_ref, loads, refs, [weight], semaphores)
    pl.when(pl.program_id(0) == 0)(start)
    rows = slot_ref.shape[0]
    slots = reply_ref.shape[0]
    hot = slot_ref[...] == lax.broadcasted_iota(jnp.int32, (rows, slots), 1)
    x = dot(hot.astype(F32).astype(LOW), reply_ref[...])
    x_ref[...] = x.astype(LOW)
    scale = lax.rsqrt(jnp.mean(x * x, axis=-1, keepdims=True) + EPS)
    normed = (x * scale * gain_ref[...]).astype(LOW)
    normed_ref[...] = normed
    wait(0)
    joint_ref[...] = dot(normed, weight[...]).astype(LOW)


ANY = pl.BlockSpec(memory_space=pl.ANY)
SMEM = pl.BlockSpec(memory_space=pltpu.SMEM)
BLOCK = 256


def full(shape):
    return pl.BlockSpec(shape, lambda *ids: (0,) * len(shape))


def down(width, rows=BLOCK):
    return pl.BlockSpec((rows, width), lambda i: (i, 0))


def front(me, slot, replies, gain, pieces, loads, width):
    tokens = slot.shape[0]
    model = replies.shape[1]
    return pl.pallas_call(
        functools.partial(front_kernel, loads, len(pieces)),
        grid=(tokens // BLOCK,),
        in_specs=[SMEM, down(1), full(replies.shape), full((1, model))] + [ANY] * len(pieces),
        out_specs=[down(model), down(model), down(width)],
        out_shape=[
            jax.ShapeDtypeStruct((tokens, model), LOW),
            jax.ShapeDtypeStruct((tokens, model), LOW),
            jax.ShapeDtypeStruct((tokens, width), LOW),
        ],
        scratch_shapes=[pltpu.VMEM((model, width), LOW), pltpu.SemaphoreType.DMA((max(len(plan) for plan in loads),))],
        compiler_params=params(),
        cost_estimate=cost(15),
        name="front",
    )(me, slot, replies, gain, *pieces)


def ffn_kernel(loads, count, me_ref, x_ref, attended_ref, d_out_ref, seed_ref, gain_ref, *rest):
    refs = rest[:count]
    (y_ref, act_ref, grad_pre_ref, grad_low_ref, normed_ref, hidden_out, low_out, attended_out, gain_out) = rest[count : count + 9]
    w_out, w_in, w_back, semaphores = rest[count + 9 :]

    start_weights, wait = weights_of(me_ref, loads, refs, [w_out, w_in, w_back], semaphores)

    @pl.when(pl.program_id(0) == 0)
    def _():
        start_weights()
        gain_out[...] = jnp.zeros_like(gain_out)

    wait(0)
    hidden = x_ref[...].astype(F32) + dot(attended_ref[...], w_out[...])
    scale = lax.rsqrt(jnp.mean(hidden * hidden, axis=-1, keepdims=True) + EPS)
    unit = hidden * scale
    gain = gain_ref[...]
    normed = (unit * gain).astype(LOW)
    normed_ref[...] = normed
    grad_out = d_out_ref[...].astype(F32) * seed_ref[...]
    grad_low = grad_out.astype(LOW)
    grad_low_ref[...] = grad_low
    wait(1)
    wait(2)
    result = hidden
    back = jnp.zeros_like(hidden)
    model = hidden.shape[1]
    for start in range(0, w_in.shape[1], model):
        span = pl.ds(start, model)
        pre = dot(normed, w_in[:, span])
        square = pre * pre
        tanh = jnp.tanh(ROOT * (pre + CUBE * square * pre))
        half = 0.5 * (1.0 + tanh)
        act = (pre * half).astype(LOW)
        slope = half + 0.5 * pre * (1.0 - tanh * tanh) * ROOT * (1.0 + 3.0 * CUBE * square)
        act_ref[:, span] = act
        result = result + dot(act, w_back[span, :])
        grad_pre = (dot_nt(grad_low, w_back[span, :]) * slope).astype(LOW)
        grad_pre_ref[:, span] = grad_pre
        back = back + dot_nt(grad_pre, w_in[:, span])
    y_ref[...] = result.astype(LOW)
    gain_out[...] += jnp.sum(back * unit, axis=0, keepdims=True)
    scaled = back * gain
    grad_hidden = grad_out + scale * (scaled - unit * jnp.mean(scaled * unit, axis=-1, keepdims=True))
    hidden_out[...] = grad_hidden
    low = grad_hidden.astype(LOW)
    low_out[...] = low
    attended_out[...] = dot_nt(low, w_out[...]).astype(LOW)


def ffn(me, x, attended, d_out, seed, gain, pieces, loads, inner, ff_width):
    tokens, model = x.shape
    low = jax.ShapeDtypeStruct((tokens, model), LOW)
    wide = jax.ShapeDtypeStruct((tokens, ff_width), LOW)
    return pl.pallas_call(
        functools.partial(ffn_kernel, loads, len(pieces)),
        grid=(tokens // BLOCK,),
        in_specs=[SMEM, down(model), down(inner), down(model), down(1), full((1, model))] + [ANY] * len(pieces),
        out_specs=[
            down(model), down(ff_width), down(ff_width), down(model), down(model), down(model), down(model), down(inner),
            full((1, model)),
        ],
        out_shape=[
            low, wide, wide, low, low, jax.ShapeDtypeStruct((tokens, model), F32), low,
            jax.ShapeDtypeStruct((tokens, inner), LOW), jax.ShapeDtypeStruct((1, model), F32),
        ],
        scratch_shapes=[
            pltpu.VMEM((inner, model), LOW),
            pltpu.VMEM((model, ff_width), LOW),
            pltpu.VMEM((ff_width, model), LOW),
            pltpu.SemaphoreType.DMA((max(len(plan) for plan in loads),)),
        ],
        compiler_params=params(),
        cost_estimate=cost(35),
        name="ffn",
    )(me, x, attended, d_out, seed, gain, *pieces)


def project_back_kernel(loads, count, me_ref, query_ref, key_ref, value_ref, x_ref, hidden_ref, gain_ref, *rest):
    refs, (out_ref, gain_out), (weight, semaphores) = rest[:count], rest[count : count + 2], rest[count + 2 :]

    start_weights, wait = weights_of(me_ref, loads, refs, [weight], semaphores)

    @pl.when(pl.program_id(0) == 0)
    def _():
        start_weights()
        gain_out[...] = jnp.zeros_like(gain_out)

    wait(0)
    inner = query_ref.shape[1]
    back = dot_nt(query_ref[...], weight[:, :inner])
    back = back + dot_nt(key_ref[...], weight[:, inner : 2 * inner])
    back = back + dot_nt(value_ref[...], weight[:, 2 * inner :])
    x = x_ref[...].astype(F32)
    scale = lax.rsqrt(jnp.mean(x * x, axis=-1, keepdims=True) + EPS)
    unit = x * scale
    gain_out[...] += jnp.sum(back * unit, axis=0, keepdims=True)
    scaled = back * gain_ref[...]
    grad = hidden_ref[...] + scale * (scaled - unit * jnp.mean(scaled * unit, axis=-1, keepdims=True))
    out_ref[...] = grad.astype(LOW)


def project_back(me, grads, x, grad_hidden, gain, pieces, loads):
    tokens, model = x.shape
    inner = grads[0].shape[1]
    return pl.pallas_call(
        functools.partial(project_back_kernel, loads, len(pieces)),
        grid=(tokens // BLOCK,),
        in_specs=[SMEM] + [down(inner)] * 3 + [down(model), down(model), full((1, model))] + [ANY] * len(pieces),
        out_specs=[down(model), full((1, model))],
        out_shape=[jax.ShapeDtypeStruct((tokens, model), LOW), jax.ShapeDtypeStruct((1, model), F32)],
        scratch_shapes=[pltpu.VMEM((model, 3 * inner), LOW), pltpu.SemaphoreType.DMA((max(len(plan) for plan in loads),))],
        compiler_params=params(),
        cost_estimate=cost(11),
        name="project_back",
    )(me, *grads, x, grad_hidden, gain, *pieces)


def store_shards(me, value, shards, first, keep_ref, send_ref):
    rows = value.shape[0] // shards
    for shard in range(shards):
        relative = me ^ shard
        part = value[shard * rows : (shard + 1) * rows, :].astype(LOW)

        @pl.when(relative % 2 == 0)
        def _():
            keep_ref[relative // 2, pl.ds(first, rows), :] = part

        @pl.when(relative % 2 == 1)
        def _():
            send_ref[relative // 2, pl.ds(first, rows), :] = part


def blocks_grad_kernel(me_ref, keep_left, send_left, right_ref, keep_ref, send_ref):
    right = right_ref[...]
    keep_ref[0] = dot_tn(keep_left[...], right).astype(LOW)
    send_ref[0] = dot_tn(send_left[...], right).astype(LOW)


def columns_grad_kernel(shards, me_ref, left_ref, right_ref, unused_keep, unused_send, keep_ref, send_ref):
    store_shards(me_ref[0], dot_tn(left_ref[...], right_ref[...]), shards, 0, keep_ref, send_ref)


def add_columns(me, left, right, shards, keep, send, start):
    tokens, model = left.shape
    rows = model // shards
    shape = jax.ShapeDtypeStruct(keep.shape, LOW)
    cuts = right.shape[1] // model
    out = pl.BlockSpec((shards // 2, rows, model), lambda i: (0, start // rows + i, 0))
    return pl.pallas_call(
        functools.partial(columns_grad_kernel, shards),
        grid=(cuts,),
        in_specs=[SMEM, full((tokens, model)), pl.BlockSpec((tokens, model), lambda i: (0, i)), ANY, ANY],
        out_specs=[out, out],
        out_shape=[shape, shape],
        input_output_aliases={3: 0, 4: 1},
        compiler_params=params(),
        cost_estimate=cost(1 + 2.5 * cuts),
        name="columns_grad",
    )(me, left, right, keep, send)


def ffn_grads(me, act, grad_low, normed, grad_pre, attended, hidden_low, shards):
    tokens, model = grad_low.shape
    wide = act.shape[1]
    first = wide // shards
    rows = model // shards
    cuts = wide // model
    shape = jax.ShapeDtypeStruct((shards // 2, first + (cuts + 1) * rows, model), LOW)
    out = pl.BlockSpec((1, first, model), lambda i, me: (i, 0, 0))
    keep, send = pl.pallas_call(
        blocks_grad_kernel,
        grid_spec=pltpu.PrefetchScalarGridSpec(
            num_scalar_prefetch=1,
            grid=(shards // 2,),
            in_specs=[
                pl.BlockSpec((tokens, first), lambda i, me: (0, me[0] ^ (2 * i))),
                pl.BlockSpec((tokens, first), lambda i, me: (0, me[0] ^ (2 * i + 1))),
                pl.BlockSpec((tokens, model), lambda i, me: (0, 0)),
            ],
            out_specs=[out, out],
        ),
        out_shape=[shape, shape],
        compiler_params=params(),
        cost_estimate=cost(9),
        name="back_grad",
    )(me, act, act, grad_low)
    keep, send = add_columns(me, normed, grad_pre, shards, keep, send, first)
    return add_columns(me, attended, hidden_low, shards, keep, send, first + cuts * rows)


SMALL_ROWS = 16


def rest_grads_kernel(shards, me_ref, normed_ref, query_ref, key_ref, value_ref, small_ref, keep_ref, send_ref):
    rows = normed_ref.shape[1] // shards
    me = me_ref[0]
    start = 0
    for right_ref in (query_ref, key_ref, value_ref):
        store_shards(me, dot_tn(normed_ref[...], right_ref[...]), shards, start, keep_ref, send_ref)
        start += rows
    store_shards(me, small_ref[...], shards, start, keep_ref, send_ref)


def rest_grads(me, normed, grads, small, shards):
    tokens, model = normed.shape
    shape = jax.ShapeDtypeStruct((shards // 2, 3 * (model // shards) + SMALL_ROWS, model), LOW)
    return pl.pallas_call(
        functools.partial(rest_grads_kernel, shards),
        in_specs=[SMEM] + [full((tokens, model))] * 4 + [full(small.shape)],
        out_specs=[full(shape.shape)] * 2,
        out_shape=[shape, shape],
        compiler_params=params(),
        cost_estimate=cost(11),
        name="rest_grads",
    )(me, normed, *grads, small)


def place_kernel(count, slot_ref, choice_ref, *rest):
    options, (out_ref, tokens, semaphore) = rest[:count], rest[count:]

    @pl.when(pl.program_id(0) == 0)
    def _():
        for number, option in enumerate(options):

            @pl.when(choice_ref[0] == number)
            def _():
                copy = pltpu.make_async_copy(option, tokens, semaphore)
                copy.start()
                copy.wait()

    rows = out_ref.shape[0]
    at = lax.broadcasted_iota(jnp.int32, (rows, tokens.shape[0]), 0) + pl.program_id(0) * rows
    out_ref[...] = dot((at == slot_ref[...]).astype(F32).astype(LOW), tokens[...]).astype(LOW)


def place(slot, choice, options, slots):
    tokens, model = options[0].shape
    return pl.pallas_call(
        functools.partial(place_kernel, len(options)),
        grid=(slots // 512,),
        in_specs=[full((1, tokens)), SMEM] + [ANY] * len(options),
        out_specs=down(model, 512),
        out_shape=jax.ShapeDtypeStruct((slots, model), LOW),
        scratch_shapes=[pltpu.VMEM((tokens, model), LOW), pltpu.SemaphoreType.DMA],
        compiler_params=params(),
        cost_estimate=cost(6),
        name="place",
    )(slot, choice, *options)


TABLE_BLOCK = 512


def table_kernel(ids_ref, rows_ref, *rest):
    out_ref = rest[-1]
    rows = out_ref.shape[0]
    at = lax.broadcasted_iota(jnp.int32, (rows, ids_ref.shape[1]), 0) + pl.program_id(0) * rows
    total = dot((at == ids_ref[...]).astype(F32).astype(LOW), rows_ref[...])
    if len(rest) > 1:
        total = total + rest[0][...]
    out_ref[...] = total


def add_to_table(ids, token_rows, before, vshard):
    model = token_rows.shape[1]
    more = [] if before is None else [before]
    return pl.pallas_call(
        table_kernel,
        grid=(pl.cdiv(vshard, TABLE_BLOCK),),
        in_specs=[full(ids.shape), full(token_rows.shape)] + [down(model, TABLE_BLOCK)] * len(more),
        out_specs=down(model, TABLE_BLOCK),
        out_shape=jax.ShapeDtypeStruct((vshard, model), F32),
        input_output_aliases={2: 0} if more else {},
        compiler_params=params(),
        cost_estimate=cost(18),
        name="table_rows",
    )(ids, token_rows, *more)


def flip(value, bits):
    shards = lax.axis_size("fsdp")
    return lax.ppermute(value, "fsdp", [(i, i ^ bits) for i in range(shards)])


def flip_line(value, bits):
    groups = lax.axis_size("dp")
    return lax.ppermute(value, "dp", [(i, i ^ bits) for i in range(groups)])


def after(value, *others):
    return lax.optimization_barrier((value,) + others)[0]


def exchange(value):
    return lax.all_to_all(value, "fsdp", split_axis=0, concat_axis=0, tiled=True)


def gather_near(own):
    return own, flip(own, 2), flip(own, 4)


def gather_far(near):
    own, by_x, by_y = near
    half = own.shape[0] // 32 * 16
    pieces = [(0, 0, own), (2, 0, by_x), (4, 0, by_y)]
    return pieces + [(6, 0, flip(by_y[:half], 2)), (6, half, flip(by_x[half:], 4))]


def gather_core(pieces):
    return pieces + [(bits ^ 1, first, flip(part, 1)) for bits, first, part in pieces]


def scatter_first(keep, arrived):
    rows = keep.shape[1]
    half = rows // 32 * 16
    across = (keep[3].astype(F32) + arrived[3].astype(F32)).astype(LOW)
    return flip(across[:half], 2), flip(across[half:], 4)


def scatter_between(keep, arrived, from_x, from_y):
    rows, columns = keep.shape[1:]
    half = from_x.shape[0]
    pad_x = jnp.concatenate([from_x, jnp.zeros((rows - half, columns), LOW)])
    pad_y = jnp.concatenate([jnp.zeros((half, columns), LOW), from_y])
    to_y = (keep[2].astype(F32) + arrived[2].astype(F32) + pad_x.astype(F32)).astype(LOW)
    to_x = (keep[1].astype(F32) + arrived[1].astype(F32) + pad_y.astype(F32)).astype(LOW)
    return to_x, to_y


def scatter_second(to_x, to_y):
    return flip(to_x, 2), flip(to_y, 4)


def scatter_last(keep, arrived, by_x, by_y):
    return (keep[0].astype(F32) + arrived[0].astype(F32) + by_x.astype(F32) + by_y.astype(F32)).astype(LOW)


def bucket_of(offset):
    distance = jnp.abs(offset)
    far_bucket = 8 + sum(((distance >= limit).astype(jnp.int32) for limit in LIMITS))
    upper = jnp.where(offset > 0, 16, 0).astype(jnp.int32)
    return upper + jnp.where(distance < 8, distance, far_bucket)


def per_device(
    token_ids,
    task_ids,
    lengths,
    instruction,
    table,
    attn_gain,
    w_query,
    w_key,
    w_value,
    w_out,
    ffn_gain,
    w_in,
    w_back,
    rel_bias,
    d_out,
):
    rows_dev, seq_len = token_ids.shape
    vshard, model = table.shape
    inner = w_query.shape[1]
    ff_width = w_in.shape[1]
    heads = rel_bias.shape[1]
    shards = lax.axis_size("fsdp")
    groups = lax.axis_size("dp")
    me = lax.axis_index("fsdp")
    at = lax.axis_index("dp")
    odd = at % 2
    me_ref = jnp.stack([me, odd]).astype(jnp.int32)
    tokens = rows_dev * seq_len
    capacity = 2 * tokens // shards
    task_count = rows_dev * groups * shards // 4
    own_gain = attn_gain.shape[0]
    buckets = rel_bias.shape[0] * shards

    flat_ids = token_ids.reshape(tokens)
    owner = flat_ids // vshard
    local_row = flat_ids - owner * vshard
    owner_hot = (owner[:, None] == jnp.arange(shards, dtype=jnp.int32)[None, :]).astype(LOW)
    token_at = jnp.arange(tokens, dtype=jnp.int32)
    before = (token_at[:, None] > token_at[None, :]).astype(LOW)
    ranks = jnp.dot(before, owner_hot, preferred_element_type=F32)
    rank_within = jnp.sum(ranks * owner_hot.astype(F32), axis=1).astype(jnp.int32)
    slot = owner * capacity + rank_within
    slots = jnp.arange(shards * capacity, dtype=jnp.int32)
    slot_hot = slots[:, None] == slot[None, :]
    requests = (jnp.sum(jnp.where(slot_hot, local_row[None, :] + 1, 0), axis=1) - 1).reshape(shards, capacity)
    small = jnp.concatenate([attn_gain, ffn_gain, rel_bias.reshape(-1)])
    small_size = small.shape[0]
    joint_own = jnp.concatenate([w_query, w_key, w_value], axis=1)
    own_rows = w_query.shape[0]
    cuts = ff_width // model
    split = shards == 8 and groups == 4
    if split:
        extra = jnp.pad(small, (0, 16 * 3 * inner - small_size)).reshape(16, 3 * inner)
        joint_near = gather_near(jnp.concatenate([joint_own, extra]))
        slab = jnp.concatenate([w_out] + [w_in[:, i * model : (i + 1) * model] for i in range(cuts)] + [w_back])
        half_rows = slab.shape[0] // 2
        ffn_near = gather_near(lax.dynamic_slice_in_dim(slab, odd * half_rows, half_rows))
    task_rows = jnp.broadcast_to(task_ids[None, :], (shards, rows_dev))
    told = exchange(jnp.concatenate([requests, task_rows], axis=1))
    if split:
        told = after(told, *joint_near)
        joint_pieces = gather_far(joint_near)
    asked = told[:, :capacity]
    task_hot = (told[:, capacity:].reshape(-1, 1) == jnp.arange(task_count, dtype=jnp.int32)[None, :]).astype(jnp.int32)
    plane_counts = jnp.sum(task_hot, axis=0)
    looked = jnp.take(table, jnp.maximum(asked, 0).reshape(-1), axis=0)
    if split:
        looked = after(looked, *ffn_near, *(part for unused_bits, unused_first, part in joint_pieces))
        joint_pieces = gather_core(joint_pieces)
        joint_loads = [plan_loads(joint_pieces, [(0, own_rows, 0, own_rows, 0)])] * 2
        lines = {
            bits: part[own_rows - first, :small_size]
            for bits, first, part in joint_pieces
            if first <= own_rows < first + part.shape[0]
        }
        small_all = jnp.stack([lines[bits] for bits in range(shards)])[jnp.arange(shards) ^ me]
        joint_pieces = [part for unused_bits, unused_first, part in joint_pieces]
    replies = exchange(looked.reshape(shards, capacity, model)).reshape(shards * capacity, model)
    if split:
        halves = gather_far(tuple(after(part, looked) for part in ffn_near))[1:]
        others = [(bits, first, flip_line(part, 1)) for bits, first, part in halves]
        replies = after(replies, *(part for unused_bits, unused_first, part in halves + others[:2]))
    if not split:
        joint_pieces, small_all, *ffn_pieces = (
            lax.all_gather(part, "fsdp", axis=0, tiled=True) for part in (joint_own, small[None], w_out, w_in, w_back)
        )
        joint_pieces = [joint_pieces]
        joint_loads = [[(0, 0, 0, None, 0, 0, 0, model)]] * 2
        ffn_loads = [[(i, i, 0, None, 0, 0, 0, part.shape[0]) for i, part in enumerate(ffn_pieces)]] * 2
    first_gain = small_all[:, :own_gain].reshape(1, model).astype(F32)
    second_gain = small_all[:, own_gain : 2 * own_gain].reshape(1, model).astype(F32)
    rel_all = small_all[:, 2 * own_gain :].reshape(buckets, heads).astype(F32)

    message = jnp.concatenate([slot, requests.reshape(-1), plane_counts])
    message = after(message, replies)
    slot_of = [slot]
    away = []
    counts = plane_counts
    for bits in range(1, groups):
        theirs = flip_line(message, bits)
        slot_of.append(theirs[:tokens])
        away.append(theirs[tokens : tokens + shards * capacity].reshape(shards, capacity))
        counts = counts + theirs[tokens + shards * capacity :]
    away = jnp.stack(away, axis=1)
    own_hot = (task_ids[:, None] == jnp.arange(task_count, dtype=jnp.int32)[None, :]).astype(F32)
    row_weight = 1.0 / jnp.sum(own_hot * counts.astype(F32)[None, :], axis=1)
    positions = jnp.arange(seq_len, dtype=jnp.int32)
    pool_mask = ((positions[None, :] < lengths[:, None]) & (instruction == 0)).astype(F32)
    seed = (pool_mask * row_weight[:, None]).reshape(tokens, 1)

    offsets = (seq_len - 1) - jnp.arange(2 * seq_len, dtype=jnp.int32)
    bucket_hot = (jnp.arange(buckets, dtype=jnp.int32)[:, None] == bucket_of(offsets)[None, :]).astype(F32)
    diagonal = lax.dot_general(rel_all, bucket_hot, (((0,), (0,)), ((), ())), precision=HIGH)

    x, normed_one, joint = front(me_ref, slot[:, None], replies, first_gain, joint_pieces, joint_loads, 3 * inner)
    away = exchange(after(away, joint))
    asked_of = [asked] + [away[:, i] for i in range(groups - 1)]
    joint = after(joint, counts)
    if split:
        joint = after(joint, *(part for unused_bits, unused_first, part in others))
        owns = gather_core([(0, 0, after(slab, replies))])
        halves = gather_core([(bits, first, after(part, replies)) for bits, first, part in halves])
        others = gather_core([(bits, first, after(part, joint)) for bits, first, part in others])
        sections = [(0, own_rows, 0, own_rows, 0)]
        sections += [(1, own_rows, i * model, own_rows, 0) for i in range(cuts)]
        sections += [(2, w_back.shape[0], 0, w_back.shape[0], 0)]
        ffn_loads = []
        for at_half in (0, half_rows):
            near = [(bits, first + at_half, part) for bits, first, part in halves]
            away_half = [(bits, first + half_rows - at_half, part) for bits, first, part in others]
            ffn_loads.append(plan_loads(owns + near + away_half, sections))
        ffn_pieces = [part for unused_bits, unused_first, part in owns + halves + others]
    attended, logs = attend(lengths, diagonal, joint, heads)
    result, act, grad_pre, grad_low, normed_two, grad_hidden, hidden_low, grad_attended, grad_second = ffn(
        me_ref, x, after(attended, away), d_out.reshape(tokens, model), seed, second_gain, ffn_pieces, ffn_loads, inner, ff_width
    )
    backward = functools.partial(attend_back, lengths, diagonal, joint)
    if split:
        keep, send = ffn_grads(me_ref, act, grad_low, normed_two, grad_pre, attended, hidden_low, shards)
        arrived = flip(send, 1)
        grads = backward(after(grad_attended, send), logs, heads, 0, 2)
        first_hop = scatter_first(keep, after(arrived, *grads))
        grads = backward(after(grad_attended, arrived, *grads), logs, heads, 2, 3, grads)
        between = scatter_between(keep, arrived, *(after(part, *grads) for part in first_hop))
        second_hop = scatter_second(*between)
        grads = backward(after(grad_attended, *between), logs, heads, 5, 1, grads)
    else:
        grads = backward(grad_attended, logs, heads, 0, heads // 2)
    *grad_joint, bias_sums = grads
    bias_sums = bias_sums.reshape(heads, 2 * seq_len)
    grad_rel = lax.dot_general(bucket_hot, bias_sums, (((1,), (1,)), ((), ())), precision=HIGH)
    token_grads, grad_first = project_back(me_ref, grad_joint, x, grad_hidden, first_gain, joint_pieces, joint_loads)
    small_grad = jnp.concatenate(
        [grad_first.reshape(shards, -1), grad_second.reshape(shards, -1), grad_rel.reshape(shards, -1)], axis=1
    )

    def shift(sent, step, *gates):
        pairs = [(i, i + 1) for i in range(step - 1, groups - 1)]
        back = [(groups - 1 - i, groups - 1 - j) for i, j in pairs]
        to_right, to_left = (after(part, *gates) for part in sent)
        return lax.ppermute(to_right, "dp", pairs), lax.ppermute(to_left, "dp", back)

    def shift(sent, step):
        pairs = [(i, i + 1) for i in range(max(step - 2, 0), groups - 1)]
        back = [(groups - 1 - i, groups - 1 - j) for i, j in pairs]
        to_right, to_left = sent
        if split and step > 1:
            to_right = to_right + jnp.where(at == step - 2, ffn_rows, jnp.zeros((), LOW))
            to_left = to_left + jnp.where(at == groups + 1 - step, ffn_rows, jnp.zeros((), LOW))
        return lax.ppermute(to_right, "dp", pairs), lax.ppermute(to_left, "dp", back)

    def place_from(number, passed, *gates):
        distance = (at ^ number) - at
        steps = sorted({(i ^ number) - i for i in range(groups)})
        options = [passed[abs(step)][step > 0] for step in steps]
        choice = sum((distance == step).astype(jnp.int32) * i for i, step in enumerate(steps))
        return place(after(slot_of[number][None, :], *gates), choice.reshape(1), options, shards * capacity)

    def table_rows(number, incoming, table_grad):
        return add_to_table(asked_of[number].reshape(1, -1), incoming, table_grad, vshard)

    gates = ()
    if split:
        small_rows = jnp.pad(small_grad[:, None], ((0, 0), (0, SMALL_ROWS - 1), (0, model - small_size)))
        small_rows = small_rows.reshape(shards * SMALL_ROWS, model)
        rest_keep, rest_send = rest_grads(me_ref, normed_one, grad_joint, small_rows, shards)
        gates = second_hop + (rest_send,)
    passed = [(token_grads, token_grads)]
    rows = place_from(0, passed, *gates)
    came = table_grad = None
    extras = second_hop if split else ()
    for number in range(groups):
        incoming = exchange(rows.reshape(shards, capacity, model)).reshape(shards * capacity, model)
        if number > 0:
            table_grad = table_rows(number - 1, came, table_grad)
        if split and number == 0:
            ffn_sum = scatter_last(keep, arrived, *extras)
            ffn_rows = jnp.pad(ffn_sum, ((0, tokens - ffn_sum.shape[0]), (0, 0)))
            rest_arrived = flip(rest_send, 1)
            extras = scatter_first(rest_keep, rest_arrived)
        elif split and number == 1:
            extras = (after(part, table_grad) for part in extras)
            extras = scatter_second(*scatter_between(rest_keep, rest_arrived, *extras))
        elif split:
            extras = tuple(after(part, table_grad) for part in extras)
            rest = scatter_last(rest_keep, rest_arrived, *extras) if number == 2 else extras[0] + extras[1]
            extras = (rest, flip_line(rest, number - 1))
        if split or number + 1 < groups:
            passed.append(shift(passed[-1], number + 1))
        if number + 1 < groups:
            rows = place_from(number + 1, passed)
            held = (incoming, rows, *passed[-1], *extras) + (() if table_grad is None else (table_grad,))
            held = lax.optimization_barrier(held)
            came, rows = held[:2]
            passed[-1] = held[2:4]
            extras = held[4 : 4 + len(extras)]
            table_grad = None if table_grad is None else held[-1]
    table_grad = table_rows(groups - 1, incoming, table_grad)

    if split:
        ffn_rows = after(ffn_rows, table_grad).astype(F32)
        extras = tuple(after(part, table_grad) for part in extras)
        for step in range(2, groups + 1):
            ffn_rows = ffn_rows + jnp.where(at == step - 1, passed[step][0], jnp.zeros((), LOW)).astype(F32)
            ffn_rows = ffn_rows + jnp.where(at == groups - step, passed[step][1], jnp.zeros((), LOW)).astype(F32)
        ffn_sum = ffn_rows[: ffn_sum.shape[0]]
        back_rows = w_back.shape[0]
        in_rows = ffn_sum[back_rows : back_rows + cuts * own_rows]
        grad_back = ffn_sum[:back_rows]
        grad_in = jnp.concatenate([in_rows[i * own_rows : (i + 1) * own_rows] for i in range(cuts)], axis=1)
        grad_out = ffn_sum[back_rows + cuts * own_rows :]
        rest = extras[0].astype(F32) + extras[1].astype(F32)
        grad_query, grad_key, grad_value = (rest[i * own_rows : (i + 1) * own_rows] for i in range(3))
        small_grad = rest[3 * own_rows, :small_size]
    else:

        def owned(left, right):
            part = dot_tn(left, right).astype(LOW)
            return lax.psum(lax.psum_scatter(part, "fsdp", scatter_dimension=0, tiled=True), "dp").astype(F32)

        grad_back = owned(act, grad_low)
        grad_in = owned(normed_two, grad_pre)
        grad_query, grad_key, grad_value = (owned(normed_one, grad) for grad in grad_joint)
        grad_out = owned(attended, hidden_low)
        small_grad = lax.psum(small_grad, ("dp", "fsdp"))[me]
    return (
        result.reshape(rows_dev, seq_len, model),
        table_grad,
        small_grad[:own_gain],
        grad_query,
        grad_key,
        grad_value,
        grad_out,
        small_grad[own_gain : 2 * own_gain],
        grad_in,
        grad_back,
        small_grad[2 * own_gain :].reshape(rel_bias.shape),
    )


def solution(mesh):
    both = ("dp", "fsdp")
    in_specs = (
        P(both, None),
        P(both),
        P(both),
        P(both, None),
        P("fsdp", None),
        P("fsdp"),
        P("fsdp", None),
        P("fsdp", None),
        P("fsdp", None),
        P("fsdp", None),
        P("fsdp"),
        P("fsdp", None),
        P("fsdp", None),
        P("fsdp", None),
        P(both, None, None),
    )
    out_specs = (
        P(both, None, None),
        P("fsdp", None),
        P("fsdp"),
        P("fsdp", None),
        P("fsdp", None),
        P("fsdp", None),
        P("fsdp", None),
        P("fsdp"),
        P("fsdp", None),
        P("fsdp", None),
        P("fsdp", None),
    )
    return jax.shard_map(per_device, mesh=mesh, in_specs=in_specs, out_specs=out_specs, check_vma=False)
```

```python
import functools
import jax
import jax.numpy as jnp
from jax import lax
from jax.experimental import pallas as pl
from jax.experimental.pallas import tpu as pltpu
from jax.sharding import PartitionSpec as P

EPS = 1e-06
NEG = -1000000000.0
LIMITS = (12, 16, 23, 32, 46, 64, 91)
HIGH = lax.Precision.HIGHEST
LOW = jnp.bfloat16
F32 = jnp.float32
VMEM_LIMIT = 56 * 1024 * 1024
PAIR = 128
ROOT = (2.0 / 3.141592653589793) ** 0.5
CUBE = 0.044715


def dot(left, right):
    return jnp.dot(left, right, preferred_element_type=F32)


def dot_nt(left, right):
    return lax.dot_general(left, right, (((1,), (1,)), ((), ())), preferred_element_type=F32)


def dot_tn(left, right):
    return lax.dot_general(left, right, (((0,), (0,)), ((), ())), preferred_element_type=F32)


def params():
    return pltpu.CompilerParams(vmem_limit_bytes=VMEM_LIMIT)


def cost(micros):
    return pl.CostEstimate(flops=int(micros * 1.15e9), bytes_accessed=int(micros * 3.6e6), transcendentals=0)


def half_lanes(size):
    return lax.broadcasted_iota(jnp.int32, (size, PAIR), 1) < PAIR // 2


def spread_bias(diagonal, seq_len):
    wide = jnp.broadcast_to(diagonal, (seq_len, 2 * seq_len))
    wide = pltpu.roll(wide, seq_len + 1, 1, stride=1, stride_axis=0)
    return wide[:, :seq_len]


def gather_bias(grad):
    seq_len = grad.shape[0]
    blocks = seq_len // PAIR
    total = None
    for block in range(blocks):
        ahead = PAIR * (blocks - 1 - block)
        parts = [grad[block * PAIR : (block + 1) * PAIR, :], jnp.zeros((PAIR, seq_len - ahead), F32)]
        if ahead:
            parts = [jnp.zeros((PAIR, ahead), F32)] + parts
        wide = jnp.concatenate(parts, axis=1)
        total = wide if total is None else total + wide
    eight = None
    for group in range(PAIR // 8):
        moved = pltpu.roll(total[8 * group : 8 * group + 8, :], PAIR - 8 - 8 * group, 1)
        eight = moved if eight is None else eight + moved
    return sum(pltpu.roll(eight[sub : sub + 1, :], 7 - sub, 1) for sub in range(8))


def attend_kernel(lengths_ref, diagonal_ref, query_ref, key_ref, value_ref, out_ref, log_ref):
    rows = lengths_ref.shape[0]
    seq_len = query_ref.shape[0] // rows
    first = half_lanes(seq_len)
    key_at = lax.broadcasted_iota(jnp.int32, (seq_len, 1), 0)
    results = [[None, None] for _ in range(rows)]
    for head in range(2):
        bias = spread_bias(diagonal_ref[0, head : head + 1, :], seq_len)
        for row in range(rows):
            span = pl.ds(row * seq_len, seq_len)
            queries = query_ref[span, :]
            queries = jnp.where(first if head == 0 else ~first, queries, jnp.zeros_like(queries))
            scores = dot_nt(key_ref[span, :], queries) + bias
            scores = jnp.where(key_at < lengths_ref[row], scores, NEG)
            largest = jnp.max(scores, axis=0, keepdims=True)
            raised = jnp.exp(scores - largest)
            totals = jnp.sum(raised, axis=0, keepdims=True)
            probs = (raised * (1.0 / totals)).astype(LOW)
            results[row][head] = dot_tn(probs, value_ref[span, :])
            log_ref[0, 2 * row + head : 2 * row + head + 1, :] = largest + jnp.log(totals)
    for row in range(rows):
        out_ref[pl.ds(row * seq_len, seq_len), :] = jnp.where(first, *results[row]).astype(LOW)


def attend(lengths, diagonal, joint, heads):
    tokens = joint.shape[0]
    pairs = heads // 2
    rows = lengths.shape[0]
    seq_len = tokens // rows
    return pl.pallas_call(
        attend_kernel,
        grid=(pairs,),
        in_specs=[
            pl.BlockSpec(memory_space=pltpu.SMEM),
            pl.BlockSpec((1, 2, 2 * seq_len), lambda p: (p, 0, 0)),
            pl.BlockSpec((tokens, PAIR), lambda p: (0, p)),
            pl.BlockSpec((tokens, PAIR), lambda p: (0, pairs + p)),
            pl.BlockSpec((tokens, PAIR), lambda p: (0, 2 * pairs + p)),
        ],
        out_specs=[
            pl.BlockSpec((tokens, PAIR), lambda p: (0, p)),
            pl.BlockSpec((1, 2 * rows, seq_len), lambda p: (p, 0, 0)),
        ],
        out_shape=[
            jax.ShapeDtypeStruct((tokens, pairs * PAIR), LOW),
            jax.ShapeDtypeStruct((pairs, 2 * rows, seq_len), F32),
        ],
        compiler_params=params(),
        cost_estimate=cost(16),
        name="attend",
    )(lengths, diagonal.reshape(pairs, 2, 2 * seq_len), joint, joint, joint)


def attend_back_kernel(
    lengths_ref, diagonal_ref, query_ref, key_ref, value_ref, grad_ref, log_ref, *outs
):
    query_out, key_out, value_out, bias_out = outs[-4:]
    rows = lengths_ref.shape[0]
    seq_len = query_ref.shape[0] // rows
    first = half_lanes(seq_len)
    key_at = lax.broadcasted_iota(jnp.int32, (seq_len, 1), 0)
    results = [[None, None] for _ in range(rows)]
    for head in range(2):
        bias = spread_bias(diagonal_ref[0, head : head + 1, :], seq_len)
        keep = first if head == 0 else ~first
        total = None
        for row in range(rows):
            span = pl.ds(row * seq_len, seq_len)
            queries = query_ref[span, :]
            keys = key_ref[span, :]
            values = value_ref[span, :]
            grads = grad_ref[span, :]
            only = jnp.where(keep, queries, jnp.zeros_like(queries))
            scores = dot_nt(keys, only) + bias
            scores = jnp.where(key_at < lengths_ref[row], scores, NEG)
            probs = jnp.exp(scores - log_ref[0, 2 * row + head : 2 * row + head + 1, :])
            grad_values = dot(probs.astype(LOW), grads)
            grad_only = jnp.where(keep, grads, jnp.zeros_like(grads))
            grad_probs = dot_nt(values, grad_only)
            weighted = jnp.sum(probs * grad_probs, axis=0, keepdims=True)
            grad_scores = (probs * (grad_probs - weighted)).astype(LOW)
            grad_keys = dot(grad_scores, queries)
            grad_queries = dot_tn(grad_scores, keys)
            wide = grad_scores.astype(F32)
            total = wide if total is None else total + wide
            results[row][head] = (grad_queries, grad_keys, grad_values)
        bias_out[0, head : head + 1, :] = gather_bias(total)
    for row in range(rows):
        span = pl.ds(row * seq_len, seq_len)
        for out_ref, one, two in zip((query_out, key_out, value_out), *results[row]):
            out_ref[span, :] = jnp.where(first, one, two).astype(LOW)


def attend_back(lengths, diagonal, joint, grad_attended, logs, heads, first, count, before=()):
    tokens = joint.shape[0]
    pairs = heads // 2
    rows = lengths.shape[0]
    seq_len = tokens // rows
    part = pl.BlockSpec((tokens, PAIR), lambda p: (0, first + p))
    whole = jax.ShapeDtypeStruct((tokens, pairs * PAIR), LOW)
    lines = pl.BlockSpec((1, 2, 2 * seq_len), lambda p: (first + p, 0, 0))
    return pl.pallas_call(
        attend_back_kernel,
        grid=(count,),
        in_specs=[
            pl.BlockSpec(memory_space=pltpu.SMEM),
            lines,
            part,
            pl.BlockSpec((tokens, PAIR), lambda p: (0, pairs + first + p)),
            pl.BlockSpec((tokens, PAIR), lambda p: (0, 2 * pairs + first + p)),
            part,
            pl.BlockSpec((1, 2 * rows, seq_len), lambda p: (first + p, 0, 0)),
        ]
        + [pl.BlockSpec(memory_space=pl.ANY)] * len(before),
        out_specs=[part, part, part, lines],
        out_shape=[whole, whole, whole, jax.ShapeDtypeStruct((pairs, 2, 2 * seq_len), F32)],
        input_output_aliases={7 + i: i for i in range(len(before))},
        compiler_params=params(),
        cost_estimate=cost(4.4 * count),
        name="attend_back",
    )(lengths, diagonal.reshape(pairs, 2, 2 * seq_len), joint, joint, joint, grad_attended, logs, *before)


def weight_copy(me, number, load, refs, targets, semaphores):
    source, target, column, relative, shard_rows, first, start, rows = load
    width = refs[source].shape[1]
    place = first if relative is None else pl.multiple_of((me ^ relative) * shard_rows + first, 16)
    return pltpu.make_async_copy(
        refs[source].at[pl.ds(start, rows), :],
        targets[target].at[pl.ds(place, rows), pl.ds(column, width)],
        semaphores.at[number],
    )


def weights_of(me_ref, plans, refs, targets, semaphores):
    def each(act):
        for value, loads in enumerate(plans):

            @pl.when(me_ref[1] == value)
            def _():
                for number, load in enumerate(loads):
                    act(number, load)

    def start():
        each(lambda number, load: weight_copy(me_ref[0], number, load, refs, targets, semaphores).start())

    def wait(target):
        def act(number, load):
            if load[1] == target:
                weight_copy(me_ref[0], number, load, refs, targets, semaphores).wait()

        @pl.when(pl.program_id(0) == 0)
        def _():
            each(act)

    return start, wait


def plan_loads(parts, sections):
    loads = []
    for source, at, relative, first, count in parts:
        start = 0
        for target, rows, column, shard_rows in sections:
            low = max(start, first)
            high = min(start + rows, first + count)
            if low < high:
                loads.append((source, target, column, relative, shard_rows, low - start, at + low - first, high - low))
            start += rows
    return loads


def front_kernel(loads, count, me_ref, slot_ref, reply_ref, gain_ref, *rest):
    refs, (x_ref, normed_ref, joint_ref), (weight, semaphores) = rest[:count], rest[count : count + 3], rest[count + 3 :]

    start, wait = weights_of(me_ref, loads, refs, [weight], semaphores)
    pl.when(pl.program_id(0) == 0)(start)
    rows = slot_ref.shape[0]
    slots = reply_ref.shape[0]
    hot = slot_ref[...] == lax.broadcasted_iota(jnp.int32, (rows, slots), 1)
    x = dot(hot.astype(F32).astype(LOW), reply_ref[...])
    x_ref[...] = x.astype(LOW)
    scale = lax.rsqrt(jnp.mean(x * x, axis=-1, keepdims=True) + EPS)
    normed = (x * scale * gain_ref[...]).astype(LOW)
    normed_ref[...] = normed
    wait(0)
    joint_ref[...] = dot(normed, weight[...]).astype(LOW)


ANY = pl.BlockSpec(memory_space=pl.ANY)
SMEM = pl.BlockSpec(memory_space=pltpu.SMEM)
BLOCK = 256


def full(shape):
    return pl.BlockSpec(shape, lambda *ids: (0,) * len(shape))


def down(width, rows=BLOCK):
    return pl.BlockSpec((rows, width), lambda i: (i, 0))


def front(me, slot, replies, gain, pieces, loads, width):
    tokens = slot.shape[0]
    model = replies.shape[1]
    return pl.pallas_call(
        functools.partial(front_kernel, loads, len(pieces)),
        grid=(tokens // BLOCK,),
        in_specs=[SMEM, down(1), full(replies.shape), full((1, model))] + [ANY] * len(pieces),
        out_specs=[down(model), down(model), down(width)],
        out_shape=[
            jax.ShapeDtypeStruct((tokens, model), LOW),
            jax.ShapeDtypeStruct((tokens, model), LOW),
            jax.ShapeDtypeStruct((tokens, width), LOW),
        ],
        scratch_shapes=[pltpu.VMEM((model, width), LOW), pltpu.SemaphoreType.DMA((max(len(plan) for plan in loads),))],
        compiler_params=params(),
        cost_estimate=cost(15),
        name="front",
    )(me, slot, replies, gain, *pieces)


def ffn_kernel(loads, count, me_ref, x_ref, attended_ref, d_out_ref, seed_ref, gain_ref, *rest):
    refs = rest[:count]
    (y_ref, act_ref, grad_pre_ref, grad_low_ref, normed_ref, hidden_out, low_out, attended_out, gain_out) = rest[count : count + 9]
    w_out, w_in, w_back, semaphores = rest[count + 9 :]

    start_weights, wait = weights_of(me_ref, loads, refs, [w_out, w_in, w_back], semaphores)

    @pl.when(pl.program_id(0) == 0)
    def _():
        start_weights()
        gain_out[...] = jnp.zeros_like(gain_out)

    wait(0)
    hidden = x_ref[...].astype(F32) + dot(attended_ref[...], w_out[...])
    scale = lax.rsqrt(jnp.mean(hidden * hidden, axis=-1, keepdims=True) + EPS)
    unit = hidden * scale
    gain = gain_ref[...]
    normed = (unit * gain).astype(LOW)
    normed_ref[...] = normed
    grad_out = d_out_ref[...].astype(F32) * seed_ref[...]
    grad_low = grad_out.astype(LOW)
    grad_low_ref[...] = grad_low
    wait(1)
    wait(2)
    result = hidden
    back = jnp.zeros_like(hidden)
    model = hidden.shape[1]
    for start in range(0, w_in.shape[1], model):
        span = pl.ds(start, model)
        pre = dot(normed, w_in[:, span])
        square = pre * pre
        tanh = jnp.tanh(ROOT * (pre + CUBE * square * pre))
        half = 0.5 * (1.0 + tanh)
        act = (pre * half).astype(LOW)
        slope = half + 0.5 * pre * (1.0 - tanh * tanh) * ROOT * (1.0 + 3.0 * CUBE * square)
        act_ref[:, span] = act
        result = result + dot(act, w_back[span, :])
        grad_pre = (dot_nt(grad_low, w_back[span, :]) * slope).astype(LOW)
        grad_pre_ref[:, span] = grad_pre
        back = back + dot_nt(grad_pre, w_in[:, span])
    y_ref[...] = result.astype(LOW)
    gain_out[...] += jnp.sum(back * unit, axis=0, keepdims=True)
    scaled = back * gain
    grad_hidden = grad_out + scale * (scaled - unit * jnp.mean(scaled * unit, axis=-1, keepdims=True))
    hidden_out[...] = grad_hidden
    low = grad_hidden.astype(LOW)
    low_out[...] = low
    attended_out[...] = dot_nt(low, w_out[...]).astype(LOW)


def ffn(me, x, attended, d_out, seed, gain, pieces, loads, inner, ff_width):
    tokens, model = x.shape
    low = jax.ShapeDtypeStruct((tokens, model), LOW)
    wide = jax.ShapeDtypeStruct((tokens, ff_width), LOW)
    return pl.pallas_call(
        functools.partial(ffn_kernel, loads, len(pieces)),
        grid=(tokens // BLOCK,),
        in_specs=[SMEM, down(model), down(inner), down(model), down(1), full((1, model))] + [ANY] * len(pieces),
        out_specs=[
            down(model), down(ff_width), down(ff_width), down(model), down(model), down(model), down(model), down(inner),
            full((1, model)),
        ],
        out_shape=[
            low, wide, wide, low, low, jax.ShapeDtypeStruct((tokens, model), F32), low,
            jax.ShapeDtypeStruct((tokens, inner), LOW), jax.ShapeDtypeStruct((1, model), F32),
        ],
        scratch_shapes=[
            pltpu.VMEM((inner, model), LOW),
            pltpu.VMEM((model, ff_width), LOW),
            pltpu.VMEM((ff_width, model), LOW),
            pltpu.SemaphoreType.DMA((max(len(plan) for plan in loads),)),
        ],
        compiler_params=params(),
        cost_estimate=cost(35),
        name="ffn",
    )(me, x, attended, d_out, seed, gain, *pieces)


def project_back_kernel(loads, count, me_ref, query_ref, key_ref, value_ref, x_ref, hidden_ref, gain_ref, *rest):
    refs, (out_ref, gain_out), (weight, semaphores) = rest[:count], rest[count : count + 2], rest[count + 2 :]

    start_weights, wait = weights_of(me_ref, loads, refs, [weight], semaphores)

    @pl.when(pl.program_id(0) == 0)
    def _():
        start_weights()
        gain_out[...] = jnp.zeros_like(gain_out)

    wait(0)
    inner = query_ref.shape[1]
    back = dot_nt(query_ref[...], weight[:, :inner])
    back = back + dot_nt(key_ref[...], weight[:, inner : 2 * inner])
    back = back + dot_nt(value_ref[...], weight[:, 2 * inner :])
    x = x_ref[...].astype(F32)
    scale = lax.rsqrt(jnp.mean(x * x, axis=-1, keepdims=True) + EPS)
    unit = x * scale
    gain_out[...] += jnp.sum(back * unit, axis=0, keepdims=True)
    scaled = back * gain_ref[...]
    grad = hidden_ref[...] + scale * (scaled - unit * jnp.mean(scaled * unit, axis=-1, keepdims=True))
    out_ref[...] = grad.astype(LOW)


def project_back(me, grads, x, grad_hidden, gain, pieces, loads):
    tokens, model = x.shape
    inner = grads[0].shape[1]
    return pl.pallas_call(
        functools.partial(project_back_kernel, loads, len(pieces)),
        grid=(tokens // BLOCK,),
        in_specs=[SMEM] + [down(inner)] * 3 + [down(model), down(model), full((1, model))] + [ANY] * len(pieces),
        out_specs=[down(model), full((1, model))],
        out_shape=[jax.ShapeDtypeStruct((tokens, model), LOW), jax.ShapeDtypeStruct((1, model), F32)],
        scratch_shapes=[pltpu.VMEM((model, 3 * inner), LOW), pltpu.SemaphoreType.DMA((max(len(plan) for plan in loads),))],
        compiler_params=params(),
        cost_estimate=cost(11),
        name="project_back",
    )(me, *grads, x, grad_hidden, gain, *pieces)


def store_shards(me, value, shards, first, keep_ref, send_ref):
    rows = value.shape[0] // shards
    for shard in range(shards):
        relative = me ^ shard
        part = value[shard * rows : (shard + 1) * rows, :].astype(LOW)

        @pl.when(relative % 2 == 0)
        def _():
            keep_ref[relative // 2, pl.ds(first, rows), :] = part

        @pl.when(relative % 2 == 1)
        def _():
            send_ref[relative // 2, pl.ds(first, rows), :] = part


def blocks_grad_kernel(me_ref, keep_left, send_left, right_ref, keep_ref, send_ref):
    right = right_ref[...]
    keep_ref[0] = dot_tn(keep_left[...], right).astype(LOW)
    send_ref[0] = dot_tn(send_left[...], right).astype(LOW)


def columns_grad_kernel(shards, me_ref, left_ref, right_ref, unused_keep, unused_send, keep_ref, send_ref):
    store_shards(me_ref[0], dot_tn(left_ref[...], right_ref[...]), shards, 0, keep_ref, send_ref)


def add_columns(me, left, right, shards, keep, send, start):
    tokens, model = left.shape
    rows = model // shards
    shape = jax.ShapeDtypeStruct(keep.shape, LOW)
    cuts = right.shape[1] // model
    out = pl.BlockSpec((shards // 2, rows, model), lambda i: (0, start // rows + i, 0))
    return pl.pallas_call(
        functools.partial(columns_grad_kernel, shards),
        grid=(cuts,),
        in_specs=[SMEM, full((tokens, model)), pl.BlockSpec((tokens, model), lambda i: (0, i)), ANY, ANY],
        out_specs=[out, out],
        out_shape=[shape, shape],
        input_output_aliases={3: 0, 4: 1},
        compiler_params=params(),
        cost_estimate=cost(1 + 2.5 * cuts),
        name="columns_grad",
    )(me, left, right, keep, send)


def ffn_grads(me, act, grad_low, normed, grad_pre, attended, hidden_low, shards):
    tokens, model = grad_low.shape
    wide = act.shape[1]
    first = wide // shards
    rows = model // shards
    cuts = wide // model
    shape = jax.ShapeDtypeStruct((shards // 2, first + (cuts + 1) * rows, model), LOW)
    out = pl.BlockSpec((1, first, model), lambda i, me: (i, 0, 0))
    keep, send = pl.pallas_call(
        blocks_grad_kernel,
        grid_spec=pltpu.PrefetchScalarGridSpec(
            num_scalar_prefetch=1,
            grid=(shards // 2,),
            in_specs=[
                pl.BlockSpec((tokens, first), lambda i, me: (0, me[0] ^ (2 * i))),
                pl.BlockSpec((tokens, first), lambda i, me: (0, me[0] ^ (2 * i + 1))),
                pl.BlockSpec((tokens, model), lambda i, me: (0, 0)),
            ],
            out_specs=[out, out],
        ),
        out_shape=[shape, shape],
        compiler_params=params(),
        cost_estimate=cost(9),
        name="back_grad",
    )(me, act, act, grad_low)
    keep, send = add_columns(me, normed, grad_pre, shards, keep, send, first)
    return add_columns(me, attended, hidden_low, shards, keep, send, first + cuts * rows)


SMALL_ROWS = 16


def rest_grads_kernel(shards, me_ref, normed_ref, query_ref, key_ref, value_ref, small_ref, keep_ref, send_ref):
    rows = normed_ref.shape[1] // shards
    me = me_ref[0]
    start = 0
    for right_ref in (query_ref, key_ref, value_ref):
        store_shards(me, dot_tn(normed_ref[...], right_ref[...]), shards, start, keep_ref, send_ref)
        start += rows
    store_shards(me, small_ref[...], shards, start, keep_ref, send_ref)


def rest_grads(me, normed, grads, small, shards):
    tokens, model = normed.shape
    shape = jax.ShapeDtypeStruct((shards // 2, 3 * (model // shards) + SMALL_ROWS, model), LOW)
    return pl.pallas_call(
        functools.partial(rest_grads_kernel, shards),
        in_specs=[SMEM] + [full((tokens, model))] * 4 + [full(small.shape)],
        out_specs=[full(shape.shape)] * 2,
        out_shape=[shape, shape],
        compiler_params=params(),
        cost_estimate=cost(11),
        name="rest_grads",
    )(me, normed, *grads, small)


def place_kernel(count, slot_ref, choice_ref, *rest):
    options, (out_ref, tokens, semaphore) = rest[:count], rest[count:]

    @pl.when(pl.program_id(0) == 0)
    def _():
        for number, option in enumerate(options):

            @pl.when(choice_ref[0] == number)
            def _():
                copy = pltpu.make_async_copy(option, tokens, semaphore)
                copy.start()
                copy.wait()

    rows = out_ref.shape[0]
    at = lax.broadcasted_iota(jnp.int32, (rows, tokens.shape[0]), 0) + pl.program_id(0) * rows
    out_ref[...] = dot((at == slot_ref[...]).astype(F32).astype(LOW), tokens[...]).astype(LOW)


def place(slot, choice, options, slots):
    tokens, model = options[0].shape
    return pl.pallas_call(
        functools.partial(place_kernel, len(options)),
        grid=(slots // 512,),
        in_specs=[full((1, tokens)), SMEM] + [ANY] * len(options),
        out_specs=down(model, 512),
        out_shape=jax.ShapeDtypeStruct((slots, model), LOW),
        scratch_shapes=[pltpu.VMEM((tokens, model), LOW), pltpu.SemaphoreType.DMA],
        compiler_params=params(),
        cost_estimate=cost(6),
        name="place",
    )(slot, choice, *options)


TABLE_BLOCK = 512


def table_kernel(ids_ref, rows_ref, *rest):
    out_ref = rest[-1]
    rows = out_ref.shape[0]
    at = lax.broadcasted_iota(jnp.int32, (rows, ids_ref.shape[1]), 0) + pl.program_id(0) * rows
    total = dot((at == ids_ref[...]).astype(F32).astype(LOW), rows_ref[...])
    if len(rest) > 1:
        total = total + rest[0][...]
    out_ref[...] = total


def add_to_table(ids, token_rows, before, vshard):
    model = token_rows.shape[1]
    more = [] if before is None else [before]
    return pl.pallas_call(
        table_kernel,
        grid=(pl.cdiv(vshard, TABLE_BLOCK),),
        in_specs=[full(ids.shape), full(token_rows.shape)] + [down(model, TABLE_BLOCK)] * len(more),
        out_specs=down(model, TABLE_BLOCK),
        out_shape=jax.ShapeDtypeStruct((vshard, model), F32),
        input_output_aliases={2: 0} if more else {},
        compiler_params=params(),
        cost_estimate=cost(18),
        name="table_rows",
    )(ids, token_rows, *more)


def flip(value, bits):
    shards = lax.axis_size("fsdp")
    return lax.ppermute(value, "fsdp", [(i, i ^ bits) for i in range(shards)])


def flip_line(value, bits):
    groups = lax.axis_size("dp")
    return lax.ppermute(value, "dp", [(i, i ^ bits) for i in range(groups)])


def after(value, *others):
    return lax.optimization_barrier((value,) + others)[0]


def exchange(value):
    return lax.all_to_all(value, "fsdp", split_axis=0, concat_axis=0, tiled=True)


def gather_near(own):
    return own, flip(own, 2), flip(own, 4)


def gather_far(near, *gates):
    own, by_x, by_y = near
    half = own.shape[0] // 32 * 16
    to_x, to_y = after(by_y[:half], *gates), after(by_x[half:], *gates)
    pieces = [(0, 0, own), (2, 0, by_x), (4, 0, by_y)]
    return pieces + [(6, 0, flip(to_x, 2)), (6, half, flip(to_y, 4))]


def gather_core(pieces):
    return pieces + [(bits ^ 1, first, flip(part, 1)) for bits, first, part in pieces]


def scatter_first(keep, arrived):
    rows = keep.shape[1]
    half = rows // 32 * 16
    across = (keep[3].astype(F32) + arrived[3].astype(F32)).astype(LOW)
    return flip(across[:half], 2), flip(across[half:], 4)


def scatter_between(keep, arrived, from_x, from_y):
    rows, columns = keep.shape[1:]
    half = from_x.shape[0]
    pad_x = jnp.concatenate([from_x, jnp.zeros((rows - half, columns), LOW)])
    pad_y = jnp.concatenate([jnp.zeros((half, columns), LOW), from_y])
    to_y = (keep[2].astype(F32) + arrived[2].astype(F32) + pad_x.astype(F32)).astype(LOW)
    to_x = (keep[1].astype(F32) + arrived[1].astype(F32) + pad_y.astype(F32)).astype(LOW)
    return to_x, to_y


def scatter_second(to_x, to_y):
    return flip(to_x, 2), flip(to_y, 4)


def scatter_last(keep, arrived, by_x, by_y):
    return (keep[0].astype(F32) + arrived[0].astype(F32) + by_x.astype(F32) + by_y.astype(F32)).astype(LOW)


def bucket_of(offset):
    distance = jnp.abs(offset)
    far_bucket = 8 + sum(((distance >= limit).astype(jnp.int32) for limit in LIMITS))
    upper = jnp.where(offset > 0, 16, 0).astype(jnp.int32)
    return upper + jnp.where(distance < 8, distance, far_bucket)


def per_device(
    token_ids,
    task_ids,
    lengths,
    instruction,
    table,
    attn_gain,
    w_query,
    w_key,
    w_value,
    w_out,
    ffn_gain,
    w_in,
    w_back,
    rel_bias,
    d_out,
):
    rows_dev, seq_len = token_ids.shape
    vshard, model = table.shape
    inner = w_query.shape[1]
    ff_width = w_in.shape[1]
    heads = rel_bias.shape[1]
    shards = lax.axis_size("fsdp")
    groups = lax.axis_size("dp")
    me = lax.axis_index("fsdp")
    at = lax.axis_index("dp")
    odd = at % 2
    me_ref = jnp.stack([me, odd]).astype(jnp.int32)
    tokens = rows_dev * seq_len
    capacity = 2 * tokens // shards
    task_count = rows_dev * groups * shards // 4
    own_gain = attn_gain.shape[0]
    buckets = rel_bias.shape[0] * shards

    flat_ids = token_ids.reshape(tokens)
    owner = flat_ids // vshard
    local_row = flat_ids - owner * vshard
    owner_hot = (owner[:, None] == jnp.arange(shards, dtype=jnp.int32)[None, :]).astype(LOW)
    token_at = jnp.arange(tokens, dtype=jnp.int32)
    before = (token_at[:, None] > token_at[None, :]).astype(LOW)
    ranks = jnp.dot(before, owner_hot, preferred_element_type=F32)
    rank_within = jnp.sum(ranks * owner_hot.astype(F32), axis=1).astype(jnp.int32)
    slot = owner * capacity + rank_within
    slots = jnp.arange(shards * capacity, dtype=jnp.int32)
    slot_hot = slots[:, None] == slot[None, :]
    requests = (jnp.sum(jnp.where(slot_hot, local_row[None, :] + 1, 0), axis=1) - 1).reshape(shards, capacity)
    small = jnp.concatenate([attn_gain, ffn_gain, rel_bias.reshape(-1)])
    small_size = small.shape[0]
    joint_own = jnp.concatenate([w_query, w_key, w_value], axis=1)
    own_rows = w_query.shape[0]
    cuts = ff_width // model
    split = shards == 8 and groups == 4
    if split:
        extra = jnp.pad(small, (0, 16 * 3 * inner - small_size)).reshape(16, 3 * inner)
        joint_near = gather_near(jnp.concatenate([joint_own, extra]))
        slab = jnp.concatenate([w_out] + [w_in[:, i * model : (i + 1) * model] for i in range(cuts)] + [w_back])
        half_rows = slab.shape[0] // 2
        half = lax.dynamic_slice_in_dim(slab, odd * half_rows, half_rows)
    task_rows = jnp.broadcast_to(task_ids[None, :], (shards, rows_dev))
    told = exchange(jnp.concatenate([requests, task_rows], axis=1))
    if split:
        told = after(told, *joint_near)
        ffn_near = gather_near(after(half, told))
        joint_pieces = gather_far(joint_near)
    asked = told[:, :capacity]
    task_hot = (told[:, capacity:].reshape(-1, 1) == jnp.arange(task_count, dtype=jnp.int32)[None, :]).astype(jnp.int32)
    plane_counts = jnp.sum(task_hot, axis=0)
    looked = jnp.take(table, jnp.maximum(asked, 0).reshape(-1), axis=0, mode="clip")
    if split:
        looked = after(looked, *ffn_near, *(part for unused_bits, unused_first, part in joint_pieces))
        joint_pieces = gather_core(joint_pieces)
        parts = [(i, 0, bits, first, part.shape[0]) for i, (bits, first, part) in enumerate(joint_pieces)]
        joint_loads = [plan_loads(parts, [(0, own_rows, 0, own_rows)])] * 2
        lines = {
            bits: part[own_rows - first, :small_size]
            for bits, first, part in joint_pieces
            if first <= own_rows < first + part.shape[0]
        }
        small_all = jnp.stack([lines[bits] for bits in range(shards)])[jnp.arange(shards) ^ me]
        joint_pieces = [part for unused_bits, unused_first, part in joint_pieces]
    replies = exchange(looked.reshape(shards, capacity, model)).reshape(shards * capacity, model)
    if split:
        near_rows = jnp.concatenate([after(part, looked) for part in ffn_near[1:]])
        near_others = flip_line(near_rows, 1)
        ffn_far = gather_far(ffn_near, replies)[3:]
    if not split:
        joint_pieces, small_all, *ffn_pieces = (
            lax.all_gather(part, "fsdp", axis=0, tiled=True) for part in (joint_own, small[None], w_out, w_in, w_back)
        )
        joint_pieces = [joint_pieces]
        joint_loads = [[(0, 0, 0, None, 0, 0, 0, model)]] * 2
        ffn_loads = [[(i, i, 0, None, 0, 0, 0, part.shape[0]) for i, part in enumerate(ffn_pieces)]] * 2
    first_gain = small_all[:, :own_gain].reshape(1, model).astype(F32)
    second_gain = small_all[:, own_gain : 2 * own_gain].reshape(1, model).astype(F32)
    rel_all = small_all[:, 2 * own_gain :].reshape(buckets, heads).astype(F32)

    message = jnp.concatenate([slot, asked.reshape(-1), plane_counts])
    message = after(message, *(joint_pieces[5:] if split else [replies]))
    messages = [flip_line(message, bits) for bits in range(1, groups)]
    positions = jnp.arange(seq_len, dtype=jnp.int32)
    pool_mask = ((positions[None, :] < lengths[:, None]) & (instruction == 0)).astype(F32)

    offsets = (seq_len - 1) - jnp.arange(2 * seq_len, dtype=jnp.int32)
    bucket_hot = (jnp.arange(buckets, dtype=jnp.int32)[:, None] == bucket_of(offsets)[None, :]).astype(F32)
    diagonal = lax.dot_general(rel_all, bucket_hot, (((0,), (0,)), ((), ())), precision=HIGH)

    x, normed_one, joint = front(me_ref, slot[:, None], replies, first_gain, joint_pieces, joint_loads, 3 * inner)
    slot_of = [slot]
    asked_of = [asked]
    counts = plane_counts
    for theirs in messages:
        theirs = after(theirs, joint)
        slot_of.append(theirs[:tokens])
        asked_of.append(theirs[tokens : tokens + shards * capacity])
        counts = counts + theirs[tokens + shards * capacity :]
    own_hot = (task_ids[:, None] == jnp.arange(task_count, dtype=jnp.int32)[None, :]).astype(F32)
    row_weight = 1.0 / jnp.sum(own_hot * counts.astype(F32)[None, :], axis=1)
    seed = (pool_mask * row_weight[:, None]).reshape(tokens, 1)
    if split:
        far_rows = jnp.concatenate([after(part, joint) for unused_bits, unused_first, part in ffn_far])
        held = [slab, near_rows, near_others, far_rows, flip_line(far_rows, 1)]
        ffn_pieces = held + [flip(after(part, joint), 1) for part in held[:4]]
        sections = [(0, own_rows, 0, own_rows)]
        sections += [(1, own_rows, i * model, own_rows) for i in range(cuts)]
        sections += [(2, w_back.shape[0], 0, w_back.shape[0])]
        ffn_loads = []
        for own_half in (0, half_rows):
            parts = []
            for core in (0, 1):
                parts.append((5 * core, 0, core, 0, 2 * half_rows))
                for source, half in ((1, own_half), (2, half_rows - own_half)):
                    parts += [(5 * core + source, 0, 2 ^ core, half, half_rows)]
                    parts += [(5 * core + source, half_rows, 4 ^ core, half, half_rows)]
                    parts += [(5 * core + source + 2, 0, 6 ^ core, half, half_rows)]
            ffn_loads.append(plan_loads(parts, sections))
    attended, logs = attend(lengths, diagonal, joint, heads)
    if split:
        ffn_pieces.append(flip(after(held[4], attended), 1))
    result, act, grad_pre, grad_low, normed_two, grad_hidden, hidden_low, grad_attended, grad_second = ffn(
        me_ref, x, attended, d_out.reshape(tokens, model), seed, second_gain, ffn_pieces, ffn_loads, inner, ff_width
    )
    backward = functools.partial(attend_back, lengths, diagonal, joint)
    if split:
        keep, send = ffn_grads(me_ref, act, grad_low, normed_two, grad_pre, attended, hidden_low, shards)
        arrived = flip(send, 1)
        grads = backward(after(grad_attended, send), logs, heads, 0, 2)
        first_hop = scatter_first(keep, after(arrived, *grads))
        grads = backward(after(grad_attended, arrived, *grads), logs, heads, 2, 3, grads)
        between = scatter_between(keep, arrived, *(after(part, *grads) for part in first_hop))
        second_hop = scatter_second(*between)
        grads = backward(after(grad_attended, *between), logs, heads, 5, 1, grads)
    else:
        grads = backward(grad_attended, logs, heads, 0, heads // 2)
    *grad_joint, bias_sums = grads
    bias_sums = bias_sums.reshape(heads, 2 * seq_len)
    grad_rel = lax.dot_general(bucket_hot, bias_sums, (((1,), (1,)), ((), ())), precision=HIGH)
    token_grads, grad_first = project_back(me_ref, grad_joint, x, grad_hidden, first_gain, joint_pieces, joint_loads)
    small_grad = jnp.concatenate(
        [grad_first.reshape(shards, -1), grad_second.reshape(shards, -1), grad_rel.reshape(shards, -1)], axis=1
    )

    def shift(sent, step, *gates):
        pairs = [(i, i + 1) for i in range(step - 1, groups - 1)]
        back = [(groups - 1 - i, groups - 1 - j) for i, j in pairs]
        to_right, to_left = (after(part, *gates) for part in sent)
        return lax.ppermute(to_right, "dp", pairs), lax.ppermute(to_left, "dp", back)

    def shift(sent, step):
        pairs = [(i, i + 1) for i in range(max(step - 2, 0), groups - 1)]
        back = [(groups - 1 - i, groups - 1 - j) for i, j in pairs]
        to_right, to_left = sent
        if split and step > 1:
            to_right = to_right + jnp.where(at == step - 2, ffn_rows, jnp.zeros((), LOW))
            to_left = to_left + jnp.where(at == groups + 1 - step, ffn_rows, jnp.zeros((), LOW))
        to_right, to_left = lax.optimization_barrier((to_right, to_left))
        return (lax.ppermute(to_right, "dp", pairs), lax.ppermute(to_left, "dp", back)), (to_right, to_left)

    def place_from(number, passed, *gates):
        distance = (at ^ number) - at
        steps = sorted({(i ^ number) - i for i in range(groups)})
        options = [passed[abs(step)][step > 0] for step in steps]
        choice = sum((distance == step).astype(jnp.int32) * i for i, step in enumerate(steps))
        return place(after(slot_of[number][None, :], *gates), choice.reshape(1), options, shards * capacity)

    def table_rows(number, incoming, table_grad):
        return add_to_table(asked_of[number].reshape(1, -1), incoming, table_grad, vshard)

    passed = [(token_grads, token_grads)]
    passed.append(shift(passed[0], 1)[0])
    rows = place_from(0, passed)
    if split:
        small_rows = jnp.pad(small_grad[:, None], ((0, 0), (0, SMALL_ROWS - 1), (0, model - small_size)))
        small_rows = after(small_rows.reshape(shards * SMALL_ROWS, model), flip(rows[:16], 1))
        rest_keep, rest_send = rest_grads(me_ref, normed_one, grad_joint, small_rows, shards)
    came = table_grad = None
    extras = second_hop if split else ()
    for number in range(groups):
        incoming = exchange(rows.reshape(shards, capacity, model)).reshape(shards * capacity, model)
        if number > 0:
            table_grad = table_rows(number - 1, came, table_grad)
        if split and number == 0:
            extras = tuple(after(part, *passed[1]) for part in extras)
            ffn_sum = scatter_last(keep, arrived, *extras)
            ffn_rows = jnp.pad(ffn_sum, ((0, tokens - ffn_sum.shape[0]), (0, 0)))
            rest_arrived = flip(rest_send, 1)
            extras = scatter_first(rest_keep, after(rest_arrived, *passed[1]))
        elif split and number == 1:
            extras = (after(part, table_grad) for part in extras)
            extras = scatter_second(*scatter_between(rest_keep, rest_arrived, *extras))
        elif split:
            extras = tuple(after(part, table_grad) for part in extras)
            rest = scatter_last(rest_keep, rest_arrived, *extras) if number == 2 else extras[0] + extras[1]
            extras = (rest, flip_line(rest, number - 1))
        if number + 1 < groups:
            sent = ()
            if split or number + 2 < groups:
                next_passed, sent = shift(tuple(after(part, rows) for part in passed[-1]), number + 2)
            rows = place_from(number + 1, passed, *sent)
            passed += [next_passed] if sent else []
            held = (incoming, rows) + (() if table_grad is None else (table_grad,))
            came, rows, *tables = lax.optimization_barrier(held)
            table_grad = tables[0] if tables else None
    if split:
        ffn_rows = after(ffn_rows, table_grad)
    table_grad = table_rows(groups - 1, incoming, table_grad)

    if split:
        ffn_rows = ffn_rows.astype(F32)
        extras = tuple(after(part, table_grad) for part in extras)
        for step in range(2, groups + 1):
            ffn_rows = ffn_rows + jnp.where(at == step - 1, passed[step][0], jnp.zeros((), LOW)).astype(F32)
            ffn_rows = ffn_rows + jnp.where(at == groups - step, passed[step][1], jnp.zeros((), LOW)).astype(F32)
        ffn_sum = ffn_rows[: ffn_sum.shape[0]]
        back_rows = w_back.shape[0]
        in_rows = ffn_sum[back_rows : back_rows + cuts * own_rows]
        grad_back = ffn_sum[:back_rows]
        grad_in = jnp.concatenate([in_rows[i * own_rows : (i + 1) * own_rows] for i in range(cuts)], axis=1)
        grad_out = ffn_sum[back_rows + cuts * own_rows :]
        rest = extras[0].astype(F32) + extras[1].astype(F32)
        grad_query, grad_key, grad_value = (rest[i * own_rows : (i + 1) * own_rows] for i in range(3))
        small_grad = rest[3 * own_rows, :small_size]
    else:

        def owned(left, right):
            part = dot_tn(left, right).astype(LOW)
            return lax.psum(lax.psum_scatter(part, "fsdp", scatter_dimension=0, tiled=True), "dp").astype(F32)

        grad_back = owned(act, grad_low)
        grad_in = owned(normed_two, grad_pre)
        grad_query, grad_key, grad_value = (owned(normed_one, grad) for grad in grad_joint)
        grad_out = owned(attended, hidden_low)
        small_grad = lax.psum(small_grad, ("dp", "fsdp"))[me]
    return (
        result.reshape(rows_dev, seq_len, model),
        table_grad,
        small_grad[:own_gain],
        grad_query,
        grad_key,
        grad_value,
        grad_out,
        small_grad[own_gain : 2 * own_gain],
        grad_in,
        grad_back,
        small_grad[2 * own_gain :].reshape(rel_bias.shape),
    )


def solution(mesh):
    both = ("dp", "fsdp")
    in_specs = (
        P(both, None),
        P(both),
        P(both),
        P(both, None),
        P("fsdp", None),
        P("fsdp"),
        P("fsdp", None),
        P("fsdp", None),
        P("fsdp", None),
        P("fsdp", None),
        P("fsdp"),
        P("fsdp", None),
        P("fsdp", None),
        P("fsdp", None),
        P(both, None, None),
    )
    out_specs = (
        P(both, None, None),
        P("fsdp", None),
        P("fsdp"),
        P("fsdp", None),
        P("fsdp", None),
        P("fsdp", None),
        P("fsdp", None),
        P("fsdp"),
        P("fsdp", None),
        P("fsdp", None),
        P("fsdp", None),
    )
    return jax.shard_map(per_device, mesh=mesh, in_specs=in_specs, out_specs=out_specs, check_vma=False)
```

```python
import functools
import jax
import jax.numpy as jnp
from jax import lax
from jax.experimental import pallas as pl
from jax.experimental.pallas import tpu as pltpu
from jax.sharding import PartitionSpec as P

EPS = 1e-06
NEG = -1000000000.0
LIMITS = (12, 16, 23, 32, 46, 64, 91)
HIGH = lax.Precision.HIGHEST
LOW = jnp.bfloat16
F32 = jnp.float32
PAIR = 128
ROOT = (2.0 / 3.141592653589793) ** 0.5
CUBE = 0.044715


def dot(left, right):
    return jnp.dot(left, right, preferred_element_type=F32)


def dot_nt(left, right):
    return lax.dot_general(left, right, (((1,), (1,)), ((), ())), preferred_element_type=F32)


def dot_tn(left, right):
    return lax.dot_general(left, right, (((0,), (0,)), ((), ())), preferred_element_type=F32)


def params(mebibytes):
    return pltpu.CompilerParams(vmem_limit_bytes=mebibytes * 1024 * 1024)


def cost(micros):
    return pl.CostEstimate(flops=int(micros * 1.15e9), bytes_accessed=int(micros * 3.6e6), transcendentals=0)


def half_lanes(size):
    return lax.broadcasted_iota(jnp.int32, (size, PAIR), 1) < PAIR // 2


def spread_bias(diagonal, seq_len):
    wide = jnp.broadcast_to(diagonal, (seq_len, 2 * seq_len))
    wide = pltpu.roll(wide, seq_len + 1, 1, stride=1, stride_axis=0)
    return wide[:, :seq_len]


def gather_bias(grad):
    seq_len = grad.shape[0]
    blocks = seq_len // PAIR
    total = None
    for block in range(blocks):
        ahead = PAIR * (blocks - 1 - block)
        parts = [grad[block * PAIR : (block + 1) * PAIR, :], jnp.zeros((PAIR, seq_len - ahead), F32)]
        if ahead:
            parts = [jnp.zeros((PAIR, ahead), F32)] + parts
        wide = jnp.concatenate(parts, axis=1)
        total = wide if total is None else total + wide
    eight = None
    for group in range(PAIR // 8):
        moved = pltpu.roll(total[8 * group : 8 * group + 8, :], PAIR - 8 - 8 * group, 1)
        eight = moved if eight is None else eight + moved
    return sum(pltpu.roll(eight[sub : sub + 1, :], 7 - sub, 1) for sub in range(8))


def attend_kernel(lengths_ref, diagonal_ref, query_ref, key_ref, value_ref, out_ref, log_ref):
    rows = lengths_ref.shape[0]
    seq_len = query_ref.shape[0] // rows
    first = half_lanes(seq_len)
    key_at = lax.broadcasted_iota(jnp.int32, (seq_len, 1), 0)
    results = [[None, None] for _ in range(rows)]
    for head in range(2):
        bias = spread_bias(diagonal_ref[0, head : head + 1, :], seq_len)
        for row in range(rows):
            span = pl.ds(row * seq_len, seq_len)
            queries = query_ref[span, :]
            queries = jnp.where(first if head == 0 else ~first, queries, jnp.zeros_like(queries))
            scores = dot_nt(key_ref[span, :], queries) + bias
            scores = jnp.where(key_at < lengths_ref[row], scores, NEG)
            largest = jnp.max(scores, axis=0, keepdims=True)
            raised = jnp.exp(scores - largest)
            totals = jnp.sum(raised, axis=0, keepdims=True)
            probs = (raised * (1.0 / totals)).astype(LOW)
            results[row][head] = dot_tn(probs, value_ref[span, :])
            log_ref[0, 2 * row + head : 2 * row + head + 1, :] = largest + jnp.log(totals)
    for row in range(rows):
        out_ref[pl.ds(row * seq_len, seq_len), :] = jnp.where(first, *results[row]).astype(LOW)


def attend(lengths, diagonal, joint, heads):
    tokens = joint.shape[0]
    pairs = heads // 2
    rows = lengths.shape[0]
    seq_len = tokens // rows
    return pl.pallas_call(
        attend_kernel,
        grid=(pairs,),
        in_specs=[
            pl.BlockSpec(memory_space=pltpu.SMEM),
            pl.BlockSpec((1, 2, 2 * seq_len), lambda p: (p, 0, 0)),
            pl.BlockSpec((tokens, PAIR), lambda p: (0, p)),
            pl.BlockSpec((tokens, PAIR), lambda p: (0, pairs + p)),
            pl.BlockSpec((tokens, PAIR), lambda p: (0, 2 * pairs + p)),
        ],
        out_specs=[
            pl.BlockSpec((tokens, PAIR), lambda p: (0, p)),
            pl.BlockSpec((1, 2 * rows, seq_len), lambda p: (p, 0, 0)),
        ],
        out_shape=[
            jax.ShapeDtypeStruct((tokens, pairs * PAIR), LOW),
            jax.ShapeDtypeStruct((pairs, 2 * rows, seq_len), F32),
        ],
        compiler_params=params(56),
        cost_estimate=cost(16),
        name="attend",
    )(lengths, diagonal.reshape(pairs, 2, 2 * seq_len), joint, joint, joint)


def attend_back_kernel(
    lengths_ref, diagonal_ref, query_ref, key_ref, value_ref, grad_ref, log_ref, *outs
):
    query_out, key_out, value_out, bias_out = outs[-4:]
    rows = lengths_ref.shape[0]
    seq_len = query_ref.shape[0] // rows
    first = half_lanes(seq_len)
    key_at = lax.broadcasted_iota(jnp.int32, (seq_len, 1), 0)
    results = [[None, None] for _ in range(rows)]
    for head in range(2):
        bias = spread_bias(diagonal_ref[0, head : head + 1, :], seq_len)
        keep = first if head == 0 else ~first
        total = None
        for row in range(rows):
            span = pl.ds(row * seq_len, seq_len)
            queries = query_ref[span, :]
            keys = key_ref[span, :]
            values = value_ref[span, :]
            grads = grad_ref[span, :]
            only = jnp.where(keep, queries, jnp.zeros_like(queries))
            scores = dot_nt(keys, only) + bias
            scores = jnp.where(key_at < lengths_ref[row], scores, NEG)
            probs = jnp.exp(scores - log_ref[0, 2 * row + head : 2 * row + head + 1, :])
            grad_values = dot(probs.astype(LOW), grads)
            grad_only = jnp.where(keep, grads, jnp.zeros_like(grads))
            grad_probs = dot_nt(values, grad_only)
            weighted = jnp.sum(probs * grad_probs, axis=0, keepdims=True)
            grad_scores = (probs * (grad_probs - weighted)).astype(LOW)
            grad_keys = dot(grad_scores, queries)
            grad_queries = dot_tn(keys, grad_scores)
            wide = grad_scores.astype(F32)
            total = wide if total is None else total + wide
            results[row][head] = (grad_queries, grad_keys, grad_values)
        bias_out[0, head : head + 1, :] = gather_bias(total)
    for row in range(rows):
        span = pl.ds(row * seq_len, seq_len)
        one, two = results[row]
        queries = jnp.concatenate([one[0][: PAIR // 2], two[0][PAIR // 2 :]], axis=0)
        query_out[span, :] = queries.astype(LOW).T
        for out_ref, number in ((key_out, 1), (value_out, 2)):
            out_ref[span, :] = jnp.where(first, one[number], two[number]).astype(LOW)


def attend_back(lengths, diagonal, joint, grad_attended, logs, heads, first, count, before=()):
    tokens = joint.shape[0]
    pairs = heads // 2
    rows = lengths.shape[0]
    seq_len = tokens // rows
    part = pl.BlockSpec((tokens, PAIR), lambda p: (0, first + p))
    whole = jax.ShapeDtypeStruct((tokens, pairs * PAIR), LOW)
    lines = pl.BlockSpec((1, 2, 2 * seq_len), lambda p: (first + p, 0, 0))
    return pl.pallas_call(
        attend_back_kernel,
        grid=(count,),
        in_specs=[
            pl.BlockSpec(memory_space=pltpu.SMEM),
            lines,
            part,
            pl.BlockSpec((tokens, PAIR), lambda p: (0, pairs + first + p)),
            pl.BlockSpec((tokens, PAIR), lambda p: (0, 2 * pairs + first + p)),
            part,
            pl.BlockSpec((1, 2 * rows, seq_len), lambda p: (first + p, 0, 0)),
        ]
        + [pl.BlockSpec(memory_space=pl.ANY)] * len(before),
        out_specs=[part, part, part, lines],
        out_shape=[whole, whole, whole, jax.ShapeDtypeStruct((pairs, 2, 2 * seq_len), F32)],
        input_output_aliases={7 + i: i for i in range(len(before))},
        compiler_params=params(56),
        cost_estimate=cost((4.4 * count) * 0.5),
        name="attend_back",
    )(lengths, diagonal.reshape(pairs, 2, 2 * seq_len), joint, joint, joint, grad_attended, logs, *before)


def weight_copy(me, number, load, refs, targets, semaphores):
    source, target, column, relative, shard_rows, first, start, rows = load
    width = refs[source].shape[1]
    place = first if relative is None else pl.multiple_of((me ^ relative) * shard_rows + first, 16)
    return pltpu.make_async_copy(
        refs[source].at[pl.ds(start, rows), :],
        targets[target].at[pl.ds(place, rows), pl.ds(column, width)],
        semaphores.at[number],
    )


def weights_of(me_ref, plans, refs, targets, semaphores):
    def each(act):
        for value, loads in enumerate(plans):

            @pl.when(me_ref[1] == value)
            def _():
                for number, load in enumerate(loads):
                    act(number, load)

    def start():
        each(lambda number, load: weight_copy(me_ref[0], number, load, refs, targets, semaphores).start())

    def wait(target):
        def act(number, load):
            if load[1] == target:
                weight_copy(me_ref[0], number, load, refs, targets, semaphores).wait()

        @pl.when(pl.program_id(0) == 0)
        def _():
            each(act)

    return start, wait


def plan_loads(parts, sections):
    loads = []
    for source, at, relative, first, count in parts:
        start = 0
        for target, rows, column, shard_rows in sections:
            low = max(start, first)
            high = min(start + rows, first + count)
            if low < high:
                loads.append((source, target, column, relative, shard_rows, low - start, at + low - first, high - low))
            start += rows
    return loads


def front_kernel(loads, count, me_ref, slot_ref, reply_ref, gain_ref, *rest):
    refs, (x_ref, normed_ref, joint_ref), (weight, semaphores) = rest[:count], rest[count : count + 3], rest[count + 3 :]

    start, wait = weights_of(me_ref, loads, refs, [weight], semaphores)
    pl.when(pl.program_id(0) == 0)(start)
    rows = slot_ref.shape[0]
    slots = reply_ref.shape[0]
    hot = slot_ref[...] == lax.broadcasted_iota(jnp.int32, (rows, slots), 1)
    x = dot(hot.astype(F32).astype(LOW), reply_ref[...])
    x_ref[...] = x.astype(LOW)
    scale = lax.rsqrt(jnp.mean(x * x, axis=-1, keepdims=True) + EPS)
    normed = (x * scale * gain_ref[...]).astype(LOW)
    normed_ref[...] = normed
    wait(0)
    joint_ref[...] = dot(normed, weight[...]).astype(LOW)


ANY = pl.BlockSpec(memory_space=pl.ANY)
SMEM = pl.BlockSpec(memory_space=pltpu.SMEM)
BLOCK = 256


def full(shape):
    return pl.BlockSpec(shape, lambda *ids: (0,) * len(shape))


def down(width, rows=BLOCK):
    return pl.BlockSpec((rows, width), lambda i: (i, 0))


def front(me, slot, replies, gain, pieces, loads, width):
    tokens = slot.shape[0]
    model = replies.shape[1]
    return pl.pallas_call(
        functools.partial(front_kernel, loads, len(pieces)),
        grid=(tokens // BLOCK,),
        in_specs=[SMEM, down(1), full(replies.shape), full((1, model))] + [ANY] * len(pieces),
        out_specs=[down(model), down(model), down(width)],
        out_shape=[
            jax.ShapeDtypeStruct((tokens, model), LOW),
            jax.ShapeDtypeStruct((tokens, model), LOW),
            jax.ShapeDtypeStruct((tokens, width), LOW),
        ],
        scratch_shapes=[pltpu.VMEM((model, width), LOW), pltpu.SemaphoreType.DMA((max(len(plan) for plan in loads),))],
        compiler_params=params(56),
        cost_estimate=cost((15) * 0.7),
        name="front",
    )(me, slot, replies, gain, *pieces)


def ffn_kernel(loads, count, me_ref, x_ref, attended_ref, d_out_ref, seed_ref, gain_ref, *rest):
    refs = rest[:count]
    (y_ref, act_ref, grad_pre_ref, grad_low_ref, normed_ref, hidden_out, low_out, attended_out, gain_out) = rest[count : count + 9]
    w_out, w_in, w_back, semaphores = rest[count + 9 :]

    start_weights, wait = weights_of(me_ref, loads, refs, [w_out, w_in, w_back], semaphores)

    @pl.when(pl.program_id(0) == 0)
    def _():
        start_weights()
        gain_out[...] = jnp.zeros_like(gain_out)

    wait(0)
    hidden = x_ref[...].astype(F32) + dot(attended_ref[...], w_out[...])
    scale = lax.rsqrt(jnp.mean(hidden * hidden, axis=-1, keepdims=True) + EPS)
    unit = hidden * scale
    gain = gain_ref[...]
    normed = (unit * gain).astype(LOW)
    normed_ref[...] = normed
    grad_out = d_out_ref[...].astype(F32) * seed_ref[...]
    grad_low = grad_out.astype(LOW)
    grad_low_ref[...] = grad_low
    wait(1)
    wait(2)
    result = hidden
    back = jnp.zeros_like(hidden)
    model = hidden.shape[1]
    for start in range(0, w_in.shape[1], model):
        span = pl.ds(start, model)
        pre = dot(normed, w_in[:, span])
        square = pre * pre
        tanh = jnp.tanh(ROOT * (pre + CUBE * square * pre))
        half = 0.5 * (1.0 + tanh)
        act = (pre * half).astype(LOW)
        slope = half + 0.5 * pre * (1.0 - tanh * tanh) * ROOT * (1.0 + 3.0 * CUBE * square)
        act_ref[:, span] = act
        result = result + dot(act, w_back[span, :])
        grad_pre = (dot_nt(grad_low, w_back[span, :]) * slope).astype(LOW)
        grad_pre_ref[:, span] = grad_pre
        back = back + dot_nt(grad_pre, w_in[:, span])
    y_ref[...] = result.astype(LOW)
    gain_out[...] += jnp.sum(back * unit, axis=0, keepdims=True)
    scaled = back * gain
    grad_hidden = grad_out + scale * (scaled - unit * jnp.mean(scaled * unit, axis=-1, keepdims=True))
    hidden_out[...] = grad_hidden
    low = grad_hidden.astype(LOW)
    low_out[...] = low
    attended_out[...] = dot_nt(low, w_out[...]).astype(LOW)


def ffn(me, x, attended, d_out, seed, gain, pieces, loads, inner, ff_width):
    tokens, model = x.shape
    low = jax.ShapeDtypeStruct((tokens, model), LOW)
    wide = jax.ShapeDtypeStruct((tokens, ff_width), LOW)
    return pl.pallas_call(
        functools.partial(ffn_kernel, loads, len(pieces)),
        grid=(tokens // BLOCK,),
        in_specs=[SMEM, down(model), down(inner), down(model), down(1), full((1, model))] + [ANY] * len(pieces),
        out_specs=[
            down(model), down(ff_width), down(ff_width), down(model), down(model), down(model), down(model), down(inner),
            full((1, model)),
        ],
        out_shape=[
            low, wide, wide, low, low, jax.ShapeDtypeStruct((tokens, model), F32), low,
            jax.ShapeDtypeStruct((tokens, inner), LOW), jax.ShapeDtypeStruct((1, model), F32),
        ],
        scratch_shapes=[
            pltpu.VMEM((inner, model), LOW),
            pltpu.VMEM((model, ff_width), LOW),
            pltpu.VMEM((ff_width, model), LOW),
            pltpu.SemaphoreType.DMA((max(len(plan) for plan in loads),)),
        ],
        compiler_params=params(56),
        cost_estimate=cost((35) * 2.0),
        name="ffn",
    )(me, x, attended, d_out, seed, gain, *pieces)


def project_back_kernel(loads, count, me_ref, query_ref, key_ref, value_ref, x_ref, hidden_ref, gain_ref, *rest):
    refs, (out_ref, gain_out), (weight, semaphores) = rest[:count], rest[count : count + 2], rest[count + 2 :]

    start_weights, wait = weights_of(me_ref, loads, refs, [weight], semaphores)

    @pl.when(pl.program_id(0) == 0)
    def _():
        start_weights()
        gain_out[...] = jnp.zeros_like(gain_out)

    wait(0)
    inner = query_ref.shape[1]
    back = dot_nt(query_ref[...], weight[:, :inner])
    back = back + dot_nt(key_ref[...], weight[:, inner : 2 * inner])
    back = back + dot_nt(value_ref[...], weight[:, 2 * inner :])
    x = x_ref[...].astype(F32)
    scale = lax.rsqrt(jnp.mean(x * x, axis=-1, keepdims=True) + EPS)
    unit = x * scale
    gain_out[...] += jnp.sum(back * unit, axis=0, keepdims=True)
    scaled = back * gain_ref[...]
    grad = hidden_ref[...] + scale * (scaled - unit * jnp.mean(scaled * unit, axis=-1, keepdims=True))
    out_ref[...] = grad.astype(LOW)


def project_back(me, grads, x, grad_hidden, gain, pieces, loads):
    tokens, model = x.shape
    inner = grads[0].shape[1]
    return pl.pallas_call(
        functools.partial(project_back_kernel, loads, len(pieces)),
        grid=(tokens // BLOCK,),
        in_specs=[SMEM] + [down(inner)] * 3 + [down(model), down(model), full((1, model))] + [ANY] * len(pieces),
        out_specs=[down(model), full((1, model))],
        out_shape=[jax.ShapeDtypeStruct((tokens, model), LOW), jax.ShapeDtypeStruct((1, model), F32)],
        scratch_shapes=[pltpu.VMEM((model, 3 * inner), LOW), pltpu.SemaphoreType.DMA((max(len(plan) for plan in loads),))],
        compiler_params=params(56),
        cost_estimate=cost(11),
        name="project_back",
    )(me, *grads, x, grad_hidden, gain, *pieces)


def store_shards(me, value, shards, first, keep_ref, send_ref):
    rows = value.shape[0] // shards
    for shard in range(shards):
        relative = me ^ shard
        part = value[shard * rows : (shard + 1) * rows, :].astype(LOW)

        @pl.when(relative % 2 == 0)
        def _():
            keep_ref[relative // 2, pl.ds(first, rows), :] = part

        @pl.when(relative % 2 == 1)
        def _():
            send_ref[relative // 2, pl.ds(first, rows), :] = part


def blocks_grad_kernel(me_ref, keep_left, send_left, right_ref, keep_ref, send_ref):
    both = dot_tn(jnp.concatenate([keep_left[...], send_left[...]], axis=1), right_ref[...]).astype(LOW)
    rows = keep_left.shape[1]
    keep_ref[0] = both[:rows]
    send_ref[0] = both[rows:]


def columns_grad_kernel(shards, me_ref, normed_ref, pre_ref, attended_ref, hidden_ref, unused_keep, unused_send, keep_ref, send_ref):
    last = pl.program_id(0) == pl.num_programs(0) - 1

    @pl.when(jnp.logical_not(last))
    def _():
        store_shards(me_ref[0], dot_tn(normed_ref[...], pre_ref[...]), shards, 0, keep_ref, send_ref)

    @pl.when(last)
    def _():
        store_shards(me_ref[0], dot_tn(attended_ref[...], hidden_ref[...]), shards, 0, keep_ref, send_ref)


def ffn_grads(me, act, grad_low, normed, grad_pre, attended, hidden_low, shards):
    tokens, model = grad_low.shape
    wide = act.shape[1]
    first = wide // shards
    rows = model // shards
    cuts = wide // model
    shape = jax.ShapeDtypeStruct((shards // 2, first + (cuts + 1) * rows, model), LOW)
    out = pl.BlockSpec((1, first, model), lambda i, me: (i, 0, 0))
    keep, send = pl.pallas_call(
        blocks_grad_kernel,
        grid_spec=pltpu.PrefetchScalarGridSpec(
            num_scalar_prefetch=1,
            grid=(shards // 2,),
            in_specs=[
                pl.BlockSpec((tokens, first), lambda i, me: (0, me[0] ^ (2 * i))),
                pl.BlockSpec((tokens, first), lambda i, me: (0, me[0] ^ (2 * i + 1))),
                pl.BlockSpec((tokens, model), lambda i, me: (0, 0)),
            ],
            out_specs=[out, out],
        ),
        out_shape=[shape, shape],
        compiler_params=params(56),
        cost_estimate=cost(9),
        name="back_grad",
    )(me, act, act, grad_low)
    out = pl.BlockSpec((shards // 2, rows, model), lambda i: (0, first // rows + i, 0))
    return pl.pallas_call(
        functools.partial(columns_grad_kernel, shards),
        grid=(cuts + 1,),
        in_specs=[
            SMEM,
            full((tokens, model)),
            pl.BlockSpec((tokens, model), lambda i: (0, jnp.minimum(i, cuts - 1))),
            full((tokens, model)),
            full((tokens, model)),
            ANY,
            ANY,
        ],
        out_specs=[out, out],
        out_shape=[shape, shape],
        input_output_aliases={5: 0, 6: 1},
        compiler_params=params(56),
        cost_estimate=cost(13),
        name="columns_grad",
    )(me, normed, grad_pre, attended, hidden_low, keep, send)


SMALL_ROWS = 16


def rest_grads_kernel(shards, me_ref, normed_ref, query_ref, key_ref, value_ref, small_ref, keep_ref, send_ref):
    rows = normed_ref.shape[1] // shards
    me = me_ref[0]
    start = 0
    for right_ref in (query_ref, key_ref, value_ref):
        store_shards(me, dot_tn(normed_ref[...], right_ref[...]), shards, start, keep_ref, send_ref)
        start += rows
    store_shards(me, small_ref[...], shards, start, keep_ref, send_ref)


def rest_grads(me, normed, grads, small, shards):
    tokens, model = normed.shape
    shape = jax.ShapeDtypeStruct((shards // 2, 3 * (model // shards) + SMALL_ROWS, model), LOW)
    return pl.pallas_call(
        functools.partial(rest_grads_kernel, shards),
        in_specs=[SMEM] + [full((tokens, model))] * 4 + [full(small.shape)],
        out_specs=[full(shape.shape)] * 2,
        out_shape=[shape, shape],
        compiler_params=params(56),
        cost_estimate=cost(11),
        name="rest_grads",
    )(me, normed, *grads, small)


def place_kernel(count, slot_ref, choice_ref, *rest):
    options, (out_ref, tokens, semaphore) = rest[:count], rest[count:]

    @pl.when(pl.program_id(0) == 0)
    def _():
        for number, option in enumerate(options):

            @pl.when(choice_ref[0] == number)
            def _():
                copy = pltpu.make_async_copy(option, tokens, semaphore)
                copy.start()
                copy.wait()

    rows = out_ref.shape[0]
    at = lax.broadcasted_iota(jnp.int32, (rows, tokens.shape[0]), 0) + pl.program_id(0) * rows
    out_ref[...] = dot((at == slot_ref[...]).astype(F32).astype(LOW), tokens[...]).astype(LOW)


def place(slot, choice, options, slots):
    tokens, model = options[0].shape
    return pl.pallas_call(
        functools.partial(place_kernel, len(options)),
        grid=(slots // 1024,),
        in_specs=[full((1, tokens)), SMEM] + [ANY] * len(options),
        out_specs=down(model, 1024),
        out_shape=jax.ShapeDtypeStruct((slots, model), LOW),
        scratch_shapes=[pltpu.VMEM((tokens, model), LOW), pltpu.SemaphoreType.DMA],
        compiler_params=params(56),
        cost_estimate=cost(6),
        name="place",
    )(slot, choice, *options)


TABLE_BLOCK = 512


def table_kernel(ids_ref, rows_ref, *rest):
    out_ref = rest[-1]
    rows = out_ref.shape[0]
    at = lax.broadcasted_iota(jnp.int32, (rows, ids_ref.shape[1]), 0) + pl.program_id(0) * rows
    total = dot((at == ids_ref[...]).astype(F32).astype(LOW), rows_ref[...])
    if len(rest) > 1:
        total = total + rest[0][...]
    out_ref[...] = total


def add_to_table(ids, token_rows, before, vshard):
    model = token_rows.shape[1]
    more = [] if before is None else [before]
    return pl.pallas_call(
        table_kernel,
        grid=(pl.cdiv(vshard, TABLE_BLOCK),),
        in_specs=[full(ids.shape), full(token_rows.shape)] + [down(model, TABLE_BLOCK)] * len(more),
        out_specs=down(model, TABLE_BLOCK),
        out_shape=jax.ShapeDtypeStruct((vshard, model), F32),
        input_output_aliases={2: 0} if more else {},
        compiler_params=params(56),
        cost_estimate=cost(18),
        name="table_rows",
    )(ids, token_rows, *more)


def flip(value, bits):
    shards = lax.axis_size("fsdp")
    return lax.ppermute(value, "fsdp", [(i, i ^ bits) for i in range(shards)])


def flip_line(value, bits):
    groups = lax.axis_size("dp")
    return lax.ppermute(value, "dp", [(i, i ^ bits) for i in range(groups)])


def after(value, *others):
    return lax.optimization_barrier((value,) + others)[0]


def exchange(value):
    return lax.all_to_all(value, "fsdp", split_axis=0, concat_axis=0, tiled=True)


def gather_near(own):
    return own, flip(own, 2), flip(own, 4)


def gather_far(near, *gates):
    own, by_x, by_y = near
    half = own.shape[0] // 32 * 16
    to_x, to_y = after(by_y[:half], *gates), after(by_x[half:], *gates)
    pieces = [(0, 0, own), (2, 0, by_x), (4, 0, by_y)]
    return pieces + [(6, 0, flip(to_x, 2)), (6, half, flip(to_y, 4))]


def gather_core(pieces):
    return pieces + [(bits ^ 1, first, flip(part, 1)) for bits, first, part in pieces]


def scatter_first(keep, arrived):
    rows = keep.shape[1]
    half = rows // 32 * 16
    across = (keep[3].astype(F32) + arrived[3].astype(F32)).astype(LOW)
    return flip(across[:half], 2), flip(across[half:], 4)


def scatter_between(keep, arrived, from_x, from_y):
    rows, columns = keep.shape[1:]
    half = from_x.shape[0]
    pad_x = jnp.concatenate([from_x, jnp.zeros((rows - half, columns), LOW)])
    pad_y = jnp.concatenate([jnp.zeros((half, columns), LOW), from_y])
    to_y = (keep[2].astype(F32) + arrived[2].astype(F32) + pad_x.astype(F32)).astype(LOW)
    to_x = (keep[1].astype(F32) + arrived[1].astype(F32) + pad_y.astype(F32)).astype(LOW)
    return to_x, to_y


def scatter_second(to_x, to_y):
    return flip(to_x, 2), flip(to_y, 4)


def scatter_last(keep, arrived, by_x, by_y):
    return (keep[0].astype(F32) + arrived[0].astype(F32) + by_x.astype(F32) + by_y.astype(F32)).astype(LOW)


def bucket_of(offset):
    distance = jnp.abs(offset)
    far_bucket = 8 + sum(((distance >= limit).astype(jnp.int32) for limit in LIMITS))
    upper = jnp.where(offset > 0, 16, 0).astype(jnp.int32)
    return upper + jnp.where(distance < 8, distance, far_bucket)


def per_device(
    token_ids,
    task_ids,
    lengths,
    instruction,
    table,
    attn_gain,
    w_query,
    w_key,
    w_value,
    w_out,
    ffn_gain,
    w_in,
    w_back,
    rel_bias,
    d_out,
):
    rows_dev, seq_len = token_ids.shape
    vshard, model = table.shape
    inner = w_query.shape[1]
    ff_width = w_in.shape[1]
    heads = rel_bias.shape[1]
    shards = lax.axis_size("fsdp")
    groups = lax.axis_size("dp")
    me = lax.axis_index("fsdp")
    at = lax.axis_index("dp")
    odd = at % 2
    me_ref = jnp.stack([me, odd]).astype(jnp.int32)
    tokens = rows_dev * seq_len
    capacity = 2 * tokens // shards
    task_count = rows_dev * groups * shards // 4
    own_gain = attn_gain.shape[0]
    buckets = rel_bias.shape[0] * shards

    flat_ids = token_ids.reshape(tokens)
    owner = flat_ids // vshard
    local_row = flat_ids - owner * vshard
    owner_hot = (owner[:, None] == jnp.arange(shards, dtype=jnp.int32)[None, :]).astype(LOW)
    token_at = jnp.arange(tokens, dtype=jnp.int32)
    before = (token_at[:, None] > token_at[None, :]).astype(LOW)
    ranks = jnp.dot(before, owner_hot, preferred_element_type=F32)
    rank_within = jnp.sum(ranks * owner_hot.astype(F32), axis=1).astype(jnp.int32)
    slot = owner * capacity + rank_within
    slots = jnp.arange(shards * capacity, dtype=jnp.int32)
    slot_hot = slots[:, None] == slot[None, :]
    requests = (jnp.sum(jnp.where(slot_hot, local_row[None, :] + 1, 0), axis=1) - 1).reshape(shards, capacity)
    small = jnp.concatenate([attn_gain, ffn_gain, rel_bias.reshape(-1)])
    small_size = small.shape[0]
    joint_own = jnp.concatenate([w_query, w_key, w_value], axis=1)
    own_rows = w_query.shape[0]
    cuts = ff_width // model
    split = shards == 8 and groups == 4
    if split:
        extra = jnp.pad(small, (0, 16 * 3 * inner - small_size)).reshape(16, 3 * inner)
        joint_near = gather_near(jnp.concatenate([joint_own, extra]))
        slab = jnp.concatenate([w_out] + [w_in[:, i * model : (i + 1) * model] for i in range(cuts)] + [w_back])
        half_rows = slab.shape[0] // 2
        half = lax.dynamic_slice_in_dim(slab, odd * half_rows, half_rows)
    task_rows = jnp.broadcast_to(task_ids[None, :], (shards, rows_dev))
    told = exchange(jnp.concatenate([requests, task_rows], axis=1))
    if split:
        told = after(told, *joint_near)
        ffn_near = gather_near(after(half, told))
        joint_pieces = gather_far(joint_near)
    asked = told[:, :capacity]
    task_hot = (told[:, capacity:].reshape(-1, 1) == jnp.arange(task_count, dtype=jnp.int32)[None, :]).astype(jnp.int32)
    plane_counts = jnp.sum(task_hot, axis=0)
    looked = jnp.take(table, jnp.maximum(asked, 0).reshape(-1), axis=0, mode="clip")
    if split:
        looked = after(looked, *ffn_near, *(part for unused_bits, unused_first, part in joint_pieces))
        joint_pieces = gather_core(joint_pieces)
        parts = [(i, 0, bits, first, part.shape[0]) for i, (bits, first, part) in enumerate(joint_pieces)]
        joint_loads = [plan_loads(parts, [(0, own_rows, 0, own_rows)])] * 2
        lines = {
            bits: part[own_rows - first, :small_size]
            for bits, first, part in joint_pieces
            if first <= own_rows < first + part.shape[0]
        }
        small_all = jnp.stack([lines[bits] for bits in range(shards)])[jnp.arange(shards) ^ me]
        joint_pieces = [part for unused_bits, unused_first, part in joint_pieces]
    replies = exchange(looked.reshape(shards, capacity, model)).reshape(shards * capacity, model)
    if split:
        near_rows = jnp.concatenate([after(part, looked) for part in ffn_near[1:]])
        near_others = flip_line(near_rows, 1)
        ffn_far = gather_far(ffn_near, replies)[3:]
    if not split:
        joint_pieces, small_all, *ffn_pieces = (
            lax.all_gather(part, "fsdp", axis=0, tiled=True) for part in (joint_own, small[None], w_out, w_in, w_back)
        )
        joint_pieces = [joint_pieces]
        joint_loads = [[(0, 0, 0, None, 0, 0, 0, model)]] * 2
        ffn_loads = [[(i, i, 0, None, 0, 0, 0, part.shape[0]) for i, part in enumerate(ffn_pieces)]] * 2
    first_gain = small_all[:, :own_gain].reshape(1, model).astype(F32)
    second_gain = small_all[:, own_gain : 2 * own_gain].reshape(1, model).astype(F32)
    rel_all = small_all[:, 2 * own_gain :].reshape(buckets, heads).astype(F32)

    message = jnp.concatenate([slot, asked.reshape(-1), plane_counts])
    message = after(message, *(joint_pieces[5:] if split else [replies]))
    messages = [flip_line(message, bits) for bits in range(1, groups)]
    positions = jnp.arange(seq_len, dtype=jnp.int32)
    pool_mask = ((positions[None, :] < lengths[:, None]) & (instruction == 0)).astype(F32)

    offsets = (seq_len - 1) - jnp.arange(2 * seq_len, dtype=jnp.int32)
    bucket_hot = (jnp.arange(buckets, dtype=jnp.int32)[:, None] == bucket_of(offsets)[None, :]).astype(F32)
    diagonal = lax.dot_general(rel_all, bucket_hot, (((0,), (0,)), ((), ())), precision=HIGH)

    x, normed_one, joint = front(me_ref, slot[:, None], replies, first_gain, joint_pieces, joint_loads, 3 * inner)
    slot_of = [slot]
    asked_of = [asked]
    counts = plane_counts
    for theirs in messages:
        theirs = after(theirs, joint)
        slot_of.append(theirs[:tokens])
        asked_of.append(theirs[tokens : tokens + shards * capacity])
        counts = counts + theirs[tokens + shards * capacity :]
    own_hot = (task_ids[:, None] == jnp.arange(task_count, dtype=jnp.int32)[None, :]).astype(F32)
    row_weight = 1.0 / jnp.sum(own_hot * counts.astype(F32)[None, :], axis=1)
    seed = (pool_mask * row_weight[:, None]).reshape(tokens, 1)
    if split:
        far_rows = jnp.concatenate([after(part, joint) for unused_bits, unused_first, part in ffn_far])
        held = [slab, near_rows, near_others, far_rows, flip_line(far_rows, 1)]
        ffn_pieces = held + [flip(after(part, joint), 1) for part in held[:4]]
        sections = [(0, own_rows, 0, own_rows)]
        sections += [(1, own_rows, i * model, own_rows) for i in range(cuts)]
        sections += [(2, w_back.shape[0], 0, w_back.shape[0])]
        ffn_loads = []
        for own_half in (0, half_rows):
            parts = []
            for core in (0, 1):
                parts.append((5 * core, 0, core, 0, 2 * half_rows))
                for source, half in ((1, own_half), (2, half_rows - own_half)):
                    parts += [(5 * core + source, 0, 2 ^ core, half, half_rows)]
                    parts += [(5 * core + source, half_rows, 4 ^ core, half, half_rows)]
                    parts += [(5 * core + source + 2, 0, 6 ^ core, half, half_rows)]
            ffn_loads.append(plan_loads(parts, sections))
    attended, logs = attend(lengths, diagonal, joint, heads)
    if split:
        ffn_pieces.append(flip(after(held[4], attended), 1))
    result, act, grad_pre, grad_low, normed_two, grad_hidden, hidden_low, grad_attended, grad_second = ffn(
        me_ref, x, attended, d_out.reshape(tokens, model), seed, second_gain, ffn_pieces, ffn_loads, inner, ff_width
    )
    backward = functools.partial(attend_back, lengths, diagonal, joint)
    if split:
        keep, send = ffn_grads(me_ref, act, grad_low, normed_two, grad_pre, attended, hidden_low, shards)
        arrived = flip(send, 1)
        grads = backward(after(grad_attended, send), logs, heads, 0, 2)
        first_hop = scatter_first(keep, after(arrived, *grads))
        grads = backward(after(grad_attended, arrived, *grads), logs, heads, 2, 4, grads)
        between = scatter_between(keep, arrived, *(after(part, *grads) for part in first_hop))
        second_hop = scatter_second(*between)
        grads = tuple(after(part, *between) for part in grads)
    else:
        grads = backward(grad_attended, logs, heads, 0, heads // 2)
    *grad_joint, bias_sums = grads
    bias_sums = bias_sums.reshape(heads, 2 * seq_len)
    grad_rel = lax.dot_general(bucket_hot, bias_sums, (((1,), (1,)), ((), ())), precision=HIGH)
    token_grads, grad_first = project_back(me_ref, grad_joint, x, grad_hidden, first_gain, joint_pieces, joint_loads)
    small_grad = jnp.concatenate(
        [grad_first.reshape(shards, -1), grad_second.reshape(shards, -1), grad_rel.reshape(shards, -1)], axis=1
    )

    def shift(sent, step, *gates):
        pairs = [(i, i + 1) for i in range(step - 1, groups - 1)]
        back = [(groups - 1 - i, groups - 1 - j) for i, j in pairs]
        to_right, to_left = (after(part, *gates) for part in sent)
        return lax.ppermute(to_right, "dp", pairs), lax.ppermute(to_left, "dp", back)

    def shift(sent, step):
        pairs = [(i, i + 1) for i in range(max(step - 2, 0), groups - 1)]
        back = [(groups - 1 - i, groups - 1 - j) for i, j in pairs]
        to_right, to_left = sent
        if split and step > 1:
            if step == 2:
                to_right = jnp.where(at == 0, ffn_rows, to_right)
                to_left = jnp.where(at == groups - 1, ffn_rows, to_left)
            else:
                to_right = to_right + jnp.where(at == step - 2, ffn_rows, jnp.zeros((), LOW))
                to_left = to_left + jnp.where(at == groups + 1 - step, ffn_rows, jnp.zeros((), LOW))
        return (lax.ppermute(to_right, "dp", pairs), lax.ppermute(to_left, "dp", back)), (to_right, to_left)

    def place_from(number, passed, *gates):
        distance = (at ^ number) - at
        steps = sorted({(i ^ number) - i for i in range(groups)})
        options = [passed[abs(step)][step > 0] for step in steps]
        choice = sum((distance == step).astype(jnp.int32) * i for i, step in enumerate(steps))
        return place(after(slot_of[number][None, :], *gates), choice.reshape(1), options, shards * capacity)

    def table_rows(number, incoming, table_grad):
        return add_to_table(asked_of[number].reshape(1, -1), incoming, table_grad, vshard)

    passed = [(token_grads, token_grads)]
    passed.append(shift(passed[0], 1)[0])
    rows = place_from(0, passed)
    if split:
        small_rows = jnp.pad(small_grad[:, None], ((0, 0), (0, SMALL_ROWS - 1), (0, model - small_size)))
        small_rows = after(small_rows.reshape(shards * SMALL_ROWS, model), flip(rows[:16], 1))
        rest_keep, rest_send = rest_grads(me_ref, normed_one, grad_joint, small_rows, shards)
    came = table_grad = None
    extras = second_hop if split else ()
    for number in range(groups):
        incoming = exchange(rows.reshape(shards, capacity, model)).reshape(shards * capacity, model)
        if number > 0:
            table_grad = table_rows(number - 1, came, table_grad)
        if split and number == 0:
            ffn_sum = scatter_last(keep, arrived, *extras)
            ffn_rows = jnp.pad(ffn_sum, ((0, tokens - ffn_sum.shape[0]), (0, 0)))
            rest_arrived = flip(rest_send, 1)
            extras = scatter_first(rest_keep, rest_arrived)
        elif split and number == 1:
            extras = (after(part, table_grad) for part in extras)
            extras = scatter_second(*scatter_between(rest_keep, rest_arrived, *extras))
        elif split:
            extras = tuple(after(part, table_grad) for part in extras)
            rest = scatter_last(rest_keep, rest_arrived, *extras) if number == 2 else extras[0] + extras[1]
            extras = (rest, flip_line(rest, number - 1))
        if number + 1 < groups:
            sent = ()
            if split or number + 2 < groups:
                next_passed, sent = shift(tuple(after(part, rows) for part in passed[-1]), number + 2)
            rows = place_from(number + 1, passed, *sent)
            passed += [next_passed] if sent else []
            held = (incoming, rows) + (() if table_grad is None else (table_grad,))
            came, rows, *tables = lax.optimization_barrier(held)
            table_grad = tables[0] if tables else None
    if split:
        ffn_rows = after(ffn_rows, table_grad)
    table_grad = table_rows(groups - 1, incoming, table_grad)

    if split:
        ffn_rows = ffn_rows.astype(F32)
        extras = tuple(after(part, table_grad) for part in extras)
        for step in range(2, groups + 1):
            ffn_rows = ffn_rows + jnp.where(at == step - 1, passed[step][0], jnp.zeros((), LOW)).astype(F32)
            ffn_rows = ffn_rows + jnp.where(at == groups - step, passed[step][1], jnp.zeros((), LOW)).astype(F32)
        ffn_sum = ffn_rows[: ffn_sum.shape[0]]
        back_rows = w_back.shape[0]
        in_rows = ffn_sum[back_rows : back_rows + cuts * own_rows]
        grad_back = ffn_sum[:back_rows]
        grad_in = jnp.concatenate([in_rows[i * own_rows : (i + 1) * own_rows] for i in range(cuts)], axis=1)
        grad_out = ffn_sum[back_rows + cuts * own_rows :]
        rest = extras[0].astype(F32) + extras[1].astype(F32)
        grad_query, grad_key, grad_value = (rest[i * own_rows : (i + 1) * own_rows] for i in range(3))
        small_grad = rest[3 * own_rows, :small_size]
    else:

        def owned(left, right):
            part = dot_tn(left, right).astype(LOW)
            return lax.psum(lax.psum_scatter(part, "fsdp", scatter_dimension=0, tiled=True), "dp").astype(F32)

        grad_back = owned(act, grad_low)
        grad_in = owned(normed_two, grad_pre)
        grad_query, grad_key, grad_value = (owned(normed_one, grad) for grad in grad_joint)
        grad_out = owned(attended, hidden_low)
        small_grad = lax.psum(small_grad, ("dp", "fsdp"))[me]
    return (
        result.reshape(rows_dev, seq_len, model),
        table_grad,
        small_grad[:own_gain],
        grad_query,
        grad_key,
        grad_value,
        grad_out,
        small_grad[own_gain : 2 * own_gain],
        grad_in,
        grad_back,
        small_grad[2 * own_gain :].reshape(rel_bias.shape),
    )


def solution(mesh):
    both = ("dp", "fsdp")
    in_specs = (
        P(both, None),
        P(both),
        P(both),
        P(both, None),
        P("fsdp", None),
        P("fsdp"),
        P("fsdp", None),
        P("fsdp", None),
        P("fsdp", None),
        P("fsdp", None),
        P("fsdp"),
        P("fsdp", None),
        P("fsdp", None),
        P("fsdp", None),
        P(both, None, None),
    )
    out_specs = (
        P(both, None, None),
        P("fsdp", None),
        P("fsdp"),
        P("fsdp", None),
        P("fsdp", None),
        P("fsdp", None),
        P("fsdp", None),
        P("fsdp"),
        P("fsdp", None),
        P("fsdp", None),
        P("fsdp", None),
    )
    return jax.shard_map(per_device, mesh=mesh, in_specs=in_specs, out_specs=out_specs, check_vma=False)
```

```python
import functools
import jax
import jax.numpy as jnp
from jax import lax
from jax.experimental import pallas as pl
from jax.experimental.pallas import tpu as pltpu
from jax.sharding import PartitionSpec as P

EPS = 1e-06
NEG = -1000000000.0
LIMITS = (12, 16, 23, 32, 46, 64, 91)
HIGH = lax.Precision.HIGHEST
LOW = jnp.bfloat16
F32 = jnp.float32
PAIR = 128
ROOT = (2.0 / 3.141592653589793) ** 0.5
CUBE = 0.044715


def dot(left, right):
    return jnp.dot(left, right, preferred_element_type=F32)


def dot_nt(left, right):
    return lax.dot_general(left, right, (((1,), (1,)), ((), ())), preferred_element_type=F32)


def dot_tn(left, right):
    return lax.dot_general(left, right, (((0,), (0,)), ((), ())), preferred_element_type=F32)


def params(mebibytes):
    return pltpu.CompilerParams(vmem_limit_bytes=mebibytes * 1024 * 1024)


def cost(micros):
    return pl.CostEstimate(flops=int(micros * 1.15e9), bytes_accessed=int(micros * 3.6e6), transcendentals=0)


def half_lanes(size):
    return lax.broadcasted_iota(jnp.int32, (size, PAIR), 1) < PAIR // 2


def spread_bias(diagonal, seq_len):
    wide = jnp.broadcast_to(diagonal, (seq_len, 2 * seq_len))
    wide = pltpu.roll(wide, seq_len + 1, 1, stride=1, stride_axis=0)
    return wide[:, :seq_len]


def gather_bias(grad):
    seq_len = grad.shape[0]
    blocks = seq_len // PAIR
    total = None
    for block in range(blocks):
        ahead = PAIR * (blocks - 1 - block)
        parts = [grad[block * PAIR : (block + 1) * PAIR, :], jnp.zeros((PAIR, seq_len - ahead), F32)]
        if ahead:
            parts = [jnp.zeros((PAIR, ahead), F32)] + parts
        wide = jnp.concatenate(parts, axis=1)
        total = wide if total is None else total + wide
    eight = None
    for group in range(PAIR // 8):
        moved = pltpu.roll(total[8 * group : 8 * group + 8, :], PAIR - 8 - 8 * group, 1)
        eight = moved if eight is None else eight + moved
    return sum(pltpu.roll(eight[sub : sub + 1, :], 7 - sub, 1) for sub in range(8))


def attend_kernel(lengths_ref, diagonal_ref, query_ref, key_ref, value_ref, out_ref, log_ref):
    rows = lengths_ref.shape[0]
    seq_len = query_ref.shape[0] // rows
    first = half_lanes(seq_len)
    key_at = lax.broadcasted_iota(jnp.int32, (seq_len, 1), 0)
    results = [[None, None] for _ in range(rows)]
    for head in range(2):
        bias = spread_bias(diagonal_ref[0, head : head + 1, :], seq_len)
        for row in range(rows):
            span = pl.ds(row * seq_len, seq_len)
            queries = query_ref[span, :]
            queries = jnp.where(first if head == 0 else ~first, queries, jnp.zeros_like(queries))
            scores = dot_nt(key_ref[span, :], queries) + bias
            scores = jnp.where(key_at < lengths_ref[row], scores, NEG)
            largest = jnp.max(scores, axis=0, keepdims=True)
            raised = jnp.exp(scores - largest)
            totals = jnp.sum(raised, axis=0, keepdims=True)
            probs = (raised * (1.0 / totals)).astype(LOW)
            results[row][head] = dot_tn(probs, value_ref[span, :])
            log_ref[0, 2 * row + head : 2 * row + head + 1, :] = largest + jnp.log(totals)
    for row in range(rows):
        out_ref[pl.ds(row * seq_len, seq_len), :] = jnp.where(first, *results[row]).astype(LOW)


def attend(lengths, diagonal, joint, heads):
    tokens = joint.shape[0]
    pairs = heads // 2
    rows = lengths.shape[0]
    seq_len = tokens // rows
    return pl.pallas_call(
        attend_kernel,
        grid=(pairs,),
        in_specs=[
            pl.BlockSpec(memory_space=pltpu.SMEM),
            pl.BlockSpec((1, 2, 2 * seq_len), lambda p: (p, 0, 0)),
            pl.BlockSpec((tokens, PAIR), lambda p: (0, p)),
            pl.BlockSpec((tokens, PAIR), lambda p: (0, pairs + p)),
            pl.BlockSpec((tokens, PAIR), lambda p: (0, 2 * pairs + p)),
        ],
        out_specs=[
            pl.BlockSpec((tokens, PAIR), lambda p: (0, p)),
            pl.BlockSpec((1, 2 * rows, seq_len), lambda p: (p, 0, 0)),
        ],
        out_shape=[
            jax.ShapeDtypeStruct((tokens, pairs * PAIR), LOW),
            jax.ShapeDtypeStruct((pairs, 2 * rows, seq_len), F32),
        ],
        compiler_params=params(56),
        cost_estimate=cost(16),
        name="attend",
    )(lengths, diagonal.reshape(pairs, 2, 2 * seq_len), joint, joint, joint)


def attend_back_kernel(
    lengths_ref, diagonal_ref, query_ref, key_ref, value_ref, grad_ref, log_ref, *outs
):
    query_out, key_out, value_out, bias_out = outs[-4:]
    rows = lengths_ref.shape[0]
    seq_len = query_ref.shape[0] // rows
    first = half_lanes(seq_len)
    key_at = lax.broadcasted_iota(jnp.int32, (seq_len, 1), 0)
    results = [[None, None] for _ in range(rows)]
    for head in range(2):
        bias = spread_bias(diagonal_ref[0, head : head + 1, :], seq_len)
        keep = first if head == 0 else ~first
        total = None
        for row in range(rows):
            span = pl.ds(row * seq_len, seq_len)
            queries = query_ref[span, :]
            keys = key_ref[span, :]
            values = value_ref[span, :]
            grads = grad_ref[span, :]
            only = jnp.where(keep, queries, jnp.zeros_like(queries))
            scores = dot_nt(keys, only) + bias
            scores = jnp.where(key_at < lengths_ref[row], scores, NEG)
            probs = jnp.exp(scores - log_ref[0, 2 * row + head : 2 * row + head + 1, :])
            grad_values = dot(probs.astype(LOW), grads)
            grad_only = jnp.where(keep, grads, jnp.zeros_like(grads))
            grad_probs = dot_nt(values, grad_only)
            weighted = jnp.sum(probs * grad_probs, axis=0, keepdims=True)
            grad_scores = (probs * (grad_probs - weighted)).astype(LOW)
            grad_keys = dot(grad_scores, queries)
            grad_queries = dot_tn(keys, grad_scores)
            wide = grad_scores.astype(F32)
            total = wide if total is None else total + wide
            results[row][head] = (grad_queries, grad_keys, grad_values)
        bias_out[0, head : head + 1, :] = gather_bias(total)
    for row in range(rows):
        span = pl.ds(row * seq_len, seq_len)
        one, two = results[row]
        queries = jnp.concatenate([one[0][: PAIR // 2], two[0][PAIR // 2 :]], axis=0)
        query_out[span, :] = queries.astype(LOW).T
        for out_ref, number in ((key_out, 1), (value_out, 2)):
            out_ref[span, :] = jnp.where(first, one[number], two[number]).astype(LOW)


def attend_back(lengths, diagonal, joint, grad_attended, logs, heads, first, count, before=()):
    tokens = joint.shape[0]
    pairs = heads // 2
    rows = lengths.shape[0]
    seq_len = tokens // rows
    part = pl.BlockSpec((tokens, PAIR), lambda p: (0, first + p))
    whole = jax.ShapeDtypeStruct((tokens, pairs * PAIR), LOW)
    lines = pl.BlockSpec((1, 2, 2 * seq_len), lambda p: (first + p, 0, 0))
    return pl.pallas_call(
        attend_back_kernel,
        grid=(count,),
        in_specs=[
            pl.BlockSpec(memory_space=pltpu.SMEM),
            lines,
            part,
            pl.BlockSpec((tokens, PAIR), lambda p: (0, pairs + first + p)),
            pl.BlockSpec((tokens, PAIR), lambda p: (0, 2 * pairs + first + p)),
            part,
            pl.BlockSpec((1, 2 * rows, seq_len), lambda p: (first + p, 0, 0)),
        ]
        + [pl.BlockSpec(memory_space=pl.ANY)] * len(before),
        out_specs=[part, part, part, lines],
        out_shape=[whole, whole, whole, jax.ShapeDtypeStruct((pairs, 2, 2 * seq_len), F32)],
        input_output_aliases={7 + i: i for i in range(len(before))},
        compiler_params=params(56),
        cost_estimate=cost((4.4 * count) * 0.5),
        name="attend_back",
    )(lengths, diagonal.reshape(pairs, 2, 2 * seq_len), joint, joint, joint, grad_attended, logs, *before)


def weight_copy(me, number, load, refs, targets, semaphores):
    source, target, column, relative, shard_rows, first, start, rows = load
    width = refs[source].shape[1]
    place = first if relative is None else pl.multiple_of((me ^ relative) * shard_rows + first, 16)
    return pltpu.make_async_copy(
        refs[source].at[pl.ds(start, rows), :],
        targets[target].at[pl.ds(place, rows), pl.ds(column, width)],
        semaphores.at[number],
    )


def weights_of(me_ref, plans, refs, targets, semaphores):
    def each(act):
        for value, loads in enumerate(plans):

            @pl.when(me_ref[1] == value)
            def _():
                for number, load in enumerate(loads):
                    act(number, load)

    def start():
        each(lambda number, load: weight_copy(me_ref[0], number, load, refs, targets, semaphores).start())

    def wait(target):
        def act(number, load):
            if load[1] == target:
                weight_copy(me_ref[0], number, load, refs, targets, semaphores).wait()

        @pl.when(pl.program_id(0) == 0)
        def _():
            each(act)

    return start, wait


def plan_loads(parts, sections):
    loads = []
    for source, at, relative, first, count in parts:
        start = 0
        for target, rows, column, shard_rows in sections:
            low = max(start, first)
            high = min(start + rows, first + count)
            if low < high:
                loads.append((source, target, column, relative, shard_rows, low - start, at + low - first, high - low))
            start += rows
    return loads


def front_kernel(loads, count, me_ref, slot_ref, reply_ref, gain_ref, *rest):
    refs, (x_ref, normed_ref, joint_ref), (weight, semaphores) = rest[:count], rest[count : count + 3], rest[count + 3 :]

    start, wait = weights_of(me_ref, loads, refs, [weight], semaphores)
    pl.when(pl.program_id(0) == 0)(start)
    rows = slot_ref.shape[0]
    slots = reply_ref.shape[0]
    hot = slot_ref[...] == lax.broadcasted_iota(jnp.int32, (rows, slots), 1)
    x = dot(hot.astype(F32).astype(LOW), reply_ref[...])
    x_ref[...] = x.astype(LOW)
    scale = lax.rsqrt(jnp.mean(x * x, axis=-1, keepdims=True) + EPS)
    normed = (x * scale * gain_ref[...]).astype(LOW)
    normed_ref[...] = normed
    wait(0)
    joint_ref[...] = dot(normed, weight[...]).astype(LOW)


ANY = pl.BlockSpec(memory_space=pl.ANY)
SMEM = pl.BlockSpec(memory_space=pltpu.SMEM)
BLOCK = 256


def full(shape):
    return pl.BlockSpec(shape, lambda *ids: (0,) * len(shape))


def down(width, rows=BLOCK):
    return pl.BlockSpec((rows, width), lambda i: (i, 0))


def front(me, slot, replies, gain, pieces, loads, width):
    tokens = slot.shape[0]
    model = replies.shape[1]
    rows = 2 * BLOCK
    return pl.pallas_call(
        functools.partial(front_kernel, loads, len(pieces)),
        grid=(tokens // rows,),
        in_specs=[SMEM, down(1, rows), full(replies.shape), full((1, model))] + [ANY] * len(pieces),
        out_specs=[down(model, rows), down(model, rows), down(width, rows)],
        out_shape=[
            jax.ShapeDtypeStruct((tokens, model), LOW),
            jax.ShapeDtypeStruct((tokens, model), LOW),
            jax.ShapeDtypeStruct((tokens, width), LOW),
        ],
        scratch_shapes=[pltpu.VMEM((model, width), LOW), pltpu.SemaphoreType.DMA((max(len(plan) for plan in loads),))],
        compiler_params=params(56),
        cost_estimate=cost((15) * 0.7),
        name="front",
    )(me, slot, replies, gain, *pieces)


def ffn_kernel(loads, count, me_ref, x_ref, attended_ref, d_out_ref, seed_ref, gain_ref, *rest):
    refs = rest[:count]
    (y_ref, act_ref, grad_pre_ref, grad_low_ref, normed_ref, hidden_out, low_out, attended_out, gain_out) = rest[count : count + 9]
    w_out, w_in, w_back, semaphores = rest[count + 9 :]

    start_weights, wait = weights_of(me_ref, loads, refs, [w_out, w_in, w_back], semaphores)

    @pl.when(pl.program_id(0) == 0)
    def _():
        start_weights()
        gain_out[...] = jnp.zeros_like(gain_out)

    wait(0)
    hidden = x_ref[...].astype(F32) + dot(attended_ref[...], w_out[...])
    scale = lax.rsqrt(jnp.mean(hidden * hidden, axis=-1, keepdims=True) + EPS)
    unit = hidden * scale
    gain = gain_ref[...]
    normed = (unit * gain).astype(LOW)
    normed_ref[...] = normed
    grad_out = d_out_ref[...].astype(F32) * seed_ref[...]
    grad_low = grad_out.astype(LOW)
    grad_low_ref[...] = grad_low
    wait(1)
    wait(2)
    result = hidden
    back = jnp.zeros_like(hidden)
    model = hidden.shape[1]
    for start in range(0, w_in.shape[1], model):
        span = pl.ds(start, model)
        pre = dot(normed, w_in[:, span])
        square = pre * pre
        tanh = jnp.tanh(ROOT * (pre + CUBE * square * pre))
        half = 0.5 * (1.0 + tanh)
        act = (pre * half).astype(LOW)
        slope = half + 0.5 * pre * (1.0 - tanh * tanh) * ROOT * (1.0 + 3.0 * CUBE * square)
        act_ref[:, span] = act
        result = result + dot(act, w_back[span, :])
        grad_pre = (dot_nt(grad_low, w_back[span, :]) * slope).astype(LOW)
        grad_pre_ref[:, span] = grad_pre
        back = back + dot_nt(grad_pre, w_in[:, span])
    y_ref[...] = result.astype(LOW)
    gain_out[...] += jnp.sum(back * unit, axis=0, keepdims=True)
    scaled = back * gain
    grad_hidden = grad_out + scale * (scaled - unit * jnp.mean(scaled * unit, axis=-1, keepdims=True))
    hidden_out[...] = grad_hidden
    low = grad_hidden.astype(LOW)
    low_out[...] = low
    attended_out[...] = dot_nt(low, w_out[...]).astype(LOW)


def ffn(me, x, attended, d_out, seed, gain, pieces, loads, inner, ff_width):
    tokens, model = x.shape
    low = jax.ShapeDtypeStruct((tokens, model), LOW)
    wide = jax.ShapeDtypeStruct((tokens, ff_width), LOW)
    return pl.pallas_call(
        functools.partial(ffn_kernel, loads, len(pieces)),
        grid=(tokens // BLOCK,),
        in_specs=[SMEM, down(model), down(inner), down(model), down(1), full((1, model))] + [ANY] * len(pieces),
        out_specs=[
            down(model), down(ff_width), down(ff_width), down(model), down(model), down(model), down(model), down(inner),
            full((1, model)),
        ],
        out_shape=[
            low, wide, wide, low, low, jax.ShapeDtypeStruct((tokens, model), F32), low,
            jax.ShapeDtypeStruct((tokens, inner), LOW), jax.ShapeDtypeStruct((1, model), F32),
        ],
        scratch_shapes=[
            pltpu.VMEM((inner, model), LOW),
            pltpu.VMEM((model, ff_width), LOW),
            pltpu.VMEM((ff_width, model), LOW),
            pltpu.SemaphoreType.DMA((max(len(plan) for plan in loads),)),
        ],
        compiler_params=params(56),
        cost_estimate=cost((35) * 2.0),
        name="ffn",
    )(me, x, attended, d_out, seed, gain, *pieces)


def project_back_kernel(loads, count, me_ref, query_ref, key_ref, value_ref, x_ref, hidden_ref, gain_ref, *rest):
    refs, (out_ref, gain_out), (weight, semaphores) = rest[:count], rest[count : count + 2], rest[count + 2 :]

    start_weights, wait = weights_of(me_ref, loads, refs, [weight], semaphores)

    @pl.when(pl.program_id(0) == 0)
    def _():
        start_weights()
        gain_out[...] = jnp.zeros_like(gain_out)

    wait(0)
    inner = query_ref.shape[1]
    back = dot_nt(query_ref[...], weight[:, :inner])
    back = back + dot_nt(key_ref[...], weight[:, inner : 2 * inner])
    back = back + dot_nt(value_ref[...], weight[:, 2 * inner :])
    x = x_ref[...].astype(F32)
    scale = lax.rsqrt(jnp.mean(x * x, axis=-1, keepdims=True) + EPS)
    unit = x * scale
    gain_out[...] += jnp.sum(back * unit, axis=0, keepdims=True)
    scaled = back * gain_ref[...]
    grad = hidden_ref[...] + scale * (scaled - unit * jnp.mean(scaled * unit, axis=-1, keepdims=True))
    out_ref[...] = grad.astype(LOW)


def project_back(me, grads, x, grad_hidden, gain, pieces, loads):
    tokens, model = x.shape
    inner = grads[0].shape[1]
    return pl.pallas_call(
        functools.partial(project_back_kernel, loads, len(pieces)),
        grid=(tokens // BLOCK,),
        in_specs=[SMEM] + [down(inner)] * 3 + [down(model), down(model), full((1, model))] + [ANY] * len(pieces),
        out_specs=[down(model), full((1, model))],
        out_shape=[jax.ShapeDtypeStruct((tokens, model), LOW), jax.ShapeDtypeStruct((1, model), F32)],
        scratch_shapes=[pltpu.VMEM((model, 3 * inner), LOW), pltpu.SemaphoreType.DMA((max(len(plan) for plan in loads),))],
        compiler_params=params(56),
        cost_estimate=cost(11),
        name="project_back",
    )(me, *grads, x, grad_hidden, gain, *pieces)


def store_shards(me, value, shards, first, keep_ref, send_ref):
    rows = value.shape[0] // shards
    for shard in range(shards):
        relative = me ^ shard
        part = value[shard * rows : (shard + 1) * rows, :].astype(LOW)

        @pl.when(relative % 2 == 0)
        def _():
            keep_ref[relative // 2, pl.ds(first, rows), :] = part

        @pl.when(relative % 2 == 1)
        def _():
            send_ref[relative // 2, pl.ds(first, rows), :] = part


def blocks_grad_kernel(me_ref, keep_left, send_left, right_ref, keep_ref, send_ref):
    both = dot_tn(jnp.concatenate([keep_left[...], send_left[...]], axis=1), right_ref[...]).astype(LOW)
    rows = keep_left.shape[1]
    keep_ref[0] = both[:rows]
    send_ref[0] = both[rows:]


def columns_grad_kernel(shards, me_ref, normed_ref, pre_ref, attended_ref, hidden_ref, unused_keep, unused_send, keep_ref, send_ref):
    last = pl.program_id(0) == pl.num_programs(0) - 1

    @pl.when(jnp.logical_not(last))
    def _():
        store_shards(me_ref[0], dot_tn(normed_ref[...], pre_ref[...]), shards, 0, keep_ref, send_ref)

    @pl.when(last)
    def _():
        store_shards(me_ref[0], dot_tn(attended_ref[...], hidden_ref[...]), shards, 0, keep_ref, send_ref)


def ffn_grads(me, act, grad_low, normed, grad_pre, attended, hidden_low, shards):
    tokens, model = grad_low.shape
    wide = act.shape[1]
    first = wide // shards
    rows = model // shards
    cuts = wide // model
    shape = jax.ShapeDtypeStruct((shards // 2, first + (cuts + 1) * rows, model), LOW)
    out = pl.BlockSpec((1, first, model), lambda i, me: (i, 0, 0))
    keep, send = pl.pallas_call(
        blocks_grad_kernel,
        grid_spec=pltpu.PrefetchScalarGridSpec(
            num_scalar_prefetch=1,
            grid=(shards // 2,),
            in_specs=[
                pl.BlockSpec((tokens, first), lambda i, me: (0, me[0] ^ (2 * i))),
                pl.BlockSpec((tokens, first), lambda i, me: (0, me[0] ^ (2 * i + 1))),
                pl.BlockSpec((tokens, model), lambda i, me: (0, 0)),
            ],
            out_specs=[out, out],
        ),
        out_shape=[shape, shape],
        compiler_params=params(56),
        cost_estimate=cost(9),
        name="back_grad",
    )(me, act, act, grad_low)
    out = pl.BlockSpec((shards // 2, rows, model), lambda i: (0, first // rows + i, 0))
    return pl.pallas_call(
        functools.partial(columns_grad_kernel, shards),
        grid=(cuts + 1,),
        in_specs=[
            SMEM,
            full((tokens, model)),
            pl.BlockSpec((tokens, model), lambda i: (0, jnp.minimum(i, cuts - 1))),
            full((tokens, model)),
            full((tokens, model)),
            ANY,
            ANY,
        ],
        out_specs=[out, out],
        out_shape=[shape, shape],
        input_output_aliases={5: 0, 6: 1},
        compiler_params=params(56),
        cost_estimate=cost(13),
        name="columns_grad",
    )(me, normed, grad_pre, attended, hidden_low, keep, send)


SMALL_ROWS = 16


def rest_grads_kernel(shards, me_ref, normed_ref, query_ref, key_ref, value_ref, small_ref, keep_ref, send_ref):
    rows = normed_ref.shape[1] // shards
    me = me_ref[0]
    start = 0
    for right_ref in (query_ref, key_ref, value_ref):
        store_shards(me, dot_tn(normed_ref[...], right_ref[...]), shards, start, keep_ref, send_ref)
        start += rows
    store_shards(me, small_ref[...], shards, start, keep_ref, send_ref)


def rest_grads(me, normed, grads, small, shards):
    tokens, model = normed.shape
    shape = jax.ShapeDtypeStruct((shards // 2, 3 * (model // shards) + SMALL_ROWS, model), LOW)
    return pl.pallas_call(
        functools.partial(rest_grads_kernel, shards),
        in_specs=[SMEM] + [full((tokens, model))] * 4 + [full(small.shape)],
        out_specs=[full(shape.shape)] * 2,
        out_shape=[shape, shape],
        compiler_params=params(56),
        cost_estimate=cost(11),
        name="rest_grads",
    )(me, normed, *grads, small)


def place_kernel(count, slot_ref, choice_ref, *rest):
    options, (out_ref, tokens, semaphore) = rest[:count], rest[count:]

    @pl.when(pl.program_id(0) == 0)
    def _():
        for number, option in enumerate(options):

            @pl.when(choice_ref[0] == number)
            def _():
                copy = pltpu.make_async_copy(option, tokens, semaphore)
                copy.start()
                copy.wait()

    rows = out_ref.shape[0]
    at = lax.broadcasted_iota(jnp.int32, (rows, tokens.shape[0]), 0) + pl.program_id(0) * rows
    out_ref[...] = dot((at == slot_ref[...]).astype(F32).astype(LOW), tokens[...]).astype(LOW)


def place(slot, choice, options, slots):
    tokens, model = options[0].shape
    return pl.pallas_call(
        functools.partial(place_kernel, len(options)),
        grid=(slots // 1024,),
        in_specs=[full((1, tokens)), SMEM] + [ANY] * len(options),
        out_specs=down(model, 1024),
        out_shape=jax.ShapeDtypeStruct((slots, model), LOW),
        scratch_shapes=[pltpu.VMEM((tokens, model), LOW), pltpu.SemaphoreType.DMA],
        compiler_params=params(56),
        cost_estimate=cost(6),
        name="place",
    )(slot, choice, *options)


TABLE_BLOCK = 512


def table_kernel(ids_ref, rows_ref, *rest):
    out_ref = rest[-1]
    rows = out_ref.shape[0]
    at = lax.broadcasted_iota(jnp.int32, (rows, ids_ref.shape[1]), 0) + pl.program_id(0) * rows
    total = dot((at == ids_ref[...]).astype(F32).astype(LOW), rows_ref[...])
    if len(rest) > 1:
        total = total + rest[0][...]
    out_ref[...] = total


def add_to_table(ids, token_rows, before, vshard):
    model = token_rows.shape[1]
    more = [] if before is None else [before]
    return pl.pallas_call(
        table_kernel,
        grid=(pl.cdiv(vshard, TABLE_BLOCK),),
        in_specs=[full(ids.shape), full(token_rows.shape)] + [down(model, TABLE_BLOCK)] * len(more),
        out_specs=down(model, TABLE_BLOCK),
        out_shape=jax.ShapeDtypeStruct((vshard, model), F32),
        input_output_aliases={2: 0} if more else {},
        compiler_params=params(56),
        cost_estimate=cost(18),
        name="table_rows",
    )(ids, token_rows, *more)


def flip(value, bits):
    shards = lax.axis_size("fsdp")
    return lax.ppermute(value, "fsdp", [(i, i ^ bits) for i in range(shards)])


def flip_line(value, bits):
    groups = lax.axis_size("dp")
    return lax.ppermute(value, "dp", [(i, i ^ bits) for i in range(groups)])


def after(value, *others):
    return lax.optimization_barrier((value,) + others)[0]


def exchange(value):
    return lax.all_to_all(value, "fsdp", split_axis=0, concat_axis=0, tiled=True)


def gather_near(own):
    return own, flip(own, 2), flip(own, 4)


def gather_far(near, *gates):
    own, by_x, by_y = near
    half = own.shape[0] // 32 * 16
    to_x, to_y = after(by_y[:half], *gates), after(by_x[half:], *gates)
    pieces = [(0, 0, own), (2, 0, by_x), (4, 0, by_y)]
    return pieces + [(6, 0, flip(to_x, 2)), (6, half, flip(to_y, 4))]


def gather_core(pieces):
    return pieces + [(bits ^ 1, first, flip(part, 1)) for bits, first, part in pieces]


def scatter_first(keep, arrived):
    rows = keep.shape[1]
    half = rows // 32 * 16
    across = (keep[3].astype(F32) + arrived[3].astype(F32)).astype(LOW)
    return flip(across[:half], 2), flip(across[half:], 4)


def scatter_between(keep, arrived, from_x, from_y):
    rows, columns = keep.shape[1:]
    half = from_x.shape[0]
    pad_x = jnp.concatenate([from_x, jnp.zeros((rows - half, columns), LOW)])
    pad_y = jnp.concatenate([jnp.zeros((half, columns), LOW), from_y])
    to_y = (keep[2].astype(F32) + arrived[2].astype(F32) + pad_x.astype(F32)).astype(LOW)
    to_x = (keep[1].astype(F32) + arrived[1].astype(F32) + pad_y.astype(F32)).astype(LOW)
    return to_x, to_y


def scatter_second(to_x, to_y):
    return flip(to_x, 2), flip(to_y, 4)


def scatter_last(keep, arrived, by_x, by_y):
    return (keep[0].astype(F32) + arrived[0].astype(F32) + by_x.astype(F32) + by_y.astype(F32)).astype(LOW)


def bucket_of(offset):
    distance = jnp.abs(offset)
    far_bucket = 8 + sum(((distance >= limit).astype(jnp.int32) for limit in LIMITS))
    upper = jnp.where(offset > 0, 16, 0).astype(jnp.int32)
    return upper + jnp.where(distance < 8, distance, far_bucket)


def per_device(
    token_ids,
    task_ids,
    lengths,
    instruction,
    table,
    attn_gain,
    w_query,
    w_key,
    w_value,
    w_out,
    ffn_gain,
    w_in,
    w_back,
    rel_bias,
    d_out,
):
    rows_dev, seq_len = token_ids.shape
    vshard, model = table.shape
    inner = w_query.shape[1]
    ff_width = w_in.shape[1]
    heads = rel_bias.shape[1]
    shards = lax.axis_size("fsdp")
    groups = lax.axis_size("dp")
    me = lax.axis_index("fsdp")
    at = lax.axis_index("dp")
    odd = at % 2
    me_ref = jnp.stack([me, odd]).astype(jnp.int32)
    tokens = rows_dev * seq_len
    capacity = 2 * tokens // shards
    task_count = rows_dev * groups * shards // 4
    own_gain = attn_gain.shape[0]
    buckets = rel_bias.shape[0] * shards

    flat_ids = token_ids.reshape(tokens)
    owner = flat_ids // vshard
    local_row = flat_ids - owner * vshard
    owner_hot = (owner[:, None] == jnp.arange(shards, dtype=jnp.int32)[None, :]).astype(LOW)
    token_at = jnp.arange(tokens, dtype=jnp.int32)
    before = (token_at[:, None] > token_at[None, :]).astype(LOW)
    ranks = jnp.dot(before, owner_hot, preferred_element_type=F32)
    rank_within = jnp.sum(ranks * owner_hot.astype(F32), axis=1).astype(jnp.int32)
    slot = owner * capacity + rank_within
    slots = jnp.arange(shards * capacity, dtype=jnp.int32)
    slot_hot = slots[:, None] == slot[None, :]
    requests = (jnp.sum(jnp.where(slot_hot, local_row[None, :] + 1, 0), axis=1) - 1).reshape(shards, capacity)
    small = jnp.concatenate([attn_gain, ffn_gain, rel_bias.reshape(-1)])
    small_size = small.shape[0]
    joint_own = jnp.concatenate([w_query, w_key, w_value], axis=1)
    own_rows = w_query.shape[0]
    cuts = ff_width // model
    split = shards == 8 and groups == 4
    if split:
        extra = jnp.pad(small, (0, 16 * 3 * inner - small_size)).reshape(16, 3 * inner)
        joint_near = gather_near(jnp.concatenate([joint_own, extra]))
        slab = jnp.concatenate([w_out] + [w_in[:, i * model : (i + 1) * model] for i in range(cuts)] + [w_back])
        half_rows = slab.shape[0] // 2
        half = lax.dynamic_slice_in_dim(slab, odd * half_rows, half_rows)
    task_rows = jnp.broadcast_to(task_ids[None, :], (shards, rows_dev))
    told = exchange(jnp.concatenate([requests, task_rows], axis=1))
    if split:
        told = after(told, *joint_near)
        ffn_near = gather_near(after(half, told))
        joint_pieces = gather_far(joint_near)
    asked = told[:, :capacity]
    task_hot = (told[:, capacity:].reshape(-1, 1) == jnp.arange(task_count, dtype=jnp.int32)[None, :]).astype(jnp.int32)
    plane_counts = jnp.sum(task_hot, axis=0)
    looked = jnp.take(table, jnp.maximum(asked, 0).reshape(-1), axis=0, mode="clip")
    if split:
        looked = after(looked, *ffn_near, *(part for unused_bits, unused_first, part in joint_pieces))
        joint_pieces = gather_core(joint_pieces)
        parts = [(i, 0, bits, first, part.shape[0]) for i, (bits, first, part) in enumerate(joint_pieces)]
        joint_loads = [plan_loads(parts, [(0, own_rows, 0, own_rows)])] * 2
        lines = {
            bits: part[own_rows - first, :small_size]
            for bits, first, part in joint_pieces
            if first <= own_rows < first + part.shape[0]
        }
        small_all = jnp.stack([lines[bits] for bits in range(shards)])[jnp.arange(shards) ^ me]
        joint_pieces = [part for unused_bits, unused_first, part in joint_pieces]
    replies = exchange(looked.reshape(shards, capacity, model)).reshape(shards * capacity, model)
    if split:
        near_rows = jnp.concatenate([after(part, looked) for part in ffn_near[1:]])
        near_others = flip_line(near_rows, 1)
        ffn_far = gather_far(ffn_near, replies)[3:]
    if not split:
        joint_pieces, small_all, *ffn_pieces = (
            lax.all_gather(part, "fsdp", axis=0, tiled=True) for part in (joint_own, small[None], w_out, w_in, w_back)
        )
        joint_pieces = [joint_pieces]
        joint_loads = [[(0, 0, 0, None, 0, 0, 0, model)]] * 2
        ffn_loads = [[(i, i, 0, None, 0, 0, 0, part.shape[0]) for i, part in enumerate(ffn_pieces)]] * 2
    first_gain = small_all[:, :own_gain].reshape(1, model).astype(F32)
    second_gain = small_all[:, own_gain : 2 * own_gain].reshape(1, model).astype(F32)
    rel_all = small_all[:, 2 * own_gain :].reshape(buckets, heads).astype(F32)

    message = jnp.concatenate([slot, asked.reshape(-1), plane_counts])
    message = after(message, *(joint_pieces[5:] if split else [replies]))
    messages = [flip_line(message, bits) for bits in range(1, groups)]
    positions = jnp.arange(seq_len, dtype=jnp.int32)
    pool_mask = ((positions[None, :] < lengths[:, None]) & (instruction == 0)).astype(F32)

    offsets = (seq_len - 1) - jnp.arange(2 * seq_len, dtype=jnp.int32)
    bucket_hot = (jnp.arange(buckets, dtype=jnp.int32)[:, None] == bucket_of(offsets)[None, :]).astype(F32)
    diagonal = lax.dot_general(rel_all, bucket_hot, (((0,), (0,)), ((), ())), precision=HIGH)

    x, normed_one, joint = front(me_ref, slot[:, None], replies, first_gain, joint_pieces, joint_loads, 3 * inner)
    slot_of = [slot]
    asked_of = [asked]
    counts = plane_counts
    for theirs in messages:
        theirs = after(theirs, joint)
        slot_of.append(theirs[:tokens])
        asked_of.append(theirs[tokens : tokens + shards * capacity])
        counts = counts + theirs[tokens + shards * capacity :]
    own_hot = (task_ids[:, None] == jnp.arange(task_count, dtype=jnp.int32)[None, :]).astype(F32)
    row_weight = 1.0 / jnp.sum(own_hot * counts.astype(F32)[None, :], axis=1)
    seed = (pool_mask * row_weight[:, None]).reshape(tokens, 1)
    if split:
        far_rows = jnp.concatenate([after(part, joint) for unused_bits, unused_first, part in ffn_far])
        held = [slab, near_rows, near_others, far_rows, flip_line(far_rows, 1)]
        ffn_pieces = held + [flip(after(part, joint), 1) for part in held[:4]]
        sections = [(0, own_rows, 0, own_rows)]
        sections += [(1, own_rows, i * model, own_rows) for i in range(cuts)]
        sections += [(2, w_back.shape[0], 0, w_back.shape[0])]
        ffn_loads = []
        for own_half in (0, half_rows):
            parts = []
            for core in (0, 1):
                parts.append((5 * core, 0, core, 0, 2 * half_rows))
                for source, half in ((1, own_half), (2, half_rows - own_half)):
                    parts += [(5 * core + source, 0, 2 ^ core, half, half_rows)]
                    parts += [(5 * core + source, half_rows, 4 ^ core, half, half_rows)]
                    parts += [(5 * core + source + 2, 0, 6 ^ core, half, half_rows)]
            ffn_loads.append(plan_loads(parts, sections))
    attended, logs = attend(lengths, diagonal, joint, heads)
    if split:
        ffn_pieces.append(flip(after(held[4], attended), 1))
    result, act, grad_pre, grad_low, normed_two, grad_hidden, hidden_low, grad_attended, grad_second = ffn(
        me_ref, x, attended, d_out.reshape(tokens, model), seed, second_gain, ffn_pieces, ffn_loads, inner, ff_width
    )
    backward = functools.partial(attend_back, lengths, diagonal, joint)
    if split:
        keep, send = ffn_grads(me_ref, act, grad_low, normed_two, grad_pre, attended, hidden_low, shards)
        arrived = flip(send, 1)
        grads = backward(after(grad_attended, send), logs, heads, 0, 2)
        first_hop = scatter_first(keep, after(arrived, *grads))
        grads = backward(after(grad_attended, arrived, *grads), logs, heads, 2, 4, grads)
        between = scatter_between(keep, arrived, *(after(part, *grads) for part in first_hop))
        second_hop = scatter_second(*between)
        grads = tuple(after(part, *between) for part in grads)
    else:
        grads = backward(grad_attended, logs, heads, 0, heads // 2)
    *grad_joint, bias_sums = grads
    bias_sums = bias_sums.reshape(heads, 2 * seq_len)
    grad_rel = lax.dot_general(bucket_hot, bias_sums, (((1,), (1,)), ((), ())), precision=HIGH)
    token_grads, grad_first = project_back(me_ref, grad_joint, x, grad_hidden, first_gain, joint_pieces, joint_loads)
    small_grad = jnp.concatenate(
        [grad_first.reshape(shards, -1), grad_second.reshape(shards, -1), grad_rel.reshape(shards, -1)], axis=1
    )

    def shift(sent, step, *gates):
        pairs = [(i, i + 1) for i in range(step - 1, groups - 1)]
        back = [(groups - 1 - i, groups - 1 - j) for i, j in pairs]
        to_right, to_left = (after(part, *gates) for part in sent)
        return lax.ppermute(to_right, "dp", pairs), lax.ppermute(to_left, "dp", back)

    def shift(sent, step):
        pairs = [(i, i + 1) for i in range(max(step - 2, 0), groups - 1)]
        back = [(groups - 1 - i, groups - 1 - j) for i, j in pairs]
        to_right, to_left = sent
        if split and step > 1:
            if step == 2:
                to_right = jnp.where(at == 0, ffn_rows, to_right)
                to_left = jnp.where(at == groups - 1, ffn_rows, to_left)
            else:
                to_right = to_right + jnp.where(at == step - 2, ffn_rows, jnp.zeros((), LOW))
                to_left = to_left + jnp.where(at == groups + 1 - step, ffn_rows, jnp.zeros((), LOW))
        return (lax.ppermute(to_right, "dp", pairs), lax.ppermute(to_left, "dp", back)), (to_right, to_left)

    def place_from(number, passed, *gates):
        distance = (at ^ number) - at
        steps = sorted({(i ^ number) - i for i in range(groups)})
        options = [passed[abs(step)][step > 0] for step in steps]
        choice = sum((distance == step).astype(jnp.int32) * i for i, step in enumerate(steps))
        return place(after(slot_of[number][None, :], *gates), choice.reshape(1), options, shards * capacity)

    def table_rows(number, incoming, table_grad):
        return add_to_table(asked_of[number].reshape(1, -1), incoming, table_grad, vshard)

    passed = [(token_grads, token_grads)]
    passed.append(shift(passed[0], 1)[0])
    rows = place_from(0, passed)
    if split:
        small_rows = jnp.pad(small_grad[:, None], ((0, 0), (0, SMALL_ROWS - 1), (0, model - small_size)))
        small_rows = after(small_rows.reshape(shards * SMALL_ROWS, model), flip(rows[:16], 1))
        rest_keep, rest_send = rest_grads(me_ref, normed_one, grad_joint, small_rows, shards)
    came = table_grad = None
    extras = second_hop if split else ()
    for number in range(groups):
        incoming = exchange(rows.reshape(shards, capacity, model)).reshape(shards * capacity, model)
        if number > 0:
            table_grad = table_rows(number - 1, came, table_grad)
        if split and number == 0:
            ffn_sum = scatter_last(keep, arrived, *extras)
            ffn_rows = jnp.pad(ffn_sum, ((0, tokens - ffn_sum.shape[0]), (0, 0)))
            rest_arrived = flip(rest_send, 1)
            extras = scatter_first(rest_keep, rest_arrived)
        elif split and number == 1:
            extras = (after(part, table_grad) for part in extras)
            extras = scatter_second(*scatter_between(rest_keep, rest_arrived, *extras))
        elif split:
            extras = tuple(after(part, table_grad) for part in extras)
            rest = scatter_last(rest_keep, rest_arrived, *extras) if number == 2 else extras[0] + extras[1]
            extras = (rest, flip_line(rest, number - 1))
        if number + 1 < groups:
            sent = ()
            if split or number + 2 < groups:
                next_passed, sent = shift(tuple(after(part, rows) for part in passed[-1]), number + 2)
            rows = place_from(number + 1, passed, *sent)
            passed += [next_passed] if sent else []
            held = (incoming, rows) + (() if table_grad is None else (table_grad,))
            came, rows, *tables = lax.optimization_barrier(held)
            table_grad = tables[0] if tables else None
    if split:
        ffn_rows = after(ffn_rows, table_grad)
    table_grad = table_rows(groups - 1, incoming, table_grad)

    if split:
        ffn_rows = ffn_rows.astype(F32)
        extras = tuple(after(part, table_grad) for part in extras)
        for step in range(2, groups + 1):
            ffn_rows = ffn_rows + jnp.where(at == step - 1, passed[step][0], jnp.zeros((), LOW)).astype(F32)
            ffn_rows = ffn_rows + jnp.where(at == groups - step, passed[step][1], jnp.zeros((), LOW)).astype(F32)
        ffn_sum = ffn_rows[: ffn_sum.shape[0]]
        back_rows = w_back.shape[0]
        in_rows = ffn_sum[back_rows : back_rows + cuts * own_rows]
        grad_back = ffn_sum[:back_rows]
        grad_in = jnp.concatenate([in_rows[i * own_rows : (i + 1) * own_rows] for i in range(cuts)], axis=1)
        grad_out = ffn_sum[back_rows + cuts * own_rows :]
        rest = extras[0].astype(F32) + extras[1].astype(F32)
        grad_query, grad_key, grad_value = (rest[i * own_rows : (i + 1) * own_rows] for i in range(3))
        small_grad = rest[3 * own_rows, :small_size]
    else:

        def owned(left, right):
            part = dot_tn(left, right).astype(LOW)
            return lax.psum(lax.psum_scatter(part, "fsdp", scatter_dimension=0, tiled=True), "dp").astype(F32)

        grad_back = owned(act, grad_low)
        grad_in = owned(normed_two, grad_pre)
        grad_query, grad_key, grad_value = (owned(normed_one, grad) for grad in grad_joint)
        grad_out = owned(attended, hidden_low)
        small_grad = lax.psum(small_grad, ("dp", "fsdp"))[me]
    return (
        result.reshape(rows_dev, seq_len, model),
        table_grad,
        small_grad[:own_gain],
        grad_query,
        grad_key,
        grad_value,
        grad_out,
        small_grad[own_gain : 2 * own_gain],
        grad_in,
        grad_back,
        small_grad[2 * own_gain :].reshape(rel_bias.shape),
    )


def solution(mesh):
    both = ("dp", "fsdp")
    in_specs = (
        P(both, None),
        P(both),
        P(both),
        P(both, None),
        P("fsdp", None),
        P("fsdp"),
        P("fsdp", None),
        P("fsdp", None),
        P("fsdp", None),
        P("fsdp", None),
        P("fsdp"),
        P("fsdp", None),
        P("fsdp", None),
        P("fsdp", None),
        P(both, None, None),
    )
    out_specs = (
        P(both, None, None),
        P("fsdp", None),
        P("fsdp"),
        P("fsdp", None),
        P("fsdp", None),
        P("fsdp", None),
        P("fsdp", None),
        P("fsdp"),
        P("fsdp", None),
        P("fsdp", None),
        P("fsdp", None),
    )
    return jax.shard_map(per_device, mesh=mesh, in_specs=in_specs, out_specs=out_specs, check_vma=False)
```
